32 devices in a mesh: groups: 2 (over y), shard: 8 (over z, x), replica: 2 (over core).
Axes of the slice: x: 2, y: 2, z: 4, core: 2. Of those that a mesh axis runs over, the one named last changes fastest.
Arguments:
- gradients: bfloat16 [2, 12, 768, 768], P('replica', 'groups', 'shard'), parts along dimension 1, may hold values from -5 to 5
- block_owner: int32 [12], P('groups'), parts along dimension 0, may hold values from 0 to 7, as said below
- left_gram: bfloat16 [16, 768, 768], P(('groups', 'shard'), 'replica'), parts along dimension 0, may hold values from -1 to 5
- right_gram: bfloat16 [16, 768, 768], P(('groups', 'shard'), 'replica'), parts along dimension 0, may hold values from -1 to 5
- left_root: bfloat16 [16, 768, 768], P(('groups', 'shard'), 'replica'), parts along dimension 0, may hold values from -1 to 3
- right_root: bfloat16 [16, 768, 768], P(('groups', 'shard'), None, 'replica'), parts along dimension 0, may hold values from -1 to 3
Outputs:
- left_new: bfloat16 [16, 768, 768], P(('groups', 'shard'), 'replica'), parts along dimension 0
- right_new: bfloat16 [16, 768, 768], P(('groups', 'shard'), 'replica'), parts along dimension 0
- update: bfloat16 [12, 768, 768], P('groups', 'shard', 'replica'), parts along dimension 0
The draws below stay inside these ranges and needn't reach their ends.
There are 2 independent parts, one for each index of `groups`. The reference program is written for one: setup_inputs(seed, part) draws one part's arguments, and reference() takes and returns one part's arrays. A program takes and returns all parts, laid end to end along the dimension named above; each array names one. Nothing has to cross between parts.
Inputs may be any that keep to these rules, and one draw needn't show every extreme that they name: `block_owner`: the 6 owners are distinct.
All inputs are finite; a program needn't handle non-finite values.
Results may differ from the reference program's by a relative error of at most 0.0059.
Values may be sent and summed in bfloat16 or wider, within the bound.
No kernel may reach another device: no remote copies, remote signals or barrier semaphores. Data moves between devices by JAX's collectives and lax.ppermute only.
A program may use at most 64 MiB of HBM per device.

```python
import math
import jax
import jax.numpy as jnp
from jax import lax

B = 768
NB = 6
N_SHARD = 8
N_REPLICA = 2


def draw_block_owner(key, part):
    key = jax.random.fold_in(key, 5)
    first_key, second_key = jax.random.split(key)
    middle = jax.random.permutation(first_key, N_SHARD - 2).astype(jnp.int32) + 1
    ends = jnp.array([0, N_SHARD - 1], jnp.int32)
    chosen = jnp.concatenate([ends, middle[:NB - 2]])
    return jax.random.permutation(second_key, chosen)


def assemble(diag_key, noise_field, lowest, highest):
    symmetric = (noise_field + jnp.swapaxes(noise_field, 1, 2)) * 0.7071
    row_index = lax.broadcasted_iota(jnp.int32, (1, B, B), 1)
    col_index = lax.broadcasted_iota(jnp.int32, (1, B, B), 2)
    identity = (row_index == col_index).astype(jnp.float32)
    levels = jnp.exp(jax.random.uniform(diag_key, (N_SHARD, B, 1), jnp.float32, math.log(lowest), math.log(highest)))
    return symmetric * (1.0 - identity) + levels * identity


def draw_left_gram(key, part):
    key = jax.random.fold_in(key, 11)
    diag_key, off_key = jax.random.split(key)
    noise_field = jnp.clip(jax.random.normal(off_key, (N_SHARD, B, B), jnp.float32), -4.0, 4.0) * 0.1
    return assemble(diag_key, noise_field, 0.5, 4.0).astype(jnp.bfloat16)


def draw_right_gram(key, part):
    key = jax.random.fold_in(key, 13)
    diag_key, off_key = jax.random.split(key)
    noise_field = jnp.clip(jax.random.normal(off_key, (N_SHARD, B, B), jnp.float32), -4.0, 4.0) * 0.1
    return assemble(diag_key, noise_field, 0.5, 4.0).astype(jnp.bfloat16)


def draw_left_root(key, part):
    key = jax.random.fold_in(key, 17)
    diag_key, off_key = jax.random.split(key)
    noise_field = jnp.clip(jax.random.normal(off_key, (N_SHARD, B, B), jnp.float32), -4.0, 4.0) * (0.5 / B ** 0.5)
    return assemble(diag_key, noise_field, 0.5, 2.0).astype(jnp.bfloat16)


def draw_right_root(key, part):
    key = jax.random.fold_in(key, 19)
    diag_key, off_key = jax.random.split(key)
    noise_field = jnp.clip(jax.random.normal(off_key, (N_SHARD, B, B), jnp.float32), -4.0, 4.0) * (0.5 / B ** 0.5)
    return assemble(diag_key, noise_field, 0.5, 2.0).astype(jnp.bfloat16)


def steps_of(own_key, extent, pieces, smallest, largest):
    level, own = 1.0, jax.random.fold_in(own_key, 6)
    for dim, parts in pieces:
        heights = jnp.exp(jax.random.uniform(jax.random.fold_in(own, dim), (parts,), jnp.float32, smallest / len(pieces), largest / len(pieces)))
        level = level * jnp.repeat(heights, extent[dim] // parts).reshape([-1 if axis == dim else 1 for axis in range(len(extent))])
    return level


def scatter_about(stream_key, extent, spread, reach, cuts=(), held_as=jnp.bfloat16):
    values = spread * jax.random.normal(stream_key, extent, jnp.float32)
    if cuts:
        values = values * steps_of(stream_key, extent, cuts, -0.22, 0.18)
    return jnp.clip(values, -reach, reach).astype(held_as)


def setup_inputs(seed: int = 0, part: int = 0) -> dict:
    seeds = jax.random.split(jax.random.key(seed), 7)
    part_keys = jax.random.split(jax.random.fold_in(seeds[6], part), 7)
    return {
        "gradients": scatter_about(part_keys[0], (N_REPLICA, NB, B, B), 0.35, 5.0, ((0, 2), (2, 8))),
        "block_owner": draw_block_owner(jax.random.fold_in(jax.random.fold_in(seeds[6], part), 71), part),
        "left_gram": draw_left_gram(jax.random.fold_in(jax.random.fold_in(seeds[6], part), 71), part),
        "right_gram": draw_right_gram(jax.random.fold_in(jax.random.fold_in(seeds[6], part), 71), part),
        "left_root": draw_left_root(jax.random.fold_in(jax.random.fold_in(seeds[6], part), 71), part),
        "right_root": draw_right_root(jax.random.fold_in(jax.random.fold_in(seeds[6], part), 71), part),
    }


def reference(gradients, block_owner, left_gram, right_gram, left_root, right_root):
    summed = (gradients[0].astype(jnp.float32) + gradients[1].astype(jnp.float32)).astype(jnp.bfloat16)

    def one_block(block_items):
        block, left_inverse, right_inverse = block_items
        left_term = jnp.dot(block, block.T, preferred_element_type=jnp.float32)
        right_term = jnp.dot(block.T, block, preferred_element_type=jnp.float32)
        left_side = jnp.dot(left_inverse, block, preferred_element_type=jnp.float32).astype(jnp.bfloat16)
        both_sides = jnp.dot(left_side, right_inverse, preferred_element_type=jnp.float32)
        grad_squares = jnp.sum(jnp.square(block.astype(jnp.float32)))
        graft = jnp.sqrt(grad_squares / (jnp.sum(both_sides * both_sides) + 1e-06))
        return (left_term, right_term, (both_sides * graft).astype(jnp.bfloat16))
    left_terms, right_terms, update = lax.map(one_block, (summed, left_root[block_owner], right_root[block_owner]))
    left_new = (0.99 * left_gram.astype(jnp.float32)).at[block_owner].add(0.01 * left_terms)
    right_new = (0.99 * right_gram.astype(jnp.float32)).at[block_owner].add(0.01 * right_terms)
    return (left_new.astype(jnp.bfloat16), right_new.astype(jnp.bfloat16), update)
```

```python
import functools

import jax
import jax.numpy as jnp
from jax import lax
from jax.experimental import pallas as pl
from jax.experimental.pallas import tpu as pltpu
from jax.sharding import PartitionSpec as P

VMEM = pl.BlockSpec(memory_space=pltpu.VMEM)
SMEM = pl.BlockSpec(memory_space=pltpu.SMEM)
PARAMS = pltpu.CompilerParams(vmem_limit_bytes=24 * 1024 * 1024)


def per_device(gradients, block_owner, left_gram, right_gram, left_root, right_root):
    owners = lax.axis_size("shard")
    half_rows = left_gram.shape[1]
    full_width = left_gram.shape[2]
    first_row = lax.axis_index("replica") * half_rows
    owner_index = lax.broadcasted_iota(jnp.int32, (owners, block_owner.shape[0]), 0)
    owner_onehot = (owner_index == block_owner[None, :]).astype(jnp.bfloat16)
    outgoing = jnp.einsum(
        "ob,brc->orc", owner_onehot, gradients[0], preferred_element_type=jnp.float32
    )
    arrived = lax.all_to_all(
        outgoing.astype(jnp.bfloat16), "shard", split_axis=0, concat_axis=0, tiled=True
    )
    total = lax.psum(arrived.astype(jnp.float32).astype(jnp.bfloat16), "replica")
    summed_block = total.reshape(full_width, full_width)
    own_rows = lax.dynamic_slice_in_dim(summed_block, first_row, half_rows, 0)
    own_cols = lax.dynamic_slice_in_dim(summed_block, first_row, half_rows, 1)
    left_term = lax.dot_general(
        own_rows, summed_block, (((1,), (1,)), ((), ())), preferred_element_type=jnp.float32
    )
    right_term = lax.dot_general(
        own_cols, summed_block, (((0,), (0,)), ((), ())), preferred_element_type=jnp.float32
    )
    left_new = (0.99 * left_gram[0].astype(jnp.float32) + 0.01 * left_term).astype(jnp.bfloat16)
    right_new = (0.99 * right_gram[0].astype(jnp.float32) + 0.01 * right_term).astype(jnp.bfloat16)
    partial_side = jnp.dot(left_root[0], summed_block, preferred_element_type=jnp.float32).astype(
        jnp.bfloat16
    )
    left_side = lax.all_gather(partial_side, "replica", axis=0, tiled=True)
    both_sides = jnp.dot(left_side, right_root[0], preferred_element_type=jnp.float32)
    side_squares = lax.psum(jnp.sum(both_sides * both_sides), "replica")
    grad_squares = jnp.sum(jnp.square(summed_block.astype(jnp.float32)))
    graft = jnp.sqrt(grad_squares / (side_squares + 1e-06))
    scaled = (
        (both_sides * graft).astype(jnp.bfloat16).reshape(owners, full_width // owners, half_rows)
    )
    returned = lax.all_to_all(scaled, "shard", split_axis=0, concat_axis=0, tiled=True)
    update = jnp.take(returned, block_owner, axis=0)
    return (left_new[None], right_new[None], update)


def pick_kernel(index_ref, mine_ref, theirs_ref, *out_refs):
    for j, out_ref in enumerate(out_refs):
        b = index_ref[j]
        total = mine_ref[b].astype(jnp.float32) + theirs_ref[b].astype(jnp.float32)
        out_ref[...] = total.astype(out_ref.dtype)


def precondition_kernel(rounds, place_ref, *refs):
    mine, theirs = refs[:rounds], refs[rounds:2 * rounds]
    left_ref, own_ref, other_ref, summed_ref, both_ref, side_sq_ref, grad_sq_ref, side_ref = refs[2 * rounds:]
    core, place = place_ref[0], place_ref[1]
    slab = mine[0].shape[0]
    half = rounds * slab
    grad_sq = jnp.zeros((1, mine[0].shape[1]), jnp.float32)
    for j in range(rounds):
        for ref, side in ((mine[j], core), (theirs[j], 1 - core)):
            row = pl.multiple_of(side * half + (place ^ j) * slab, slab)
            block = ref[...]
            summed_ref[pl.ds(row, slab), :] = block
            wide = block.astype(jnp.float32)
            grad_sq += jnp.sum(wide * wide, axis=0, keepdims=True)
    grad_sq_ref[...] = jnp.sum(grad_sq, axis=1, keepdims=True)
    side_ref[...] = jnp.dot(
        left_ref[...], summed_ref[...], preferred_element_type=jnp.float32
    ).astype(side_ref.dtype)
    side_sq = jnp.zeros((1, 1), jnp.float32)
    for ref, side in ((own_ref, core), (other_ref, 1 - core)):
        both = jnp.dot(side_ref[...], ref[...], preferred_element_type=jnp.float32)
        width = ref.shape[1]
        both_ref[:, pl.ds(pl.multiple_of(side * width, 128), width)] = both
        side_sq += jnp.sum(jnp.sum(both * both, axis=0, keepdims=True), axis=1, keepdims=True)
    side_sq_ref[...] = side_sq


def scale_kernel(rounds, place_ref, graft_ref, both_ref, *out_refs):
    place, keep = place_ref[1], place_ref[2]
    graft = graft_ref[0]
    for j in range(rounds):
        slab, width = out_refs[j].shape[1:]
        row = pl.multiple_of((place ^ j) * slab, slab)
        for k, side in ((0, keep), (1, 1 - keep)):
            col = pl.multiple_of(side * width, 128)
            piece = both_ref[pl.ds(row, slab), pl.ds(col, width)]
            out_refs[j][k] = (piece * graft).astype(out_refs[j].dtype)


def place_kernel(rounds, index_ref, *refs):
    mine, theirs, out_ref = refs[:rounds], refs[rounds:2 * rounds], refs[2 * rounds]
    for j in range(rounds):
        for k, ref in ((0, mine[j]), (1, theirs[j])):
            b = index_ref[2 * j + k]

            @pl.when(b >= 0)
            def _():
                out_ref[b] = ref[...]


def per_device_paired(gradients, block_owner, left_gram, right_gram, left_root, right_root):
    owners = lax.axis_size("shard")
    rounds = owners // 2
    blocks, slab, width = gradients.shape[1:]
    half_rows = left_gram.shape[1]
    shard, core = lax.axis_index("shard"), lax.axis_index("replica")
    side, place = shard // rounds, shard % rounds
    swap = [(0, 1), (1, 0)]

    def turn(j):
        return [
            ((h * rounds + l) * 2 + r, (r * rounds + (l ^ j)) * 2 + h)
            for h in range(2) for l in range(rounds) for r in range(2) if j or h != r
        ]

    def other_core(x):
        return lax.ppermute(x, "replica", swap)

    def trade(x, j):
        got = lax.ppermute(x, ("shard", "replica"), turn(j))
        return got if j else jnp.where(side == core, x, got)

    block_index = jnp.arange(blocks, dtype=jnp.int32)

    def block_of(owner):
        return jnp.max(jnp.where(block_owner == owner, block_index, -1))

    gradient = gradients[0]
    other_gradient = other_core(gradient)
    sent_index = jnp.stack(
        [jnp.maximum(block_of(core * rounds + (place ^ j)), 0) for j in range(rounds)]
    )
    outgoing = pl.pallas_call(
        pick_kernel,
        out_shape=[jax.ShapeDtypeStruct((slab, width), jnp.bfloat16)] * rounds,
        in_specs=[SMEM, VMEM, VMEM],
        out_specs=[VMEM] * rounds,
        compiler_params=PARAMS,
    )(sent_index, gradient, other_gradient)
    mine = [trade(outgoing[j], j) for j in range(rounds)]
    other_right = other_core(right_root[0])
    theirs = [other_core(m) for m in mine]
    place_info = jnp.stack([core, place, side]).astype(jnp.int32)
    summed, both_sides, side_sq, grad_sq = pl.pallas_call(
        functools.partial(precondition_kernel, rounds),
        out_shape=[
            jax.ShapeDtypeStruct((width, width), jnp.bfloat16),
            jax.ShapeDtypeStruct((half_rows, width), jnp.float32),
            jax.ShapeDtypeStruct((1, 1), jnp.float32),
            jax.ShapeDtypeStruct((1, 1), jnp.float32),
        ],
        in_specs=[SMEM] + [VMEM] * (2 * rounds + 3),
        out_specs=[VMEM] * 4,
        scratch_shapes=[pltpu.VMEM((half_rows, width), jnp.bfloat16)],
        compiler_params=PARAMS,
    )(place_info, *mine, *theirs, left_root[0], right_root[0], other_right)
    side_squares = side_sq + other_core(side_sq)
    graft = jnp.sqrt(grad_sq / (side_squares + 1e-06))
    scaled = pl.pallas_call(
        functools.partial(scale_kernel, rounds),
        out_shape=[jax.ShapeDtypeStruct((2, slab, width // 2), jnp.bfloat16)] * rounds,
        in_specs=[SMEM, SMEM, VMEM],
        out_specs=[VMEM] * rounds,
        compiler_params=PARAMS,
    )(place_info, graft.reshape(1), both_sides)
    returned = [trade(scaled[j], j) for j in range(rounds)]
    kept = [x[0] for x in returned]
    passed = [other_core(x[1]) for x in returned]

    present = block_of(shard) >= 0
    share = jnp.where(present, 0.01, 0.0).astype(jnp.float32)
    first_row = core * half_rows
    own_rows = lax.dynamic_slice_in_dim(summed, first_row, half_rows, 0)
    own_cols = lax.dynamic_slice_in_dim(summed, first_row, half_rows, 1)
    left_term = lax.dot_general(
        own_rows, summed, (((1,), (1,)), ((), ())), preferred_element_type=jnp.float32
    )
    right_term = lax.dot_general(
        own_cols, summed, (((0,), (0,)), ((), ())), preferred_element_type=jnp.float32
    )
    left_new = (0.99 * left_gram[0].astype(jnp.float32) + share * left_term).astype(jnp.bfloat16)
    right_new = (0.99 * right_gram[0].astype(jnp.float32) + share * right_term).astype(jnp.bfloat16)

    placed_index = jnp.stack(
        [
            block_of(c * rounds + (place ^ j))
            for j in range(rounds) for c in (core, 1 - core)
        ]
    )
    update = pl.pallas_call(
        functools.partial(place_kernel, rounds),
        out_shape=jax.ShapeDtypeStruct((blocks, slab, width // 2), jnp.bfloat16),
        in_specs=[SMEM] + [VMEM] * (2 * rounds),
        out_specs=VMEM,
        compiler_params=PARAMS,
    )(placed_index, *kept, *passed)
    return (left_new[None], right_new[None], update)


def solution(mesh):
    owners = mesh.shape["shard"]
    paired = mesh.shape["replica"] == 2 and owners in (2, 4, 8, 16)
    return jax.shard_map(
        per_device_paired if paired else per_device,
        mesh=mesh,
        in_specs=(
            P("replica", "groups", "shard", None),
            P("groups"),
            P(("groups", "shard"), "replica", None),
            P(("groups", "shard"), "replica", None),
            P(("groups", "shard"), "replica", None),
            P(("groups", "shard"), None, "replica"),
        ),
        out_specs=(
            P(("groups", "shard"), "replica", None),
            P(("groups", "shard"), "replica", None),
            P("groups", "shard", "replica"),
        ),
        check_vma=False,
    )
```

```python
import functools

import jax
import jax.numpy as jnp
from jax import lax
from jax.experimental import pallas as pl
from jax.experimental.pallas import tpu as pltpu
from jax.sharding import PartitionSpec as P

VMEM = pl.BlockSpec(memory_space=pltpu.VMEM)
SMEM = pl.BlockSpec(memory_space=pltpu.SMEM)
ANY = pl.BlockSpec(memory_space=pl.ANY)
EARLY = 1
PARAMS = pltpu.CompilerParams(vmem_limit_bytes=24 * 1024 * 1024)


def per_device(gradients, block_owner, left_gram, right_gram, left_root, right_root):
    owners = lax.axis_size("shard")
    half_rows = left_gram.shape[1]
    full_width = left_gram.shape[2]
    first_row = lax.axis_index("replica") * half_rows
    owner_index = lax.broadcasted_iota(jnp.int32, (owners, block_owner.shape[0]), 0)
    owner_onehot = (owner_index == block_owner[None, :]).astype(jnp.bfloat16)
    outgoing = jnp.einsum(
        "ob,brc->orc", owner_onehot, gradients[0], preferred_element_type=jnp.float32
    )
    arrived = lax.all_to_all(
        outgoing.astype(jnp.bfloat16), "shard", split_axis=0, concat_axis=0, tiled=True
    )
    total = lax.psum(arrived.astype(jnp.float32).astype(jnp.bfloat16), "replica")
    summed_block = total.reshape(full_width, full_width)
    own_rows = lax.dynamic_slice_in_dim(summed_block, first_row, half_rows, 0)
    own_cols = lax.dynamic_slice_in_dim(summed_block, first_row, half_rows, 1)
    left_term = lax.dot_general(
        own_rows, summed_block, (((1,), (1,)), ((), ())), preferred_element_type=jnp.float32
    )
    right_term = lax.dot_general(
        own_cols, summed_block, (((0,), (0,)), ((), ())), preferred_element_type=jnp.float32
    )
    left_new = (0.99 * left_gram[0].astype(jnp.float32) + 0.01 * left_term).astype(jnp.bfloat16)
    right_new = (0.99 * right_gram[0].astype(jnp.float32) + 0.01 * right_term).astype(jnp.bfloat16)
    partial_side = jnp.dot(left_root[0], summed_block, preferred_element_type=jnp.float32).astype(
        jnp.bfloat16
    )
    left_side = lax.all_gather(partial_side, "replica", axis=0, tiled=True)
    both_sides = jnp.dot(left_side, right_root[0], preferred_element_type=jnp.float32)
    side_squares = lax.psum(jnp.sum(both_sides * both_sides), "replica")
    grad_squares = jnp.sum(jnp.square(summed_block.astype(jnp.float32)))
    graft = jnp.sqrt(grad_squares / (side_squares + 1e-06))
    scaled = (
        (both_sides * graft).astype(jnp.bfloat16).reshape(owners, full_width // owners, half_rows)
    )
    returned = lax.all_to_all(scaled, "shard", split_axis=0, concat_axis=0, tiled=True)
    update = jnp.take(returned, block_owner, axis=0)
    return (left_new[None], right_new[None], update)


def device_place(rounds):
    shard = lax.axis_index("shard")
    return lax.div(shard, rounds), lax.rem(shard, rounds), lax.axis_index("replica")


def block_of(owner_ref, owner):
    block = jnp.int32(-1)
    for b in range(owner_ref.shape[0]):
        block = jnp.where(owner_ref[b] == owner, b, block)
    return block


def sent_block(owner_ref, rounds, j):
    side, place, core = device_place(rounds)
    return jnp.maximum(block_of(owner_ref, (side ^ core) * rounds + (place ^ j)), 0)


def fetch_kernel(owner_ref, gradient_ref, out_ref, sem):
    rounds = out_ref.shape[0]
    copies = [
        pltpu.make_async_copy(
            gradient_ref.at[sent_block(owner_ref, rounds, j)], out_ref.at[j], sem.at[j]
        )
        for j in range(rounds)
    ]
    for copy in copies:
        copy.start()
    for copy in copies:
        copy.wait()


def pick_kernel(owner_ref, mine_ref, theirs_ref, *out_refs):
    rounds = len(out_refs)
    for j, out_ref in enumerate(out_refs):
        other = theirs_ref[sent_block(owner_ref, rounds, j)]
        total = mine_ref[j].astype(jnp.float32) + other.astype(jnp.float32)
        out_ref[...] = total.astype(out_ref.dtype)


def slab_for(ref, keep, row, slab, scale=None):
    width = ref.shape[1] // 2
    pieces = []
    for side in (keep, 1 - keep):
        piece = ref[pl.ds(row, slab), pl.ds(pl.multiple_of(side * width, 128), width)]
        pieces.append(piece if scale is None else piece * scale)
    return pieces


def precondition_kernel(rounds, early, *refs):
    mine, theirs = refs[:rounds], refs[rounds:2 * rounds]
    left_ref, own_ref, other_ref, summed_ref, both_ref, side_sq_ref, grad_sq_ref = refs[
        2 * rounds:2 * rounds + 7
    ]
    early_refs, side_ref = refs[2 * rounds + 7:-1], refs[-1]
    side, place, core = device_place(rounds)
    slab, full = mine[0].shape
    half = rounds * slab
    grad_sq = jnp.zeros((1, full), jnp.float32)
    for j in range(rounds):
        for ref, rows_side in ((mine[j], side ^ core), (theirs[j], side ^ (1 - core))):
            row = pl.multiple_of(rows_side * half + (place ^ j) * slab, slab)
            block = ref[...]
            summed_ref[pl.ds(row, slab), :] = block
            wide = block.astype(jnp.float32)
            grad_sq += jnp.sum(wide * wide, axis=0, keepdims=True)
    grad_sq_ref[...] = jnp.sum(grad_sq, axis=1, keepdims=True)
    side_ref[...] = jnp.dot(
        left_ref[...], summed_ref[...], preferred_element_type=jnp.float32
    ).astype(side_ref.dtype)
    side_sq = jnp.zeros((1, 1), jnp.float32)
    for ref, columns_side in ((own_ref, core), (other_ref, 1 - core)):
        both = jnp.dot(side_ref[...], ref[...], preferred_element_type=jnp.float32)
        width = ref.shape[1]
        both_ref[:, pl.ds(pl.multiple_of(columns_side * width, 128), width)] = both
        side_sq += jnp.sum(jnp.sum(both * both, axis=0, keepdims=True), axis=1, keepdims=True)
    side_sq_ref[...] = side_sq
    for j, out_ref in zip(early, early_refs):
        row = pl.multiple_of((place ^ j) * slab, slab)
        for k, piece in enumerate(slab_for(both_ref, core, row, slab)):
            out_ref[k] = piece.astype(out_ref.dtype)


def scale_kernel(rounds, late, mine_sq_ref, theirs_sq_ref, grad_sq_ref, both_ref, graft_ref, *out_refs):
    side, place, core = device_place(rounds)
    slab = both_ref.shape[0] // rounds
    side_sq = mine_sq_ref[...] + theirs_sq_ref[...]
    graft = jnp.sqrt(grad_sq_ref[...] / (side_sq + 1e-06))
    graft_ref[...] = jnp.broadcast_to(graft, graft_ref.shape)
    for j, out_ref in zip(late, out_refs):
        row = pl.multiple_of((place ^ j) * slab, slab)
        for k, piece in enumerate(slab_for(both_ref, core, row, slab, graft)):
            out_ref[k] = piece.astype(out_ref.dtype)


def gram_kernel(owner_ref, summed_ref, left_ref, right_ref, after_ref, left_out, right_out):
    half = left_ref.shape[0]
    first = pl.multiple_of(lax.axis_index("replica") * half, 128)
    present = block_of(owner_ref, lax.axis_index("shard")) >= 0
    share = jnp.where(present, 0.01, 0.0).astype(jnp.float32)
    summed = summed_ref[...]
    left_term = lax.dot_general(
        summed_ref[pl.ds(first, half), :], summed, (((1,), (1,)), ((), ())),
        preferred_element_type=jnp.float32,
    )
    left_out[...] = (0.99 * left_ref[...].astype(jnp.float32) + share * left_term).astype(
        left_out.dtype
    )
    right_term = lax.dot_general(
        summed_ref[:, pl.ds(first, half)], summed, (((0,), (0,)), ((), ())),
        preferred_element_type=jnp.float32,
    )
    right_out[...] = (0.99 * right_ref[...].astype(jnp.float32) + share * right_term).astype(
        right_out.dtype
    )


def place_kernel(rounds, early, owner_ref, *refs):
    slabs = (refs[:rounds], refs[rounds:2 * rounds])
    grafts = refs[2 * rounds:2 * rounds + 2 * len(early)]
    out_ref, scaled_ref, sem = refs[2 * rounds + 2 * len(early):]
    side, place, core = device_place(rounds)
    pending = []
    for j in [j for j in range(rounds) if j not in early] + list(early):
        for k in range(2):
            owner = (side ^ core ^ k) * rounds + (place ^ j)
            block = block_of(owner_ref, owner)
            source = slabs[k][j].at[0] if k == 0 else slabs[k][j]
            if j in early:
                n = 2 * early.index(j) + k
                ref = slabs[k][j]
                value = ref[0] if k == 0 else ref[...]
                scaled = value.astype(jnp.float32) * grafts[n][0:1, 0:1]
                scaled_ref[n] = scaled.astype(scaled_ref.dtype)
                source = scaled_ref.at[n]
            copy = pltpu.make_async_copy(
                source, out_ref.at[jnp.maximum(block, 0)], sem.at[2 * j + k]
            )

            @pl.when(block >= 0)
            def _(copy=copy):
                copy.start()

            pending.append((block, copy))
    for block, copy in pending:

        @pl.when(block >= 0)
        def _(copy=copy):
            copy.wait()


def per_device_paired(gradients, block_owner, left_gram, right_gram, left_root, right_root):
    rounds = lax.axis_size("shard") // 2
    blocks, slab, width = gradients.shape[1:]
    half_rows = left_gram.shape[1]
    order = [j for i in range((rounds + 1) // 2) for j in dict.fromkeys((i + rounds // 2, i))]
    early, late = order[:EARLY], order[EARLY:]
    places = [(h, l, r) for h in range(2) for l in range(rounds) for r in range(2)]

    def device(h, l, r):
        return (h * rounds + l) * 2 + r

    def other_core(x):
        return lax.ppermute(x, "replica", [(0, 1), (1, 0)])

    def trade(x, j):
        pairs = [(device(h, l, r), device(h ^ r, l ^ j, r)) for h, l, r in places]
        return lax.ppermute(x, ("shard", "replica"), pairs)

    def shape(dims, dtype=jnp.bfloat16):
        return jax.ShapeDtypeStruct(dims, dtype)

    def call(kernel, out_shape, in_specs, *args, **options):
        return pl.pallas_call(
            kernel, out_shape=out_shape, in_specs=in_specs, compiler_params=PARAMS, **options
        )(*args)

    other_gradient = other_core(gradients[0])
    fetched = call(
        fetch_kernel, shape((rounds, slab, width)), [SMEM, ANY], block_owner, gradients[0],
        out_specs=VMEM, scratch_shapes=[pltpu.SemaphoreType.DMA((rounds,))],
    )
    outgoing = call(
        pick_kernel, [shape((slab, width))] * rounds, [SMEM, VMEM, VMEM],
        block_owner, fetched, other_gradient, out_specs=[VMEM] * rounds,
    )
    mine = {j: trade(outgoing[j], j) for j in order}
    other_right = other_core(right_root[0])
    left_rows = lax.ppermute(
        left_root[0], ("shard", "replica"),
        [(device(h, l, r), device(h, l, r ^ h)) for h, l, r in places],
    )
    theirs = {j: other_core(mine[j]) for j in order}
    one = shape((1, 1), jnp.float32)
    slab_shape = shape((2, slab, width // 2))
    summed, both_sides, side_sq, grad_sq, *first = call(
        functools.partial(precondition_kernel, rounds, early),
        [shape((width, width)), shape((half_rows, width), jnp.float32), one, one]
        + [slab_shape] * len(early),
        [VMEM] * (2 * rounds + 3),
        *[mine[j] for j in range(rounds)], *[theirs[j] for j in range(rounds)],
        left_rows, right_root[0], other_right,
        out_specs=[VMEM] * (4 + len(early)),
        scratch_shapes=[pltpu.VMEM((half_rows, width), jnp.bfloat16)],
    )
    returned = {j: trade(x, j) for j, x in zip(early, first)}
    graft, *rest = call(
        functools.partial(scale_kernel, rounds, late),
        [shape((8, 128), jnp.float32)] + [slab_shape] * len(late),
        [VMEM] * 4, side_sq, other_core(side_sq), grad_sq, both_sides,
        out_specs=[VMEM] * (1 + len(late)),
    )
    returned.update((j, trade(x, j)) for j, x in zip(late, rest))
    grafts = []
    for j in early:
        came = trade(graft, j)
        grafts += [came, other_core(came)]
    passed = {j: other_core(returned[j][1]) for j in order}

    left_new, right_new = call(
        gram_kernel, [shape(left_gram.shape[1:]), shape(right_gram.shape[1:])],
        [SMEM, VMEM, VMEM, VMEM, ANY],
        block_owner, summed, left_gram[0], right_gram[0], returned[order[0]],
        out_specs=[VMEM, VMEM],
        cost_estimate=pl.CostEstimate(
            flops=4 * half_rows * width * width, bytes_accessed=8 * half_rows * width,
            transcendentals=0,
        ),
    )
    update = call(
        functools.partial(place_kernel, rounds, early), shape((blocks, slab, width // 2)),
        [SMEM] + [VMEM] * (2 * rounds + len(grafts)), block_owner,
        *[returned[j] for j in range(rounds)], *[passed[j] for j in range(rounds)], *grafts,
        out_specs=ANY,
        scratch_shapes=[
            pltpu.VMEM((max(1, 2 * len(early)), slab, width // 2), jnp.bfloat16),
            pltpu.SemaphoreType.DMA((2 * rounds,)),
        ],
    )
    return (left_new[None], right_new[None], update)


def solution(mesh):
    owners = mesh.shape["shard"]
    paired = mesh.shape["replica"] == 2 and owners in (2, 4, 8, 16)
    return jax.shard_map(
        per_device_paired if paired else per_device,
        mesh=mesh,
        in_specs=(
            P("replica", "groups", "shard", None),
            P("groups"),
            P(("groups", "shard"), "replica", None),
            P(("groups", "shard"), "replica", None),
            P(("groups", "shard"), "replica", None),
            P(("groups", "shard"), None, "replica"),
        ),
        out_specs=(
            P(("groups", "shard"), "replica", None),
            P(("groups", "shard"), "replica", None),
            P("groups", "shard", "replica"),
        ),
        check_vma=False,
    )
```

```python
import functools

import jax
import jax.numpy as jnp
from jax import lax
from jax.experimental import pallas as pl
from jax.experimental.pallas import tpu as pltpu
from jax.sharding import PartitionSpec as P

VMEM = pl.BlockSpec(memory_space=pltpu.VMEM)
SMEM = pl.BlockSpec(memory_space=pltpu.SMEM)
ANY = pl.BlockSpec(memory_space=pl.ANY)
EARLY = 1
PARAMS = pltpu.CompilerParams(vmem_limit_bytes=24 * 1024 * 1024)


def per_device(gradients, block_owner, left_gram, right_gram, left_root, right_root):
    owners = lax.axis_size("shard")
    half_rows = left_gram.shape[1]
    full_width = left_gram.shape[2]
    first_row = lax.axis_index("replica") * half_rows
    owner_index = lax.broadcasted_iota(jnp.int32, (owners, block_owner.shape[0]), 0)
    owner_onehot = (owner_index == block_owner[None, :]).astype(jnp.bfloat16)
    outgoing = jnp.einsum(
        "ob,brc->orc", owner_onehot, gradients[0], preferred_element_type=jnp.float32
    )
    arrived = lax.all_to_all(
        outgoing.astype(jnp.bfloat16), "shard", split_axis=0, concat_axis=0, tiled=True
    )
    total = lax.psum(arrived.astype(jnp.float32).astype(jnp.bfloat16), "replica")
    summed_block = total.reshape(full_width, full_width)
    own_rows = lax.dynamic_slice_in_dim(summed_block, first_row, half_rows, 0)
    own_cols = lax.dynamic_slice_in_dim(summed_block, first_row, half_rows, 1)
    left_term = lax.dot_general(
        own_rows, summed_block, (((1,), (1,)), ((), ())), preferred_element_type=jnp.float32
    )
    right_term = lax.dot_general(
        own_cols, summed_block, (((0,), (0,)), ((), ())), preferred_element_type=jnp.float32
    )
    left_new = (0.99 * left_gram[0].astype(jnp.float32) + 0.01 * left_term).astype(jnp.bfloat16)
    right_new = (0.99 * right_gram[0].astype(jnp.float32) + 0.01 * right_term).astype(jnp.bfloat16)
    partial_side = jnp.dot(left_root[0], summed_block, preferred_element_type=jnp.float32).astype(
        jnp.bfloat16
    )
    left_side = lax.all_gather(partial_side, "replica", axis=0, tiled=True)
    both_sides = jnp.dot(left_side, right_root[0], preferred_element_type=jnp.float32)
    side_squares = lax.psum(jnp.sum(both_sides * both_sides), "replica")
    grad_squares = jnp.sum(jnp.square(summed_block.astype(jnp.float32)))
    graft = jnp.sqrt(grad_squares / (side_squares + 1e-06))
    scaled = (
        (both_sides * graft).astype(jnp.bfloat16).reshape(owners, full_width // owners, half_rows)
    )
    returned = lax.all_to_all(scaled, "shard", split_axis=0, concat_axis=0, tiled=True)
    update = jnp.take(returned, block_owner, axis=0)
    return (left_new[None], right_new[None], update)


def device_place(rounds):
    shard = lax.axis_index("shard")
    return lax.div(shard, rounds), lax.rem(shard, rounds), lax.axis_index("replica")


def block_of(owner_ref, owner):
    block = jnp.int32(-1)
    for b in range(owner_ref.shape[0]):
        block = jnp.where(owner_ref[b] == owner, b, block)
    return block


def sent_block(owner_ref, rounds, j):
    side, place, core = device_place(rounds)
    return jnp.maximum(block_of(owner_ref, (side ^ core) * rounds + (place ^ j)), 0)


def fetch_kernel(owner_ref, gradient_ref, out_ref):
    rounds = out_ref.shape[0]
    for j in range(rounds):
        out_ref[j] = gradient_ref[sent_block(owner_ref, rounds, j)]


def pick_kernel(owner_ref, mine_ref, theirs_ref, *out_refs):
    rounds = len(out_refs)
    for j, out_ref in enumerate(out_refs):
        other = theirs_ref[sent_block(owner_ref, rounds, j)]
        total = mine_ref[j].astype(jnp.float32) + other.astype(jnp.float32)
        out_ref[...] = total.astype(out_ref.dtype)


def slab_for(ref, keep, row, slab, scale=None):
    width = ref.shape[1] // 2
    pieces = []
    for side in (keep, 1 - keep):
        piece = ref[pl.ds(row, slab), pl.ds(pl.multiple_of(side * width, 128), width)]
        pieces.append(piece if scale is None else piece * scale)
    return pieces


def precondition_kernel(rounds, early, *refs):
    mine, theirs = refs[:rounds], refs[rounds:2 * rounds]
    left_refs, right_refs = refs[2 * rounds:2 * rounds + 2], refs[2 * rounds + 2:2 * rounds + 4]
    summed_ref, both_ref, side_sq_ref, grad_sq_ref = refs[2 * rounds + 4:2 * rounds + 8]
    early_refs, side_ref = refs[2 * rounds + 8:-1], refs[-1]
    side, place, core = device_place(rounds)
    slab, full = mine[0].shape
    half = rounds * slab
    grad_sq = jnp.zeros((1, full), jnp.float32)
    for j in range(rounds):
        for ref, rows_side in ((mine[j], side ^ core), (theirs[j], side ^ (1 - core))):
            row = pl.multiple_of(rows_side * half + (place ^ j) * slab, slab)
            block = ref[...]
            summed_ref[pl.ds(row, slab), :] = block
            wide = block.astype(jnp.float32)
            grad_sq += jnp.sum(wide * wide, axis=0, keepdims=True)
    total = jnp.sum(grad_sq, axis=1, keepdims=True)
    grad_sq_ref[...] = jnp.broadcast_to(total, grad_sq_ref.shape)
    for h, left_ref in enumerate(left_refs):

        @pl.when(side == h)
        def _(left_ref=left_ref):
            side_ref[...] = jnp.dot(
                left_ref[...], summed_ref[...], preferred_element_type=jnp.float32
            ).astype(side_ref.dtype)

    side_sq = jnp.zeros((1, 1), jnp.float32)
    for ref, columns_side in zip(right_refs, (core, 1 - core)):
        both = jnp.dot(side_ref[...], ref[...], preferred_element_type=jnp.float32)
        width = ref.shape[1]
        both_ref[:, pl.ds(pl.multiple_of(columns_side * width, 128), width)] = both
        side_sq += jnp.sum(jnp.sum(both * both, axis=0, keepdims=True), axis=1, keepdims=True)
    side_sq_ref[...] = jnp.broadcast_to(side_sq, side_sq_ref.shape)
    for j, out_ref in zip(early, early_refs):
        row = pl.multiple_of((place ^ j) * slab, slab)
        for k, piece in enumerate(slab_for(both_ref, core, row, slab)):
            out_ref[k] = piece.astype(out_ref.dtype)


def scale_kernel(rounds, late, mine_sq_ref, theirs_sq_ref, grad_sq_ref, both_ref, graft_ref, *out_refs):
    side, place, core = device_place(rounds)
    slab = both_ref.shape[0] // rounds
    side_sq = mine_sq_ref[...] + theirs_sq_ref[...]
    graft_ref[...] = jnp.sqrt(grad_sq_ref[...] / (side_sq + 1e-06))
    graft = graft_ref[0:1, 0:1]
    for j, out_ref in zip(late, out_refs):
        row = pl.multiple_of((place ^ j) * slab, slab)
        for k, piece in enumerate(slab_for(both_ref, core, row, slab, graft)):
            out_ref[k] = piece.astype(out_ref.dtype)


def gram_kernel(owner_ref, summed_ref, left_ref, right_ref, after_ref, left_out, right_out):
    half = left_ref.shape[0]
    first = pl.multiple_of(lax.axis_index("replica") * half, 128)
    present = block_of(owner_ref, lax.axis_index("shard")) >= 0
    share = jnp.where(present, 0.01, 0.0).astype(jnp.float32)
    summed = summed_ref[...]
    left_term = lax.dot_general(
        summed_ref[pl.ds(first, half), :], summed, (((1,), (1,)), ((), ())),
        preferred_element_type=jnp.float32,
    )
    left_out[...] = (0.99 * left_ref[...].astype(jnp.float32) + share * left_term).astype(
        left_out.dtype
    )
    right_term = lax.dot_general(
        summed_ref[:, pl.ds(first, half)], summed, (((0,), (0,)), ((), ())),
        preferred_element_type=jnp.float32,
    )
    right_out[...] = (0.99 * right_ref[...].astype(jnp.float32) + share * right_term).astype(
        right_out.dtype
    )


def place_kernel(rounds, early, owner_ref, *refs):
    slabs = (refs[:rounds], refs[rounds:2 * rounds])
    grafts = refs[2 * rounds:2 * rounds + 2 * len(early)]
    out_ref, scaled_ref, sem = refs[2 * rounds + 2 * len(early):]
    side, place, core = device_place(rounds)
    pending = []
    for j in [j for j in range(rounds) if j not in early] + list(early):
        for k in range(2):
            owner = (side ^ core ^ k) * rounds + (place ^ j)
            block = block_of(owner_ref, owner)
            source = slabs[k][j].at[0] if k == 0 else slabs[k][j]
            if j in early:
                n = 2 * early.index(j) + k
                ref = slabs[k][j]
                value = ref[0] if k == 0 else ref[...]
                scaled = value.astype(jnp.float32) * grafts[n][0:1, 0:1]
                scaled_ref[n] = scaled.astype(scaled_ref.dtype)
                source = scaled_ref.at[n]
            copy = pltpu.make_async_copy(
                source, out_ref.at[jnp.maximum(block, 0)], sem.at[2 * j + k]
            )

            @pl.when(block >= 0)
            def _(copy=copy):
                copy.start()

            pending.append((block, copy))
    for block, copy in pending:

        @pl.when(block >= 0)
        def _(copy=copy):
            copy.wait()


def per_device_paired(gradients, block_owner, left_gram, right_gram, left_root, right_root):
    rounds = lax.axis_size("shard") // 2
    blocks, slab, width = gradients.shape[1:]
    half_rows = left_gram.shape[1]
    order = [j for i in range((rounds + 1) // 2) for j in dict.fromkeys((i + rounds // 2, i))]
    early, late = order[:EARLY], order[EARLY:]
    places = [(h, l, r) for h in range(2) for l in range(rounds) for r in range(2)]

    def device(h, l, r):
        return (h * rounds + l) * 2 + r

    def other_core(x):
        return lax.ppermute(x, "replica", [(0, 1), (1, 0)])

    def trade(x, j):
        pairs = [(device(h, l, r), device(h ^ r, l ^ j, r)) for h, l, r in places]
        return lax.ppermute(x, ("shard", "replica"), pairs)

    def shape(dims, dtype=jnp.bfloat16):
        return jax.ShapeDtypeStruct(dims, dtype)

    def call(kernel, out_shape, in_specs, *args, **options):
        return pl.pallas_call(
            kernel, out_shape=out_shape, in_specs=in_specs, compiler_params=PARAMS, **options
        )(*args)

    other_gradient = other_core(gradients[0])
    fetched = call(
        fetch_kernel, shape((rounds, slab, width)), [SMEM, VMEM], block_owner, gradients[0],
        out_specs=VMEM,
    )
    outgoing = call(
        pick_kernel, [shape((slab, width))] * rounds, [SMEM, VMEM, VMEM],
        block_owner, fetched, other_gradient, out_specs=[VMEM] * rounds,
    )
    mine = {j: trade(outgoing[j], j) for j in order}
    other_right = other_core(right_root[0])
    other_left = other_core(left_root[0])
    theirs = {j: other_core(mine[j]) for j in order}
    one = shape((8, 128), jnp.float32)
    slab_shape = shape((2, slab, width // 2))
    summed, both_sides, side_sq, grad_sq, *first = call(
        functools.partial(precondition_kernel, rounds, early),
        [shape((width, width)), shape((half_rows, width), jnp.float32), one, one]
        + [slab_shape] * len(early),
        [VMEM] * (2 * rounds + 4),
        *[mine[j] for j in range(rounds)], *[theirs[j] for j in range(rounds)],
        left_root[0], other_left, right_root[0], other_right,
        out_specs=[VMEM] * (4 + len(early)),
        scratch_shapes=[pltpu.VMEM((half_rows, width), jnp.bfloat16)],
    )
    returned = {j: trade(x, j) for j, x in zip(early, first)}
    graft, *rest = call(
        functools.partial(scale_kernel, rounds, late),
        [shape((8, 128), jnp.float32)] + [slab_shape] * len(late),
        [VMEM] * 4, side_sq, other_core(side_sq), grad_sq, both_sides,
        out_specs=[VMEM] * (1 + len(late)),
    )
    returned.update((j, trade(x, j)) for j, x in zip(late, rest))
    grafts = []
    if early:
        graft, returned[order[0]] = lax.optimization_barrier((graft, returned[order[0]]))
    for j in early:
        came = trade(graft, j)
        grafts += [came, other_core(came)]
    left_new, right_new = call(
        gram_kernel, [shape(left_gram.shape[1:]), shape(right_gram.shape[1:])],
        [SMEM, VMEM, VMEM, VMEM, ANY],
        block_owner, summed, left_gram[0], right_gram[0], returned[order[0]],
        out_specs=[VMEM, VMEM],
        cost_estimate=pl.CostEstimate(
            flops=4 * half_rows * width * width, bytes_accessed=8 * half_rows * width,
            transcendentals=0,
        ),
    )
    left_new, right_new, returned[order[-1]] = lax.optimization_barrier(
        (left_new, right_new, returned[order[-1]])
    )
    passed = {j: other_core(returned[j][1]) for j in order}
    update = call(
        functools.partial(place_kernel, rounds, early), shape((blocks, slab, width // 2)),
        [SMEM] + [VMEM] * (2 * rounds + len(grafts)), block_owner,
        *[returned[j] for j in range(rounds)], *[passed[j] for j in range(rounds)], *grafts,
        out_specs=ANY,
        scratch_shapes=[
            pltpu.VMEM((max(1, 2 * len(early)), slab, width // 2), jnp.bfloat16),
            pltpu.SemaphoreType.DMA((2 * rounds,)),
        ],
    )
    return (left_new[None], right_new[None], update)


def solution(mesh):
    owners = mesh.shape["shard"]
    paired = mesh.shape["replica"] == 2 and owners in (2, 4, 8, 16)
    return jax.shard_map(
        per_device_paired if paired else per_device,
        mesh=mesh,
        in_specs=(
            P("replica", "groups", "shard", None),
            P("groups"),
            P(("groups", "shard"), "replica", None),
            P(("groups", "shard"), "replica", None),
            P(("groups", "shard"), "replica", None),
            P(("groups", "shard"), None, "replica"),
        ),
        out_specs=(
            P(("groups", "shard"), "replica", None),
            P(("groups", "shard"), "replica", None),
            P("groups", "shard", "replica"),
        ),
        check_vma=False,
    )
```

```python
import functools

import jax
import jax.numpy as jnp
from jax import lax
from jax.experimental import pallas as pl
from jax.experimental.pallas import tpu as pltpu
from jax.sharding import PartitionSpec as P

VMEM = pl.BlockSpec(memory_space=pltpu.VMEM)
SMEM = pl.BlockSpec(memory_space=pltpu.SMEM)
ANY = pl.BlockSpec(memory_space=pl.ANY)
EARLY = 0
PARAMS = pltpu.CompilerParams(vmem_limit_bytes=24 * 1024 * 1024)


def per_device(gradients, block_owner, left_gram, right_gram, left_root, right_root):
    owners = lax.axis_size("shard")
    half_rows = left_gram.shape[1]
    full_width = left_gram.shape[2]
    first_row = lax.axis_index("replica") * half_rows
    owner_index = lax.broadcasted_iota(jnp.int32, (owners, block_owner.shape[0]), 0)
    owner_onehot = (owner_index == block_owner[None, :]).astype(jnp.bfloat16)
    outgoing = jnp.einsum(
        "ob,brc->orc", owner_onehot, gradients[0], preferred_element_type=jnp.float32
    )
    arrived = lax.all_to_all(
        outgoing.astype(jnp.bfloat16), "shard", split_axis=0, concat_axis=0, tiled=True
    )
    total = lax.psum(arrived.astype(jnp.float32).astype(jnp.bfloat16), "replica")
    summed_block = total.reshape(full_width, full_width)
    own_rows = lax.dynamic_slice_in_dim(summed_block, first_row, half_rows, 0)
    own_cols = lax.dynamic_slice_in_dim(summed_block, first_row, half_rows, 1)
    left_term = lax.dot_general(
        own_rows, summed_block, (((1,), (1,)), ((), ())), preferred_element_type=jnp.float32
    )
    right_term = lax.dot_general(
        own_cols, summed_block, (((0,), (0,)), ((), ())), preferred_element_type=jnp.float32
    )
    left_new = (0.99 * left_gram[0].astype(jnp.float32) + 0.01 * left_term).astype(jnp.bfloat16)
    right_new = (0.99 * right_gram[0].astype(jnp.float32) + 0.01 * right_term).astype(jnp.bfloat16)
    partial_side = jnp.dot(left_root[0], summed_block, preferred_element_type=jnp.float32).astype(
        jnp.bfloat16
    )
    left_side = lax.all_gather(partial_side, "replica", axis=0, tiled=True)
    both_sides = jnp.dot(left_side, right_root[0], preferred_element_type=jnp.float32)
    side_squares = lax.psum(jnp.sum(both_sides * both_sides), "replica")
    grad_squares = jnp.sum(jnp.square(summed_block.astype(jnp.float32)))
    graft = jnp.sqrt(grad_squares / (side_squares + 1e-06))
    scaled = (
        (both_sides * graft).astype(jnp.bfloat16).reshape(owners, full_width // owners, half_rows)
    )
    returned = lax.all_to_all(scaled, "shard", split_axis=0, concat_axis=0, tiled=True)
    update = jnp.take(returned, block_owner, axis=0)
    return (left_new[None], right_new[None], update)


def device_place(rounds):
    shard = lax.axis_index("shard")
    return lax.div(shard, rounds), lax.rem(shard, rounds), lax.axis_index("replica")


def block_of(owner_ref, owner):
    block = jnp.int32(-1)
    for b in range(owner_ref.shape[0]):
        block = jnp.where(owner_ref[b] == owner, b, block)
    return block


def sent_block(owner_ref, rounds, j):
    side, place, core = device_place(rounds)
    return jnp.maximum(block_of(owner_ref, (side ^ core) * rounds + (place ^ j)), 0)


def fetch_kernel(owner_ref, gradient_ref, out_ref):
    rounds = out_ref.shape[0]
    for j in range(rounds):
        out_ref[j] = gradient_ref[sent_block(owner_ref, rounds, j)]


def pick_kernel(owner_ref, mine_ref, theirs_ref, *out_refs):
    rounds = len(out_refs)
    for j, out_ref in enumerate(out_refs):
        other = theirs_ref[sent_block(owner_ref, rounds, j)]
        total = mine_ref[j].astype(jnp.float32) + other.astype(jnp.float32)
        out_ref[...] = total.astype(out_ref.dtype)


def slab_for(ref, keep, row, slab, scale=None):
    width = ref.shape[1] // 2
    pieces = []
    for side in (keep, 1 - keep):
        piece = ref[pl.ds(row, slab), pl.ds(pl.multiple_of(side * width, 128), width)]
        pieces.append(piece if scale is None else piece * scale)
    return pieces


def precondition_kernel(rounds, early, *refs):
    mine, theirs = refs[:rounds], refs[rounds:2 * rounds]
    left_refs, right_refs = refs[2 * rounds:2 * rounds + 2], refs[2 * rounds + 2:2 * rounds + 4]
    summed_ref, both_ref, side_sq_ref, grad_sq_ref = refs[2 * rounds + 4:2 * rounds + 8]
    early_refs, side_ref = refs[2 * rounds + 8:-1], refs[-1]
    side, place, core = device_place(rounds)
    slab, full = mine[0].shape
    half = rounds * slab
    grad_sq = jnp.zeros((1, full), jnp.float32)
    for j in range(rounds):
        for ref, rows_side in ((mine[j], side ^ core), (theirs[j], side ^ (1 - core))):
            row = pl.multiple_of(rows_side * half + (place ^ j) * slab, slab)
            block = ref[...]
            summed_ref[pl.ds(row, slab), :] = block
            wide = block.astype(jnp.float32)
            grad_sq += jnp.sum(wide * wide, axis=0, keepdims=True)
    total = jnp.sum(grad_sq, axis=1, keepdims=True)
    grad_sq_ref[...] = jnp.broadcast_to(total, grad_sq_ref.shape)
    for h, left_ref in enumerate(left_refs):

        @pl.when(side == h)
        def _(left_ref=left_ref):
            side_ref[...] = jnp.dot(
                left_ref[...], summed_ref[...], preferred_element_type=jnp.float32
            ).astype(side_ref.dtype)

    side_sq = jnp.zeros((1, 1), jnp.float32)
    for ref, columns_side in zip(right_refs, (core, 1 - core)):
        both = jnp.dot(side_ref[...], ref[...], preferred_element_type=jnp.float32)
        width = ref.shape[1]
        both_ref[:, pl.ds(pl.multiple_of(columns_side * width, 128), width)] = both
        side_sq += jnp.sum(jnp.sum(both * both, axis=0, keepdims=True), axis=1, keepdims=True)
    side_sq_ref[...] = jnp.broadcast_to(side_sq, side_sq_ref.shape)
    for j, out_ref in zip(early, early_refs):
        row = pl.multiple_of((place ^ j) * slab, slab)
        for k, piece in enumerate(slab_for(both_ref, core, row, slab)):
            out_ref[k] = piece.astype(out_ref.dtype)


def scale_kernel(rounds, late, mine_sq_ref, theirs_sq_ref, grad_sq_ref, both_ref, graft_ref, *out_refs):
    side, place, core = device_place(rounds)
    slab = both_ref.shape[0] // rounds
    side_sq = mine_sq_ref[...] + theirs_sq_ref[...]
    graft_ref[...] = jnp.sqrt(grad_sq_ref[...] / (side_sq + 1e-06))
    graft = graft_ref[0:1, 0:1]
    for j, out_ref in zip(late, out_refs):
        row = pl.multiple_of((place ^ j) * slab, slab)
        for k, piece in enumerate(slab_for(both_ref, core, row, slab, graft)):
            out_ref[k] = piece.astype(out_ref.dtype)


def gram_kernel(owner_ref, summed_ref, left_ref, right_ref, after_ref, left_out, right_out):
    half = left_ref.shape[0]
    first = pl.multiple_of(lax.axis_index("replica") * half, 128)
    present = block_of(owner_ref, lax.axis_index("shard")) >= 0
    share = jnp.where(present, 0.01, 0.0).astype(jnp.float32)
    summed = summed_ref[...]
    left_term = lax.dot_general(
        summed_ref[pl.ds(first, half), :], summed, (((1,), (1,)), ((), ())),
        preferred_element_type=jnp.float32,
    )
    left_out[...] = (0.99 * left_ref[...].astype(jnp.float32) + share * left_term).astype(
        left_out.dtype
    )
    right_term = lax.dot_general(
        summed_ref[:, pl.ds(first, half)], summed, (((0,), (0,)), ((), ())),
        preferred_element_type=jnp.float32,
    )
    right_out[...] = (0.99 * right_ref[...].astype(jnp.float32) + share * right_term).astype(
        right_out.dtype
    )


def place_kernel(rounds, early, owner_ref, *refs):
    slabs = (refs[:rounds], refs[rounds:2 * rounds])
    grafts = refs[2 * rounds:2 * rounds + 2 * len(early)]
    out_ref, scaled_ref, sem = refs[2 * rounds + 2 * len(early):]
    side, place, core = device_place(rounds)
    pending = []
    for j in [j for j in range(rounds) if j not in early] + list(early):
        for k in range(2):
            owner = (side ^ core ^ k) * rounds + (place ^ j)
            block = block_of(owner_ref, owner)
            source = slabs[k][j].at[0] if k == 0 else slabs[k][j]
            if j in early:
                n = 2 * early.index(j) + k
                ref = slabs[k][j]
                value = ref[0] if k == 0 else ref[...]
                scaled = value.astype(jnp.float32) * grafts[n][0:1, 0:1]
                scaled_ref[n] = scaled.astype(scaled_ref.dtype)
                source = scaled_ref.at[n]
            copy = pltpu.make_async_copy(
                source, out_ref.at[jnp.maximum(block, 0)], sem.at[2 * j + k]
            )

            @pl.when(block >= 0)
            def _(copy=copy):
                copy.start()

            pending.append((block, copy))
    for block, copy in pending:

        @pl.when(block >= 0)
        def _(copy=copy):
            copy.wait()


def per_device_paired(gradients, block_owner, left_gram, right_gram, left_root, right_root):
    rounds = lax.axis_size("shard") // 2
    blocks, slab, width = gradients.shape[1:]
    half_rows = left_gram.shape[1]
    order = [j for i in range((rounds + 1) // 2) for j in dict.fromkeys((i + rounds // 2, i))]
    early, late = order[:EARLY], order[EARLY:]
    places = [(h, l, r) for h in range(2) for l in range(rounds) for r in range(2)]

    def device(h, l, r):
        return (h * rounds + l) * 2 + r

    def other_core(x):
        return lax.ppermute(x, "replica", [(0, 1), (1, 0)])

    def trade(x, j):
        pairs = [(device(h, l, r), device(h ^ r, l ^ j, r)) for h, l, r in places]
        return lax.ppermute(x, ("shard", "replica"), pairs)

    def shape(dims, dtype=jnp.bfloat16):
        return jax.ShapeDtypeStruct(dims, dtype)

    def call(kernel, out_shape, in_specs, *args, **options):
        return pl.pallas_call(
            kernel, out_shape=out_shape, in_specs=in_specs, compiler_params=PARAMS, **options
        )(*args)

    other_gradient = other_core(gradients[0])
    fetched = call(
        fetch_kernel, shape((rounds, slab, width)), [SMEM, VMEM], block_owner, gradients[0],
        out_specs=VMEM,
    )
    outgoing = call(
        pick_kernel, [shape((slab, width))] * rounds, [SMEM, VMEM, VMEM],
        block_owner, fetched, other_gradient, out_specs=[VMEM] * rounds,
    )
    mine = {j: trade(outgoing[j], j) for j in order}
    other_right = other_core(right_root[0])
    other_left = other_core(left_root[0])
    theirs = {j: other_core(mine[j]) for j in order}
    one = shape((8, 128), jnp.float32)
    slab_shape = shape((2, slab, width // 2))
    summed, both_sides, side_sq, grad_sq, *first = call(
        functools.partial(precondition_kernel, rounds, early),
        [shape((width, width)), shape((half_rows, width), jnp.float32), one, one]
        + [slab_shape] * len(early),
        [VMEM] * (2 * rounds + 4),
        *[mine[j] for j in range(rounds)], *[theirs[j] for j in range(rounds)],
        left_root[0], other_left, right_root[0], other_right,
        out_specs=[VMEM] * (4 + len(early)),
        scratch_shapes=[pltpu.VMEM((half_rows, width), jnp.bfloat16)],
    )
    returned = {j: trade(x, j) for j, x in zip(early, first)}
    graft, *rest = call(
        functools.partial(scale_kernel, rounds, late),
        [shape((8, 128), jnp.float32)] + [slab_shape] * len(late),
        [VMEM] * 4, side_sq, other_core(side_sq), grad_sq, both_sides,
        out_specs=[VMEM] * (1 + len(late)),
    )
    returned.update((j, trade(x, j)) for j, x in zip(late, rest))
    grafts = []
    if early:
        graft, returned[order[0]] = lax.optimization_barrier((graft, returned[order[0]]))
    for j in early:
        came = trade(graft, j)
        grafts += [came, other_core(came)]
    left_new, right_new = call(
        gram_kernel, [shape(left_gram.shape[1:]), shape(right_gram.shape[1:])],
        [SMEM, VMEM, VMEM, VMEM, ANY],
        block_owner, summed, left_gram[0], right_gram[0], returned[order[0]],
        out_specs=[VMEM, VMEM],
        cost_estimate=pl.CostEstimate(
            flops=4 * half_rows * width * width, bytes_accessed=8 * half_rows * width,
            transcendentals=0,
        ),
    )
    left_new, right_new, returned[order[-1]] = lax.optimization_barrier(
        (left_new, right_new, returned[order[-1]])
    )
    passed = {j: other_core(returned[j][1]) for j in order}
    update = call(
        functools.partial(place_kernel, rounds, early), shape((blocks, slab, width // 2)),
        [SMEM] + [VMEM] * (2 * rounds + len(grafts)), block_owner,
        *[returned[j] for j in range(rounds)], *[passed[j] for j in range(rounds)], *grafts,
        out_specs=ANY,
        scratch_shapes=[
            pltpu.VMEM((max(1, 2 * len(early)), slab, width // 2), jnp.bfloat16),
            pltpu.SemaphoreType.DMA((2 * rounds,)),
        ],
    )
    return (left_new[None], right_new[None], update)


def solution(mesh):
    owners = mesh.shape["shard"]
    paired = mesh.shape["replica"] == 2 and owners in (2, 4, 8, 16)
    return jax.shard_map(
        per_device_paired if paired else per_device,
        mesh=mesh,
        in_specs=(
            P("replica", "groups", "shard", None),
            P("groups"),
            P(("groups", "shard"), "replica", None),
            P(("groups", "shard"), "replica", None),
            P(("groups", "shard"), "replica", None),
            P(("groups", "shard"), None, "replica"),
        ),
        out_specs=(
            P(("groups", "shard"), "replica", None),
            P(("groups", "shard"), "replica", None),
            P("groups", "shard", "replica"),
        ),
        check_vma=False,
    )
```

```python
import functools

import jax
import jax.numpy as jnp
from jax import lax
from jax.experimental import pallas as pl
from jax.experimental.pallas import tpu as pltpu
from jax.sharding import PartitionSpec as P

VMEM = pl.BlockSpec(memory_space=pltpu.VMEM)
SMEM = pl.BlockSpec(memory_space=pltpu.SMEM)
ANY = pl.BlockSpec(memory_space=pl.ANY)
LIGHT = pl.CostEstimate(flops=0, bytes_accessed=0, transcendentals=0)
PARAMS = pltpu.CompilerParams(vmem_limit_bytes=24 * 1024 * 1024)


def per_device(gradients, block_owner, left_gram, right_gram, left_root, right_root):
    owners = lax.axis_size("shard")
    half_rows = left_gram.shape[1]
    full_width = left_gram.shape[2]
    first_row = lax.axis_index("replica") * half_rows
    owner_index = lax.broadcasted_iota(jnp.int32, (owners, block_owner.shape[0]), 0)
    owner_onehot = (owner_index == block_owner[None, :]).astype(jnp.bfloat16)
    outgoing = jnp.einsum(
        "ob,brc->orc", owner_onehot, gradients[0], preferred_element_type=jnp.float32
    )
    arrived = lax.all_to_all(
        outgoing.astype(jnp.bfloat16), "shard", split_axis=0, concat_axis=0, tiled=True
    )
    total = lax.psum(arrived.astype(jnp.float32).astype(jnp.bfloat16), "replica")
    summed_block = total.reshape(full_width, full_width)
    own_rows = lax.dynamic_slice_in_dim(summed_block, first_row, half_rows, 0)
    own_cols = lax.dynamic_slice_in_dim(summed_block, first_row, half_rows, 1)
    left_term = lax.dot_general(
        own_rows, summed_block, (((1,), (1,)), ((), ())), preferred_element_type=jnp.float32
    )
    right_term = lax.dot_general(
        own_cols, summed_block, (((0,), (0,)), ((), ())), preferred_element_type=jnp.float32
    )
    left_new = (0.99 * left_gram[0].astype(jnp.float32) + 0.01 * left_term).astype(jnp.bfloat16)
    right_new = (0.99 * right_gram[0].astype(jnp.float32) + 0.01 * right_term).astype(jnp.bfloat16)
    partial_side = jnp.dot(left_root[0], summed_block, preferred_element_type=jnp.float32).astype(
        jnp.bfloat16
    )
    left_side = lax.all_gather(partial_side, "replica", axis=0, tiled=True)
    both_sides = jnp.dot(left_side, right_root[0], preferred_element_type=jnp.float32)
    side_squares = lax.psum(jnp.sum(both_sides * both_sides), "replica")
    grad_squares = jnp.sum(jnp.square(summed_block.astype(jnp.float32)))
    graft = jnp.sqrt(grad_squares / (side_squares + 1e-06))
    scaled = (
        (both_sides * graft).astype(jnp.bfloat16).reshape(owners, full_width // owners, half_rows)
    )
    returned = lax.all_to_all(scaled, "shard", split_axis=0, concat_axis=0, tiled=True)
    update = jnp.take(returned, block_owner, axis=0)
    return (left_new[None], right_new[None], update)


def codes_of(owners):
    half, quarter = owners // 2, owners // 4
    return (
        [half + i for i in range(quarter)] + [i for i in reversed(range(quarter))],
        [half + quarter + i for i in range(quarter)] + [quarter + i for i in range(quarter)],
    )


def partner(codes, k, other=False):
    core = lax.axis_index("replica")
    first = core == (1 if other else 0)
    return lax.axis_index("shard") ^ jnp.where(first, codes[0][k], codes[1][k])


def block_of(owner_ref, owner):
    block = jnp.int32(-1)
    for b in range(owner_ref.shape[0]):
        block = jnp.where(owner_ref[b] == owner, b, block)
    return block


def sent_block(codes, owner_ref, k):
    return jnp.maximum(block_of(owner_ref, partner(codes, k)), 0)


def squares(value):
    wide = value.astype(jnp.float32)
    return jnp.sum(jnp.sum(wide * wide, axis=0, keepdims=True), axis=1, keepdims=True)


def fetch_kernel(codes, owner_ref, gradient_ref, out_ref):
    for k in range(out_ref.shape[0]):
        out_ref[k] = gradient_ref[sent_block(codes, owner_ref, k)]


def pick_kernel(codes, owner_ref, mine_ref, theirs_ref, *out_refs):
    for k, out_ref in enumerate(out_refs):
        other = theirs_ref[sent_block(codes, owner_ref, k)]
        total = mine_ref[k].astype(jnp.float32) + other.astype(jnp.float32)
        out_ref[...] = total.astype(out_ref.dtype)


def order_kernel(codes, slots, own_ref, other_ref, *refs):
    out_refs, rows_ref = refs[:-1], refs[-1]
    half, full = own_ref.shape
    rounds = len(codes[0])
    slab = half // rounds
    core = lax.axis_index("replica")
    for k in range(rounds):
        shard = partner(codes, k)
        row = pl.multiple_of(lax.rem(shard, rounds) * slab, slab)
        for ref, near in ((own_ref, True), (other_ref, False)):

            @pl.when((lax.div(shard, rounds) == core) == near)
            def _(ref=ref):
                rows_ref[k * slab:(k + 1) * slab, :] = ref[pl.ds(row, slab), :]

    for out_ref, group in zip(out_refs, slots):
        column = lax.broadcasted_iota(jnp.int32, (1, len(group) * slab), 1)
        source = column
        for n, (k, other) in enumerate(group):
            inside = (column >= n * slab) & (column < (n + 1) * slab)
            shift = (partner(codes, k, other) - n) * slab
            source = jnp.where(inside, column + shift, source)
        row_index = lax.broadcasted_iota(jnp.int32, (full, len(group) * slab), 0)
        choose = (row_index == source).astype(jnp.float32).astype(rows_ref.dtype)
        out_ref[...] = jnp.dot(
            rows_ref[...], choose, preferred_element_type=jnp.float32
        ).astype(out_ref.dtype)


def begin_kernel(left_ref, *refs):
    *slabs, total_ref, grad_sq_ref, stacked_ref = refs
    slab = slabs[0].shape[0]
    for n, ref in enumerate(slabs):
        stacked_ref[n * slab:(n + 1) * slab, :] = ref[...]
    total_ref[...] = jnp.dot(
        left_ref[...], stacked_ref[...], preferred_element_type=jnp.float32
    )
    grad_sq_ref[...] = jnp.broadcast_to(squares(stacked_ref[...]), grad_sq_ref.shape)


def finish_kernel(early, left_ref, total_ref, begun_sq_ref, own_ref, other_ref, *refs):
    *slabs, both_ref, side_sq_ref, grad_sq_ref = refs[:-2 - len(early)]
    early_refs, stacked_ref, side_ref = refs[-2 - len(early):-2], refs[-2], refs[-1]
    slab = slabs[0].shape[0]
    for n, ref in enumerate(slabs):
        stacked_ref[n * slab:(n + 1) * slab, :] = ref[...]
    side = total_ref[...] + jnp.dot(
        left_ref[...], stacked_ref[...], preferred_element_type=jnp.float32
    )
    side_ref[...] = side.astype(side_ref.dtype)
    side_sq = jnp.zeros((1, 1), jnp.float32)
    for n, ref in enumerate((own_ref, other_ref)):
        both = jnp.dot(side_ref[...], ref[...], preferred_element_type=jnp.float32)
        both_ref[n] = both
        side_sq += squares(both)
        for k, out_ref in zip(early, early_refs):
            out_ref[n] = both[k * slab:(k + 1) * slab].astype(out_ref.dtype)
    side_sq_ref[...] = jnp.broadcast_to(side_sq, side_sq_ref.shape)
    grad_sq_ref[...] = begun_sq_ref[...] + squares(stacked_ref[...])


def scale_kernel(late, mine_sq_ref, theirs_sq_ref, grad_sq_ref, both_ref, graft_ref, *out_refs):
    side_sq = mine_sq_ref[...] + theirs_sq_ref[...]
    graft_ref[...] = jnp.sqrt(grad_sq_ref[...] / (side_sq + 1e-06))
    graft = graft_ref[0:1, 0:1]
    for k, out_ref in zip(late, out_refs):
        slab = out_ref.shape[1]
        for n in range(2):
            piece = both_ref[n, k * slab:(k + 1) * slab] * graft
            out_ref[n] = piece.astype(out_ref.dtype)


def gram_kernel(codes, owner_ref, left_ref, right_ref, after_ref, *refs):
    rounds = len(codes[0])
    slabs, (left_out, right_out, summed_ref) = refs[:2 * rounds], refs[2 * rounds:]
    slab = slabs[0].shape[0]
    for k in range(rounds):
        for ref, other in ((slabs[k], False), (slabs[rounds + k], True)):
            row = pl.multiple_of(partner(codes, k, other) * slab, slab)
            summed_ref[pl.ds(row, slab), :] = ref[...]
    half = left_ref.shape[0]
    first = pl.multiple_of(lax.axis_index("replica") * half, 128)
    present = block_of(owner_ref, lax.axis_index("shard")) >= 0
    share = jnp.where(present, 0.01, 0.0).astype(jnp.float32)
    summed = summed_ref[...]
    left_term = lax.dot_general(
        summed_ref[pl.ds(first, half), :], summed, (((1,), (1,)), ((), ())),
        preferred_element_type=jnp.float32,
    )
    left_out[...] = (0.99 * left_ref[...].astype(jnp.float32) + share * left_term).astype(
        left_out.dtype
    )
    right_term = lax.dot_general(
        summed_ref[:, pl.ds(first, half)], summed, (((0,), (0,)), ((), ())),
        preferred_element_type=jnp.float32,
    )
    right_out[...] = (0.99 * right_ref[...].astype(jnp.float32) + share * right_term).astype(
        right_out.dtype
    )


def place_kernel(codes, early, owner_ref, *refs):
    rounds = len(codes[0])
    slabs = (refs[:rounds], refs[rounds:2 * rounds])
    grafts = refs[2 * rounds:2 * rounds + 2 * len(early)]
    out_ref, scaled_ref, sem = refs[2 * rounds + 2 * len(early):]
    pending = []
    for k in [k for k in range(rounds) if k not in early] + list(early):
        for n in range(2):
            block = block_of(owner_ref, partner(codes, k, n == 1))
            source = slabs[n][k].at[0] if n == 0 else slabs[n][k]
            if k in early:
                m = 2 * early.index(k) + n
                scaled = source[...].astype(jnp.float32) * grafts[m][0:1, 0:1]
                scaled_ref[m] = scaled.astype(scaled_ref.dtype)
                source = scaled_ref.at[m]
            copy = pltpu.make_async_copy(
                source, out_ref.at[jnp.maximum(block, 0)], sem.at[2 * k + n]
            )

            @pl.when(block >= 0)
            def _(copy=copy):
                copy.start()

            pending.append((block, copy))
    for block, copy in pending:

        @pl.when(block >= 0)
        def _(copy=copy):
            copy.wait()


def per_device_paired(gradients, block_owner, left_gram, right_gram, left_root, right_root):
    owners = lax.axis_size("shard")
    rounds = owners // 2
    codes = codes_of(owners)
    blocks, slab, width = gradients.shape[1:]
    half_rows = left_gram.shape[1]
    last = owners // 4 - 1
    early = [0]
    late = [k for k in range(rounds) if k not in early]
    sooner = [(k, other) for k in range(rounds) if k != last for other in (False, True)]
    slots = (sooner, [(last, False), (last, True)])

    def other_core(x):
        return lax.ppermute(x, "replica", [(0, 1), (1, 0)])

    def trade(x, k):
        pairs = [(s * 2 + r, (s ^ codes[r][k]) * 2 + r) for s in range(owners) for r in range(2)]
        return lax.ppermute(x, ("shard", "replica"), pairs)

    def shape(dims, dtype=jnp.bfloat16):
        return jax.ShapeDtypeStruct(dims, dtype)

    def call(kernel, out_shape, in_specs, *args, cost_estimate=LIGHT, **options):
        return pl.pallas_call(
            kernel, out_shape=out_shape, in_specs=in_specs, compiler_params=PARAMS,
            cost_estimate=cost_estimate, **options
        )(*args)

    one = shape((8, 128), jnp.float32)
    other_gradient = other_core(gradients[0])
    fetched = call(
        functools.partial(fetch_kernel, codes), shape((rounds, slab, width)), [SMEM, VMEM],
        block_owner, gradients[0], out_specs=VMEM,
    )
    outgoing = call(
        functools.partial(pick_kernel, codes), [shape((slab, width))] * rounds,
        [SMEM, VMEM, VMEM], block_owner, fetched, other_gradient, out_specs=[VMEM] * rounds,
    )
    mine = [trade(outgoing[k], k) for k in range(rounds)]
    other_right = other_core(right_root[0])
    other_left = other_core(left_root[0])
    left_sooner, left_last = call(
        functools.partial(order_kernel, codes, slots),
        [shape((half_rows, len(group) * slab)) for group in slots], [VMEM, VMEM],
        left_root[0], other_left, out_specs=[VMEM, VMEM],
        scratch_shapes=[pltpu.VMEM((half_rows, width), jnp.bfloat16)],
    )
    mine[last], left_sooner, left_last = lax.optimization_barrier(
        (mine[last], left_sooner, left_last)
    )
    theirs = [other_core(x) for x in mine]
    begun, begun_sq = call(
        begin_kernel, [shape((half_rows, width), jnp.float32), one],
        [VMEM] * (1 + len(sooner)), left_sooner,
        *[(theirs if other else mine)[k] for k, other in sooner], out_specs=[VMEM, VMEM],
        scratch_shapes=[pltpu.VMEM((len(sooner) * slab, width), jnp.bfloat16)],
    )
    slab_shape = shape((2, slab, width // 2))
    both_sides, side_sq, grad_sq, *first = call(
        functools.partial(finish_kernel, early),
        [shape((2, half_rows, width // 2), jnp.float32), one, one] + [slab_shape] * len(early),
        [VMEM] * 7, left_last, begun, begun_sq, right_root[0], other_right,
        mine[last], theirs[last], out_specs=[VMEM] * (3 + len(early)),
        scratch_shapes=[
            pltpu.VMEM((2 * slab, width), jnp.bfloat16),
            pltpu.VMEM((half_rows, width), jnp.bfloat16),
        ],
    )
    returned = {k: trade(x, k) for k, x in zip(early, first)}
    graft, *rest = call(
        functools.partial(scale_kernel, late), [one] + [slab_shape] * len(late),
        [VMEM] * 4, side_sq, other_core(side_sq), grad_sq, both_sides,
        out_specs=[VMEM] * (1 + len(late)),
    )
    returned.update((k, trade(x, k)) for k, x in zip(late, rest))
    grafts = []
    for k in early:
        graft, returned[k] = lax.optimization_barrier((graft, returned[k]))
        came = trade(graft, k)
        grafts += [came, other_core(came)]

    left_new, right_new = call(
        functools.partial(gram_kernel, codes),
        [shape(left_gram.shape[1:]), shape(right_gram.shape[1:])],
        [SMEM, VMEM, VMEM, ANY] + [VMEM] * (2 * rounds),
        block_owner, left_gram[0], right_gram[0], grafts[0] if early else returned[0],
        *mine, *theirs, out_specs=[VMEM, VMEM],
        scratch_shapes=[pltpu.VMEM((width, width), jnp.bfloat16)],
        cost_estimate=pl.CostEstimate(
            flops=4 * half_rows * width * width, bytes_accessed=8 * half_rows * width,
            transcendentals=0,
        ),
    )
    left_new, right_new, returned[last] = lax.optimization_barrier(
        (left_new, right_new, returned[last])
    )
    passed = [other_core(returned[k][1]) for k in range(rounds)]
    update = call(
        functools.partial(place_kernel, codes, early), shape((blocks, slab, width // 2)),
        [SMEM] + [VMEM] * (2 * rounds + len(grafts)), block_owner,
        *[returned[k] for k in range(rounds)], *passed, *grafts,
        out_specs=ANY,
        scratch_shapes=[
            pltpu.VMEM((max(1, 2 * len(early)), slab, width // 2), jnp.bfloat16),
            pltpu.SemaphoreType.DMA((2 * rounds,)),
        ],
    )
    return (left_new[None], right_new[None], update)


def solution(mesh):
    owners = mesh.shape["shard"]
    paired = mesh.shape["replica"] == 2 and owners in (4, 8, 16)
    return jax.shard_map(
        per_device_paired if paired else per_device,
        mesh=mesh,
        in_specs=(
            P("replica", "groups", "shard", None),
            P("groups"),
            P(("groups", "shard"), "replica", None),
            P(("groups", "shard"), "replica", None),
            P(("groups", "shard"), "replica", None),
            P(("groups", "shard"), None, "replica"),
        ),
        out_specs=(
            P(("groups", "shard"), "replica", None),
            P(("groups", "shard"), "replica", None),
            P("groups", "shard", "replica"),
        ),
        check_vma=False,
    )
```

```python
import functools

import jax
import jax.numpy as jnp
from jax import lax
from jax.experimental import pallas as pl
from jax.experimental.pallas import tpu as pltpu
from jax.sharding import PartitionSpec as P

VMEM = pl.BlockSpec(memory_space=pltpu.VMEM)
SMEM = pl.BlockSpec(memory_space=pltpu.SMEM)
ANY = pl.BlockSpec(memory_space=pl.ANY)
LIGHT = pl.CostEstimate(flops=0, bytes_accessed=0, transcendentals=0)
PARAMS = pltpu.CompilerParams(vmem_limit_bytes=24 * 1024 * 1024)


def per_device(gradients, block_owner, left_gram, right_gram, left_root, right_root):
    owners = lax.axis_size("shard")
    half_rows = left_gram.shape[1]
    full_width = left_gram.shape[2]
    first_row = lax.axis_index("replica") * half_rows
    owner_index = lax.broadcasted_iota(jnp.int32, (owners, block_owner.shape[0]), 0)
    owner_onehot = (owner_index == block_owner[None, :]).astype(jnp.bfloat16)
    outgoing = jnp.einsum(
        "ob,brc->orc", owner_onehot, gradients[0], preferred_element_type=jnp.float32
    )
    arrived = lax.all_to_all(
        outgoing.astype(jnp.bfloat16), "shard", split_axis=0, concat_axis=0, tiled=True
    )
    total = lax.psum(arrived.astype(jnp.float32).astype(jnp.bfloat16), "replica")
    summed_block = total.reshape(full_width, full_width)
    own_rows = lax.dynamic_slice_in_dim(summed_block, first_row, half_rows, 0)
    own_cols = lax.dynamic_slice_in_dim(summed_block, first_row, half_rows, 1)
    left_term = lax.dot_general(
        own_rows, summed_block, (((1,), (1,)), ((), ())), preferred_element_type=jnp.float32
    )
    right_term = lax.dot_general(
        own_cols, summed_block, (((0,), (0,)), ((), ())), preferred_element_type=jnp.float32
    )
    left_new = (0.99 * left_gram[0].astype(jnp.float32) + 0.01 * left_term).astype(jnp.bfloat16)
    right_new = (0.99 * right_gram[0].astype(jnp.float32) + 0.01 * right_term).astype(jnp.bfloat16)
    partial_side = jnp.dot(left_root[0], summed_block, preferred_element_type=jnp.float32).astype(
        jnp.bfloat16
    )
    left_side = lax.all_gather(partial_side, "replica", axis=0, tiled=True)
    both_sides = jnp.dot(left_side, right_root[0], preferred_element_type=jnp.float32)
    side_squares = lax.psum(jnp.sum(both_sides * both_sides), "replica")
    grad_squares = jnp.sum(jnp.square(summed_block.astype(jnp.float32)))
    graft = jnp.sqrt(grad_squares / (side_squares + 1e-06))
    scaled = (
        (both_sides * graft).astype(jnp.bfloat16).reshape(owners, full_width // owners, half_rows)
    )
    returned = lax.all_to_all(scaled, "shard", split_axis=0, concat_axis=0, tiled=True)
    update = jnp.take(returned, block_owner, axis=0)
    return (left_new[None], right_new[None], update)


def codes_of(owners):
    half, quarter = owners // 2, owners // 4
    return (
        [half + i for i in range(quarter)] + [i for i in reversed(range(quarter))],
        [half + quarter + i for i in range(quarter)] + [quarter + i for i in range(quarter)],
    )


def partner(codes, k, other=False):
    core = lax.axis_index("replica")
    first = core == (1 if other else 0)
    return lax.axis_index("shard") ^ jnp.where(first, codes[0][k], codes[1][k])


def block_of(owner_ref, owner):
    block = jnp.int32(-1)
    for b in range(owner_ref.shape[0]):
        block = jnp.where(owner_ref[b] == owner, b, block)
    return block


def sent_block(codes, owner_ref, k):
    return jnp.maximum(block_of(owner_ref, partner(codes, k)), 0)


def squares(value):
    wide = value.astype(jnp.float32)
    return jnp.sum(jnp.sum(wide * wide, axis=0, keepdims=True), axis=1, keepdims=True)


def fetch_kernel(codes, owner_ref, gradient_ref, out_ref):
    for k in range(out_ref.shape[0]):
        out_ref[k] = gradient_ref[sent_block(codes, owner_ref, k)]


def pick_kernel(codes, owner_ref, mine_ref, theirs_ref, *out_refs):
    for k, out_ref in enumerate(out_refs):
        other = theirs_ref[sent_block(codes, owner_ref, k)]
        total = mine_ref[k].astype(jnp.float32) + other.astype(jnp.float32)
        out_ref[...] = total.astype(out_ref.dtype)


def order_kernel(codes, slots, own_ref, other_ref, *refs):
    out_refs, rows_ref = refs[:-1], refs[-1]
    half, full = own_ref.shape
    rounds = len(codes[0])
    slab = half // rounds
    core = lax.axis_index("replica")
    for k in range(rounds):
        shard = partner(codes, k)
        row = pl.multiple_of(lax.rem(shard, rounds) * slab, slab)
        for ref, near in ((own_ref, True), (other_ref, False)):

            @pl.when((lax.div(shard, rounds) == core) == near)
            def _(ref=ref):
                rows_ref[k * slab:(k + 1) * slab, :] = ref[pl.ds(row, slab), :]

    for out_ref, group in zip(out_refs, slots):
        column = lax.broadcasted_iota(jnp.int32, (1, len(group) * slab), 1)
        source = column
        for n, (k, other) in enumerate(group):
            inside = (column >= n * slab) & (column < (n + 1) * slab)
            shift = (partner(codes, k, other) - n) * slab
            source = jnp.where(inside, column + shift, source)
        row_index = lax.broadcasted_iota(jnp.int32, (full, len(group) * slab), 0)
        choose = (row_index == source).astype(jnp.float32).astype(rows_ref.dtype)
        out_ref[...] = jnp.dot(
            rows_ref[...], choose, preferred_element_type=jnp.float32
        ).astype(out_ref.dtype)


def begin_kernel(left_ref, *refs):
    *slabs, total_ref, grad_sq_ref, stacked_ref = refs
    slab = slabs[0].shape[0]
    for n, ref in enumerate(slabs):
        stacked_ref[n * slab:(n + 1) * slab, :] = ref[...]
    total_ref[...] = jnp.dot(
        left_ref[...], stacked_ref[...], preferred_element_type=jnp.float32
    )
    grad_sq_ref[...] = jnp.broadcast_to(squares(stacked_ref[...]), grad_sq_ref.shape)


def finish_kernel(early, left_ref, total_ref, begun_sq_ref, own_ref, other_ref, *refs):
    *slabs, both_ref, side_sq_ref, grad_sq_ref = refs[:-2 - len(early)]
    early_refs, stacked_ref, side_ref = refs[-2 - len(early):-2], refs[-2], refs[-1]
    slab = slabs[0].shape[0]
    for n, ref in enumerate(slabs):
        stacked_ref[n * slab:(n + 1) * slab, :] = ref[...]
    side = total_ref[...] + jnp.dot(
        left_ref[...], stacked_ref[...], preferred_element_type=jnp.float32
    )
    side_ref[...] = side.astype(side_ref.dtype)
    side_sq = jnp.zeros((1, 1), jnp.float32)
    for n, ref in enumerate((own_ref, other_ref)):
        both = jnp.dot(side_ref[...], ref[...], preferred_element_type=jnp.float32)
        both_ref[n] = both
        side_sq += squares(both)
        for k, out_ref in zip(early, early_refs):
            out_ref[n] = both[k * slab:(k + 1) * slab].astype(out_ref.dtype)
    side_sq_ref[...] = jnp.broadcast_to(side_sq, side_sq_ref.shape)
    grad_sq_ref[...] = begun_sq_ref[...] + squares(stacked_ref[...])


def scale_kernel(late, mine_sq_ref, theirs_sq_ref, grad_sq_ref, both_ref, graft_ref, *out_refs):
    side_sq = mine_sq_ref[...] + theirs_sq_ref[...]
    graft_ref[...] = jnp.sqrt(grad_sq_ref[...] / (side_sq + 1e-06))
    graft = graft_ref[0:1, 0:1]
    for k, out_ref in zip(late, out_refs):
        slab = out_ref.shape[1]
        for n in range(2):
            piece = both_ref[n, k * slab:(k + 1) * slab] * graft
            out_ref[n] = piece.astype(out_ref.dtype)


def gram_kernel(codes, owner_ref, left_ref, right_ref, after_ref, *refs):
    rounds = len(codes[0])
    slabs, (left_out, right_out, summed_ref) = refs[:2 * rounds], refs[2 * rounds:]
    slab = slabs[0].shape[0]
    for k in range(rounds):
        for ref, other in ((slabs[k], False), (slabs[rounds + k], True)):
            row = pl.multiple_of(partner(codes, k, other) * slab, slab)
            summed_ref[pl.ds(row, slab), :] = ref[...]
    half = left_ref.shape[0]
    first = pl.multiple_of(lax.axis_index("replica") * half, 128)
    present = block_of(owner_ref, lax.axis_index("shard")) >= 0
    share = jnp.where(present, 0.01, 0.0).astype(jnp.float32)
    summed = summed_ref[...]
    left_term = lax.dot_general(
        summed_ref[pl.ds(first, half), :], summed, (((1,), (1,)), ((), ())),
        preferred_element_type=jnp.float32,
    )
    left_out[...] = (0.99 * left_ref[...].astype(jnp.float32) + share * left_term).astype(
        left_out.dtype
    )
    right_term = lax.dot_general(
        summed_ref[:, pl.ds(first, half)], summed, (((0,), (0,)), ((), ())),
        preferred_element_type=jnp.float32,
    )
    right_out[...] = (0.99 * right_ref[...].astype(jnp.float32) + share * right_term).astype(
        right_out.dtype
    )


def place_kernel(codes, early, owner_ref, *refs):
    rounds = len(codes[0])
    slabs = (refs[:rounds], refs[rounds:2 * rounds])
    grafts = refs[2 * rounds:2 * rounds + 2 * len(early)]
    out_ref, scaled_ref, sem = refs[2 * rounds + 2 * len(early):]
    pending = []
    for k in [k for k in range(rounds) if k not in early] + list(early):
        for n in range(2):
            block = block_of(owner_ref, partner(codes, k, n == 1))
            source = slabs[n][k].at[0] if n == 0 else slabs[n][k]
            if k in early:
                m = 2 * early.index(k) + n
                scaled = source[...].astype(jnp.float32) * grafts[m][0:1, 0:1]
                scaled_ref[m] = scaled.astype(scaled_ref.dtype)
                source = scaled_ref.at[m]
            copy = pltpu.make_async_copy(
                source, out_ref.at[jnp.maximum(block, 0)], sem.at[2 * k + n]
            )

            @pl.when(block >= 0)
            def _(copy=copy):
                copy.start()

            pending.append((block, copy))
    for block, copy in pending:

        @pl.when(block >= 0)
        def _(copy=copy):
            copy.wait()


def per_device_paired(gradients, block_owner, left_gram, right_gram, left_root, right_root):
    owners = lax.axis_size("shard")
    rounds = owners // 2
    codes = codes_of(owners)
    blocks, slab, width = gradients.shape[1:]
    half_rows = left_gram.shape[1]
    last = owners // 4 - 1
    early = []
    late = [k for k in range(rounds) if k not in early]
    slots = [[(k, other) for k in range(rounds)] for other in (False, True)]

    def other_core(x):
        return lax.ppermute(x, "replica", [(0, 1), (1, 0)])

    def trade(x, k):
        pairs = [(s * 2 + r, (s ^ codes[r][k]) * 2 + r) for s in range(owners) for r in range(2)]
        return lax.ppermute(x, ("shard", "replica"), pairs)

    def shape(dims, dtype=jnp.bfloat16):
        return jax.ShapeDtypeStruct(dims, dtype)

    def call(kernel, out_shape, in_specs, *args, cost_estimate=LIGHT, **options):
        return pl.pallas_call(
            kernel, out_shape=out_shape, in_specs=in_specs, compiler_params=PARAMS,
            cost_estimate=cost_estimate, **options
        )(*args)

    one = shape((8, 128), jnp.float32)
    other_gradient = other_core(gradients[0])
    fetched = call(
        functools.partial(fetch_kernel, codes), shape((rounds, slab, width)), [SMEM, VMEM],
        block_owner, gradients[0], out_specs=VMEM,
    )
    outgoing = call(
        functools.partial(pick_kernel, codes), [shape((slab, width))] * rounds,
        [SMEM, VMEM, VMEM], block_owner, fetched, other_gradient, out_specs=[VMEM] * rounds,
    )
    mine = [trade(outgoing[k], k) for k in range(rounds)]
    other_right = other_core(right_root[0])
    other_left = other_core(left_root[0])
    left_mine, left_theirs = call(
        functools.partial(order_kernel, codes, slots),
        [shape((half_rows, len(group) * slab)) for group in slots], [VMEM, VMEM],
        left_root[0], other_left, out_specs=[VMEM, VMEM],
        scratch_shapes=[pltpu.VMEM((half_rows, width), jnp.bfloat16)],
    )
    left_mine, left_theirs, *mine = lax.optimization_barrier((left_mine, left_theirs, *mine))
    theirs = [other_core(x) for x in mine]
    begun, begun_sq = call(
        begin_kernel, [shape((half_rows, width), jnp.float32), one],
        [VMEM] * (1 + rounds), left_mine, *mine, out_specs=[VMEM, VMEM],
        scratch_shapes=[pltpu.VMEM((half_rows, width), jnp.bfloat16)],
    )
    slab_shape = shape((2, slab, width // 2))
    both_sides, side_sq, grad_sq, *first = call(
        functools.partial(finish_kernel, early),
        [shape((2, half_rows, width // 2), jnp.float32), one, one] + [slab_shape] * len(early),
        [VMEM] * (5 + rounds), left_theirs, begun, begun_sq, right_root[0], other_right,
        *theirs, out_specs=[VMEM] * (3 + len(early)),
        scratch_shapes=[pltpu.VMEM((half_rows, width), jnp.bfloat16)] * 2,
    )
    returned = {k: trade(x, k) for k, x in zip(early, first)}
    graft, *rest = call(
        functools.partial(scale_kernel, late), [one] + [slab_shape] * len(late),
        [VMEM] * 4, side_sq, other_core(side_sq), grad_sq, both_sides,
        out_specs=[VMEM] * (1 + len(late)),
    )
    returned.update((k, trade(x, k)) for k, x in zip(late, rest))
    grafts = []
    for k in early:
        graft, returned[last + 1] = lax.optimization_barrier((graft, returned[last + 1]))
        came = trade(graft, k)
        grafts += [came, other_core(came)]

    left_new, right_new = call(
        functools.partial(gram_kernel, codes),
        [shape(left_gram.shape[1:]), shape(right_gram.shape[1:])],
        [SMEM, VMEM, VMEM, ANY] + [VMEM] * (2 * rounds),
        block_owner, left_gram[0], right_gram[0], returned[0],
        *mine, *theirs, out_specs=[VMEM, VMEM],
        scratch_shapes=[pltpu.VMEM((width, width), jnp.bfloat16)],
        cost_estimate=pl.CostEstimate(
            flops=4 * half_rows * width * width, bytes_accessed=8 * half_rows * width,
            transcendentals=0,
        ),
    )
    left_new, right_new, *rest = lax.optimization_barrier(
        (left_new, right_new, *[returned[k] for k in range(1, rounds)])
    )
    returned.update(enumerate(rest, 1))
    passed = [other_core(returned[k][1]) for k in range(rounds)]
    update = call(
        functools.partial(place_kernel, codes, early), shape((blocks, slab, width // 2)),
        [SMEM] + [VMEM] * (2 * rounds + len(grafts)), block_owner,
        *[returned[k] for k in range(rounds)], *passed, *grafts,
        out_specs=ANY,
        scratch_shapes=[
            pltpu.VMEM((max(1, 2 * len(early)), slab, width // 2), jnp.bfloat16),
            pltpu.SemaphoreType.DMA((2 * rounds,)),
        ],
    )
    return (left_new[None], right_new[None], update)


def solution(mesh):
    owners = mesh.shape["shard"]
    paired = mesh.shape["replica"] == 2 and owners in (4, 8, 16)
    return jax.shard_map(
        per_device_paired if paired else per_device,
        mesh=mesh,
        in_specs=(
            P("replica", "groups", "shard", None),
            P("groups"),
            P(("groups", "shard"), "replica", None),
            P(("groups", "shard"), "replica", None),
            P(("groups", "shard"), "replica", None),
            P(("groups", "shard"), None, "replica"),
        ),
        out_specs=(
            P(("groups", "shard"), "replica", None),
            P(("groups", "shard"), "replica", None),
            P("groups", "shard", "replica"),
        ),
        check_vma=False,
    )
```

```python
import functools

import jax
import jax.numpy as jnp
from jax import lax
from jax.experimental import pallas as pl
from jax.experimental.pallas import tpu as pltpu
from jax.sharding import PartitionSpec as P

VMEM = pl.BlockSpec(memory_space=pltpu.VMEM)
SMEM = pl.BlockSpec(memory_space=pltpu.SMEM)
ANY = pl.BlockSpec(memory_space=pl.ANY)
LIGHT = pl.CostEstimate(flops=0, bytes_accessed=0, transcendentals=0)
ORDER = {2: (1, 0), 4: (2, 1, 0, 3)}
PARAMS = pltpu.CompilerParams(vmem_limit_bytes=24 * 1024 * 1024)


def per_device(gradients, block_owner, left_gram, right_gram, left_root, right_root):
    owners = lax.axis_size("shard")
    half_rows = left_gram.shape[1]
    full_width = left_gram.shape[2]
    first_row = lax.axis_index("replica") * half_rows
    owner_index = lax.broadcasted_iota(jnp.int32, (owners, block_owner.shape[0]), 0)
    owner_onehot = (owner_index == block_owner[None, :]).astype(jnp.bfloat16)
    outgoing = jnp.einsum(
        "ob,brc->orc", owner_onehot, gradients[0], preferred_element_type=jnp.float32
    )
    arrived = lax.all_to_all(
        outgoing.astype(jnp.bfloat16), "shard", split_axis=0, concat_axis=0, tiled=True
    )
    total = lax.psum(arrived.astype(jnp.float32).astype(jnp.bfloat16), "replica")
    summed_block = total.reshape(full_width, full_width)
    own_rows = lax.dynamic_slice_in_dim(summed_block, first_row, half_rows, 0)
    own_cols = lax.dynamic_slice_in_dim(summed_block, first_row, half_rows, 1)
    left_term = lax.dot_general(
        own_rows, summed_block, (((1,), (1,)), ((), ())), preferred_element_type=jnp.float32
    )
    right_term = lax.dot_general(
        own_cols, summed_block, (((0,), (0,)), ((), ())), preferred_element_type=jnp.float32
    )
    left_new = (0.99 * left_gram[0].astype(jnp.float32) + 0.01 * left_term).astype(jnp.bfloat16)
    right_new = (0.99 * right_gram[0].astype(jnp.float32) + 0.01 * right_term).astype(jnp.bfloat16)
    partial_side = jnp.dot(left_root[0], summed_block, preferred_element_type=jnp.float32).astype(
        jnp.bfloat16
    )
    left_side = lax.all_gather(partial_side, "replica", axis=0, tiled=True)
    both_sides = jnp.dot(left_side, right_root[0], preferred_element_type=jnp.float32)
    side_squares = lax.psum(jnp.sum(both_sides * both_sides), "replica")
    grad_squares = jnp.sum(jnp.square(summed_block.astype(jnp.float32)))
    graft = jnp.sqrt(grad_squares / (side_squares + 1e-06))
    scaled = (
        (both_sides * graft).astype(jnp.bfloat16).reshape(owners, full_width // owners, half_rows)
    )
    returned = lax.all_to_all(scaled, "shard", split_axis=0, concat_axis=0, tiled=True)
    update = jnp.take(returned, block_owner, axis=0)
    return (left_new[None], right_new[None], update)


def codes_of(owners):
    near = ORDER[owners // 2]
    return near, tuple(owners // 2 + code for code in near)


def partner(codes, k, other=False):
    core = lax.axis_index("replica")
    first = core == (1 if other else 0)
    return lax.axis_index("shard") ^ jnp.where(first, codes[0][k], codes[1][k])


def block_of(owner_ref, owner):
    block = jnp.int32(-1)
    for b in range(owner_ref.shape[0]):
        block = jnp.where(owner_ref[b] == owner, b, block)
    return block


def sent_block(codes, owner_ref, k):
    return jnp.maximum(block_of(owner_ref, partner(codes, k)), 0)


def squares(value):
    wide = value.astype(jnp.float32)
    return jnp.sum(jnp.sum(wide * wide, axis=0, keepdims=True), axis=1, keepdims=True)


def fetch_kernel(codes, owner_ref, gradient_ref, out_ref):
    for k in range(out_ref.shape[0]):
        out_ref[k] = gradient_ref[sent_block(codes, owner_ref, k)]


def pick_kernel(codes, owner_ref, mine_ref, theirs_ref, *out_refs):
    for k, out_ref in enumerate(out_refs):
        other = theirs_ref[sent_block(codes, owner_ref, k)]
        total = mine_ref[k].astype(jnp.float32) + other.astype(jnp.float32)
        out_ref[...] = total.astype(out_ref.dtype)


def order_kernel(codes, slots, own_ref, other_ref, *refs):
    out_refs, rows_ref = refs[:-1], refs[-1]
    half, full = own_ref.shape
    rounds = len(codes[0])
    slab = half // rounds
    core = lax.axis_index("replica")
    for n in range(2 * rounds):
        shard = partner(codes, n % rounds, n >= rounds)
        row = pl.multiple_of(lax.rem(shard, rounds) * slab, slab)
        for ref, near in ((own_ref, True), (other_ref, False)):

            @pl.when((lax.div(shard, rounds) == core) == near)
            def _(ref=ref):
                rows_ref[n * slab:(n + 1) * slab, :] = ref[pl.ds(row, slab), :]

    for out_ref, group in zip(out_refs, slots):
        column = lax.broadcasted_iota(jnp.int32, (1, len(group) * slab), 1)
        source = column
        for n, (k, other) in enumerate(group):
            inside = (column >= n * slab) & (column < (n + 1) * slab)
            shift = (partner(codes, k, other) - n) * slab
            source = jnp.where(inside, column + shift, source)
        row_index = lax.broadcasted_iota(jnp.int32, (full, len(group) * slab), 0)
        choose = (row_index == source).astype(jnp.float32).astype(rows_ref.dtype)
        out_ref[...] = jnp.dot(
            rows_ref[...], choose, preferred_element_type=jnp.float32
        ).astype(out_ref.dtype)


def begin_kernel(left_ref, *refs):
    *slabs, total_ref, grad_sq_ref, stacked_ref = refs
    slab = slabs[0].shape[0]
    for n, ref in enumerate(slabs):
        stacked_ref[n * slab:(n + 1) * slab, :] = ref[...]
    total_ref[...] = jnp.dot(
        left_ref[...], stacked_ref[...], preferred_element_type=jnp.float32
    )
    grad_sq_ref[...] = jnp.broadcast_to(squares(stacked_ref[...]), grad_sq_ref.shape)


def finish_kernel(left_ref, total_ref, begun_sq_ref, own_ref, other_ref, slab_ref, *refs):
    *whole_refs, keep_ref, pass_ref, side_ref, both_ref = refs
    last = slab_ref[...]
    side = total_ref[...] + jnp.dot(left_ref[...], last, preferred_element_type=jnp.float32)
    side_ref[...] = side.astype(side_ref.dtype)
    grad_sq = begun_sq_ref[0:1, 0:1] + squares(last)
    half, slab = own_ref.shape[1], slab_ref.shape[0]
    side_sq = jnp.zeros((1, 1), jnp.float32)
    for n, ref in enumerate((own_ref, other_ref)):
        both = jnp.dot(side_ref[...], ref[...], preferred_element_type=jnp.float32)
        both_ref[n] = both[:half]
        side_sq += squares(both)
    graft = jnp.sqrt(grad_sq / (side_sq + 1e-06))
    for k, out_ref in enumerate(whole_refs):
        out_ref[...] = (both_ref[:, k * slab:(k + 1) * slab] * graft).astype(out_ref.dtype)
    for n, out_ref in enumerate((keep_ref, pass_ref)):
        out_ref[...] = (both_ref[n, half - slab:] * graft).astype(out_ref.dtype)


def gram_kernel(codes, owner_ref, left_ref, right_ref, after_ref, *refs):
    rounds = len(codes[0])
    slabs, (left_out, right_out, summed_ref) = refs[:2 * rounds], refs[2 * rounds:]
    slab = slabs[0].shape[0]
    for k in range(rounds):
        for ref, other in ((slabs[k], False), (slabs[rounds + k], True)):
            row = pl.multiple_of(partner(codes, k, other) * slab, slab)
            summed_ref[pl.ds(row, slab), :] = ref[...]
    half = left_ref.shape[0]
    first = pl.multiple_of(lax.axis_index("replica") * half, 128)
    present = block_of(owner_ref, lax.axis_index("shard")) >= 0
    share = jnp.where(present, 0.01, 0.0).astype(jnp.float32)
    summed = summed_ref[...]
    left_term = lax.dot_general(
        summed_ref[pl.ds(first, half), :], summed, (((1,), (1,)), ((), ())),
        preferred_element_type=jnp.float32,
    )
    left_out[...] = (0.99 * left_ref[...].astype(jnp.float32) + share * left_term).astype(
        left_out.dtype
    )
    right_term = lax.dot_general(
        summed_ref[:, pl.ds(first, half)], summed, (((0,), (0,)), ((), ())),
        preferred_element_type=jnp.float32,
    )
    right_out[...] = (0.99 * right_ref[...].astype(jnp.float32) + share * right_term).astype(
        right_out.dtype
    )


def place_kernel(codes, owner_ref, *refs):
    rounds = len(codes[0])
    slabs, (out_ref, sem) = refs[:2 * rounds], refs[2 * rounds:]
    pending = []
    for k in range(rounds):
        for n in range(2):
            block = block_of(owner_ref, partner(codes, k, n == 1))
            source = slabs[n * rounds + k]
            if len(source.shape) == 3:
                source = source.at[0]
            copy = pltpu.make_async_copy(
                source, out_ref.at[jnp.maximum(block, 0)], sem.at[2 * k + n]
            )

            @pl.when(block >= 0)
            def _(copy=copy):
                copy.start()

            pending.append((block, copy))
    for block, copy in pending:

        @pl.when(block >= 0)
        def _(copy=copy):
            copy.wait()


def per_device_paired(gradients, block_owner, left_gram, right_gram, left_root, right_root):
    owners = lax.axis_size("shard")
    rounds = owners // 2
    last = rounds - 1
    codes = codes_of(owners)
    blocks, slab, width = gradients.shape[1:]
    half_rows = left_gram.shape[1]
    slots = [(k, other) for k in range(rounds) for other in (False, True)]
    slots = (slots[:-1], slots[-1:])

    def other_core(x):
        return lax.ppermute(x, "replica", [(0, 1), (1, 0)])

    def trade(x, k, turn=0):
        pairs = [
            (s * 2 + r, (s ^ codes[r][k]) * 2 + (r ^ turn)) for s in range(owners) for r in range(2)
        ]
        return lax.ppermute(x, ("shard", "replica"), pairs)

    def shape(dims, dtype=jnp.bfloat16):
        return jax.ShapeDtypeStruct(dims, dtype)

    def call(kernel, out_shape, in_specs, *args, cost_estimate=LIGHT, **options):
        return pl.pallas_call(
            kernel, out_shape=out_shape, in_specs=in_specs, compiler_params=PARAMS,
            cost_estimate=cost_estimate, **options
        )(*args)

    other_gradient = other_core(gradients[0])
    fetched = call(
        functools.partial(fetch_kernel, codes), shape((rounds, slab, width)), [SMEM, VMEM],
        block_owner, gradients[0], out_specs=VMEM,
    )
    outgoing = call(
        functools.partial(pick_kernel, codes), [shape((slab, width))] * rounds,
        [SMEM, VMEM, VMEM], block_owner, fetched, other_gradient, out_specs=[VMEM] * rounds,
    )
    mine = [trade(outgoing[k], k) for k in range(rounds)]
    other_left, other_right = other_core(left_root[0]), other_core(right_root[0])
    left_sooner, left_last = call(
        functools.partial(order_kernel, codes, slots),
        [shape((2 * half_rows, len(group) * slab)) for group in slots], [VMEM, VMEM],
        left_root[0], other_left, out_specs=[VMEM, VMEM],
        scratch_shapes=[pltpu.VMEM((2 * half_rows, width), jnp.bfloat16)],
    )
    mine[0], left_sooner, left_last = lax.optimization_barrier((mine[0], left_sooner, left_last))
    theirs = [other_core(x) for x in mine]
    sooner = [(theirs if other else mine)[k] for k, other in slots[0]]
    begun, begun_sq = call(
        begin_kernel,
        [shape((2 * half_rows, width), jnp.float32), shape((8, 128), jnp.float32)],
        [VMEM] * (1 + len(sooner)), left_sooner, *sooner, out_specs=[VMEM, VMEM],
        scratch_shapes=[pltpu.VMEM((len(sooner) * slab, width), jnp.bfloat16)],
    )
    *whole, keep, cross = call(
        finish_kernel,
        [shape((2, slab, width // 2))] * last + [shape((slab, width // 2))] * 2, [VMEM] * 6,
        left_last, begun, begun_sq, right_root[0], other_right, theirs[last],
        out_specs=[VMEM] * (last + 2),
        scratch_shapes=[
            pltpu.VMEM((2 * half_rows, width), jnp.bfloat16),
            pltpu.VMEM((2, half_rows, width // 2), jnp.float32),
        ],
    )
    returned = [trade(x, k) for k, x in enumerate(whole)] + [trade(keep, last)]
    crossed = trade(cross, last, turn=1)
    left_new, right_new = call(
        functools.partial(gram_kernel, codes),
        [shape(left_gram.shape[1:]), shape(right_gram.shape[1:])],
        [SMEM, VMEM, VMEM, ANY] + [VMEM] * (2 * rounds),
        block_owner, left_gram[0], right_gram[0], returned[0], *mine, *theirs,
        out_specs=[VMEM, VMEM],
        scratch_shapes=[pltpu.VMEM((width, width), jnp.bfloat16)],
        cost_estimate=pl.CostEstimate(
            flops=4 * half_rows * width * width, bytes_accessed=8 * half_rows * width,
            transcendentals=0,
        ),
    )
    left_new, right_new, *returned[1:last] = lax.optimization_barrier(
        (left_new, right_new, *returned[1:last])
    )
    passed = [other_core(x[1]) for x in returned[:last]] + [crossed]
    update = call(
        functools.partial(place_kernel, codes), shape((blocks, slab, width // 2)),
        [SMEM] + [ANY] * (2 * rounds), block_owner, *returned, *passed,
        out_specs=ANY, scratch_shapes=[pltpu.SemaphoreType.DMA((2 * rounds,))],
    )
    return (left_new[None], right_new[None], update)


def solution(mesh):
    owners = mesh.shape["shard"]
    paired = mesh.shape["replica"] == 2 and owners // 2 in ORDER
    return jax.shard_map(
        per_device_paired if paired else per_device,
        mesh=mesh,
        in_specs=(
            P("replica", "groups", "shard", None),
            P("groups"),
            P(("groups", "shard"), "replica", None),
            P(("groups", "shard"), "replica", None),
            P(("groups", "shard"), "replica", None),
            P(("groups", "shard"), None, "replica"),
        ),
        out_specs=(
            P(("groups", "shard"), "replica", None),
            P(("groups", "shard"), "replica", None),
            P("groups", "shard", "replica"),
        ),
        check_vma=False,
    )
```

```python
import functools

import jax
import jax.numpy as jnp
from jax import lax
from jax.experimental import pallas as pl
from jax.experimental.pallas import tpu as pltpu
from jax.sharding import PartitionSpec as P

VMEM = pl.BlockSpec(memory_space=pltpu.VMEM)
SMEM = pl.BlockSpec(memory_space=pltpu.SMEM)
ANY = pl.BlockSpec(memory_space=pl.ANY)
LIGHT = pl.CostEstimate(flops=0, bytes_accessed=0, transcendentals=0)
ORDER = {2: (1, 0), 4: (2, 1, 0, 3)}
PARAMS = pltpu.CompilerParams(vmem_limit_bytes=24 * 1024 * 1024)


def per_device(gradients, block_owner, left_gram, right_gram, left_root, right_root):
    owners = lax.axis_size("shard")
    half_rows = left_gram.shape[1]
    full_width = left_gram.shape[2]
    first_row = lax.axis_index("replica") * half_rows
    owner_index = lax.broadcasted_iota(jnp.int32, (owners, block_owner.shape[0]), 0)
    owner_onehot = (owner_index == block_owner[None, :]).astype(jnp.bfloat16)
    outgoing = jnp.einsum(
        "ob,brc->orc", owner_onehot, gradients[0], preferred_element_type=jnp.float32
    )
    arrived = lax.all_to_all(
        outgoing.astype(jnp.bfloat16), "shard", split_axis=0, concat_axis=0, tiled=True
    )
    total = lax.psum(arrived.astype(jnp.float32).astype(jnp.bfloat16), "replica")
    summed_block = total.reshape(full_width, full_width)
    own_rows = lax.dynamic_slice_in_dim(summed_block, first_row, half_rows, 0)
    own_cols = lax.dynamic_slice_in_dim(summed_block, first_row, half_rows, 1)
    left_term = lax.dot_general(
        own_rows, summed_block, (((1,), (1,)), ((), ())), preferred_element_type=jnp.float32
    )
    right_term = lax.dot_general(
        own_cols, summed_block, (((0,), (0,)), ((), ())), preferred_element_type=jnp.float32
    )
    left_new = (0.99 * left_gram[0].astype(jnp.float32) + 0.01 * left_term).astype(jnp.bfloat16)
    right_new = (0.99 * right_gram[0].astype(jnp.float32) + 0.01 * right_term).astype(jnp.bfloat16)
    partial_side = jnp.dot(left_root[0], summed_block, preferred_element_type=jnp.float32).astype(
        jnp.bfloat16
    )
    left_side = lax.all_gather(partial_side, "replica", axis=0, tiled=True)
    both_sides = jnp.dot(left_side, right_root[0], preferred_element_type=jnp.float32)
    side_squares = lax.psum(jnp.sum(both_sides * both_sides), "replica")
    grad_squares = jnp.sum(jnp.square(summed_block.astype(jnp.float32)))
    graft = jnp.sqrt(grad_squares / (side_squares + 1e-06))
    scaled = (
        (both_sides * graft).astype(jnp.bfloat16).reshape(owners, full_width // owners, half_rows)
    )
    returned = lax.all_to_all(scaled, "shard", split_axis=0, concat_axis=0, tiled=True)
    update = jnp.take(returned, block_owner, axis=0)
    return (left_new[None], right_new[None], update)


def codes_of(owners):
    near = ORDER[owners // 2]
    return near, tuple(owners // 2 + code for code in near)


def partner(codes, k, other=False):
    core = lax.axis_index("replica")
    first = core == (1 if other else 0)
    return lax.axis_index("shard") ^ jnp.where(first, codes[0][k], codes[1][k])


def block_of(owner_ref, owner):
    block = jnp.int32(-1)
    for b in range(owner_ref.shape[0]):
        block = jnp.where(owner_ref[b] == owner, b, block)
    return block


def sent_block(codes, owner_ref, k):
    return jnp.maximum(block_of(owner_ref, partner(codes, k)), 0)


def squares(value):
    wide = value.astype(jnp.float32)
    return jnp.sum(jnp.sum(wide * wide, axis=0, keepdims=True), axis=1, keepdims=True)


def fetch_kernel(gradient_ref, out_ref):
    out_ref[...] = gradient_ref[...]


def pick_kernel(codes, owner_ref, mine_ref, theirs_ref, *out_refs):
    for k, out_ref in enumerate(out_refs):
        b = sent_block(codes, owner_ref, k)
        total = mine_ref[b].astype(jnp.float32) + theirs_ref[b].astype(jnp.float32)
        out_ref[...] = total.astype(out_ref.dtype)


def order_kernel(codes, slots, own_ref, other_ref, *refs):
    out_refs, rows_ref = refs[:-1], refs[-1]
    half, full = own_ref.shape
    rounds = len(codes[0])
    slab = half // rounds
    core = lax.axis_index("replica")
    for n in range(2 * rounds):
        shard = partner(codes, n % rounds, n >= rounds)
        row = pl.multiple_of(lax.rem(shard, rounds) * slab, slab)
        for ref, near in ((own_ref, True), (other_ref, False)):

            @pl.when((lax.div(shard, rounds) == core) == near)
            def _(ref=ref):
                rows_ref[n * slab:(n + 1) * slab, :] = ref[pl.ds(row, slab), :]

    for out_ref, group in zip(out_refs, slots):
        column = lax.broadcasted_iota(jnp.int32, (1, len(group) * slab), 1)
        source = column
        for n, (k, other) in enumerate(group):
            inside = (column >= n * slab) & (column < (n + 1) * slab)
            shift = (partner(codes, k, other) - n) * slab
            source = jnp.where(inside, column + shift, source)
        row_index = lax.broadcasted_iota(jnp.int32, (full, len(group) * slab), 0)
        choose = (row_index == source).astype(jnp.float32).astype(rows_ref.dtype)
        out_ref[...] = jnp.dot(
            rows_ref[...], choose, preferred_element_type=jnp.float32
        ).astype(out_ref.dtype)


def begin_kernel(left_ref, *refs):
    *slabs, total_ref, grad_sq_ref, stacked_ref = refs
    slab = slabs[0].shape[0]
    for n, ref in enumerate(slabs):
        stacked_ref[n * slab:(n + 1) * slab, :] = ref[...]
    total_ref[...] = jnp.dot(
        left_ref[...], stacked_ref[...], preferred_element_type=jnp.float32
    )
    grad_sq_ref[...] = jnp.broadcast_to(squares(stacked_ref[...]), grad_sq_ref.shape)


def finish_kernel(count, left_ref, total_ref, begun_sq_ref, own_ref, other_ref, *refs):
    slabs = refs[:count]
    *whole_refs, keep_ref, pass_ref, stacked_ref, side_ref, both_ref = refs[count:]
    slab = slabs[0].shape[0]
    for n, ref in enumerate(slabs):
        stacked_ref[n * slab:(n + 1) * slab, :] = ref[...]
    last = stacked_ref[...]
    side = total_ref[...] + jnp.dot(left_ref[...], last, preferred_element_type=jnp.float32)
    side_ref[...] = side.astype(side_ref.dtype)
    grad_sq = begun_sq_ref[0:1, 0:1] + squares(last)
    half = own_ref.shape[1]
    side_sq = jnp.zeros((1, 1), jnp.float32)
    for n, ref in enumerate((own_ref, other_ref)):
        both = jnp.dot(side_ref[...], ref[...], preferred_element_type=jnp.float32)
        both_ref[n] = both[:half]
        side_sq += squares(both)
    graft = jnp.sqrt(grad_sq / (side_sq + 1e-06))
    for k, out_ref in enumerate(whole_refs):
        out_ref[...] = (both_ref[:, k * slab:(k + 1) * slab] * graft).astype(out_ref.dtype)
    for n, out_ref in enumerate((keep_ref, pass_ref)):
        out_ref[...] = (both_ref[n, half - slab:] * graft).astype(out_ref.dtype)


def gram_kernel(codes, owner_ref, left_ref, right_ref, after_ref, *refs):
    rounds = len(codes[0])
    slabs, (left_out, right_out, summed_ref) = refs[:2 * rounds], refs[2 * rounds:]
    slab = slabs[0].shape[0]
    for k in range(rounds):
        for ref, other in ((slabs[k], False), (slabs[rounds + k], True)):
            row = pl.multiple_of(partner(codes, k, other) * slab, slab)
            summed_ref[pl.ds(row, slab), :] = ref[...]
    half = left_ref.shape[0]
    first = pl.multiple_of(lax.axis_index("replica") * half, 128)
    present = block_of(owner_ref, lax.axis_index("shard")) >= 0
    share = jnp.where(present, 0.01, 0.0).astype(jnp.float32)
    summed = summed_ref[...]
    left_term = lax.dot_general(
        summed_ref[pl.ds(first, half), :], summed, (((1,), (1,)), ((), ())),
        preferred_element_type=jnp.float32,
    )
    left_out[...] = (0.99 * left_ref[...].astype(jnp.float32) + share * left_term).astype(
        left_out.dtype
    )
    right_term = lax.dot_general(
        summed_ref[:, pl.ds(first, half)], summed, (((0,), (0,)), ((), ())),
        preferred_element_type=jnp.float32,
    )
    right_out[...] = (0.99 * right_ref[...].astype(jnp.float32) + share * right_term).astype(
        right_out.dtype
    )


def place_kernel(codes, owner_ref, *refs):
    rounds = len(codes[0])
    slabs, (out_ref, sem) = refs[:2 * rounds], refs[2 * rounds:]
    pending = []
    for k in range(rounds):
        for n in range(2):
            block = block_of(owner_ref, partner(codes, k, n == 1))
            source = slabs[n * rounds + k]
            if len(source.shape) == 3:
                source = source.at[0]
            copy = pltpu.make_async_copy(
                source, out_ref.at[jnp.maximum(block, 0)], sem.at[2 * k + n]
            )

            @pl.when(block >= 0)
            def _(copy=copy):
                copy.start()

            pending.append((block, copy))
    for block, copy in pending:

        @pl.when(block >= 0)
        def _(copy=copy):
            copy.wait()


def per_device_paired(gradients, block_owner, left_gram, right_gram, left_root, right_root):
    owners = lax.axis_size("shard")
    rounds = owners // 2
    last = rounds - 1
    codes = codes_of(owners)
    blocks, slab, width = gradients.shape[1:]
    half_rows = left_gram.shape[1]
    slots = [(k, other) for k in range(rounds) for other in (False, True)]
    after = [(k, True) for k in range(max(last - 1, 0), rounds)]
    slots = ([x for x in slots if x not in after], after)

    def other_core(x):
        return lax.ppermute(x, "replica", [(0, 1), (1, 0)])

    def trade(x, k, turn=0):
        pairs = [
            (s * 2 + r, (s ^ codes[r][k]) * 2 + (r ^ turn)) for s in range(owners) for r in range(2)
        ]
        return lax.ppermute(x, ("shard", "replica"), pairs)

    def shape(dims, dtype=jnp.bfloat16):
        return jax.ShapeDtypeStruct(dims, dtype)

    def call(kernel, out_shape, in_specs, *args, params=PARAMS, cost_estimate=LIGHT, **options):
        return pl.pallas_call(
            kernel, out_shape=out_shape, in_specs=in_specs, compiler_params=params,
            cost_estimate=cost_estimate, **options
        )(*args)

    other_gradient = other_core(gradients[0])
    block_owner = other_core(block_owner)
    fetched = call(
        fetch_kernel, shape((blocks, slab, width)), [VMEM], gradients[0], out_specs=VMEM
    )
    *outgoing, = call(
        functools.partial(pick_kernel, codes), [shape((slab, width))] * rounds,
        [SMEM, VMEM, VMEM], block_owner, fetched, other_gradient, out_specs=[VMEM] * rounds,
    )
    mine = [trade(outgoing[k], k) for k in range(rounds)]
    other_left, other_right = other_core(left_root[0]), other_core(right_root[0])
    left_sooner, left_last = call(
        functools.partial(order_kernel, codes, slots),
        [shape((2 * half_rows, len(group) * slab)) for group in slots], [VMEM, VMEM],
        left_root[0], other_left, out_specs=[VMEM, VMEM],
        scratch_shapes=[pltpu.VMEM((2 * half_rows, width), jnp.bfloat16)],
    )
    mine[0], left_sooner, left_last = lax.optimization_barrier((mine[0], left_sooner, left_last))
    theirs = [other_core(x) for x in mine]
    sooner = [(theirs if other else mine)[k] for k, other in slots[0]]
    begun, begun_sq = call(
        begin_kernel,
        [shape((2 * half_rows, width), jnp.float32), shape((8, 128), jnp.float32)],
        [VMEM] * (1 + len(sooner)), left_sooner, *sooner, out_specs=[VMEM, VMEM],
        scratch_shapes=[pltpu.VMEM((len(sooner) * slab, width), jnp.bfloat16)],
    )
    *whole, keep, cross = call(
        functools.partial(finish_kernel, len(after)),
        [shape((2, slab, width // 2))] * last + [shape((slab, width // 2))] * 2,
        [VMEM] * (5 + len(after)),
        left_last, begun, begun_sq, right_root[0], other_right, *[theirs[k] for k, _ in after],
        out_specs=[VMEM] * (last + 2),
        scratch_shapes=[
            pltpu.VMEM((len(after) * slab, width), jnp.bfloat16),
            pltpu.VMEM((2 * half_rows, width), jnp.bfloat16),
            pltpu.VMEM((2, half_rows, width // 2), jnp.float32),
        ],
    )
    returned = [trade(x, k) for k, x in enumerate(whole)] + [trade(keep, last)]
    crossed = trade(cross, last, turn=1)
    left_new, right_new = call(
        functools.partial(gram_kernel, codes),
        [shape(left_gram.shape[1:]), shape(right_gram.shape[1:])],
        [SMEM, VMEM, VMEM, ANY] + [VMEM] * (2 * rounds),
        block_owner, left_gram[0], right_gram[0], returned[0], *mine, *theirs,
        out_specs=[VMEM, VMEM],
        scratch_shapes=[pltpu.VMEM((width, width), jnp.bfloat16)],
        cost_estimate=pl.CostEstimate(
            flops=4 * half_rows * width * width, bytes_accessed=8 * half_rows * width,
            transcendentals=0,
        ),
    )
    left_new, right_new, returned[1] = lax.optimization_barrier((left_new, right_new, returned[1]))
    passed = [other_core(x[1]) for x in returned[:last]] + [crossed]
    update = call(
        functools.partial(place_kernel, codes), shape((blocks, slab, width // 2)),
        [SMEM] + [ANY] * (2 * rounds), block_owner, *returned, *passed,
        out_specs=ANY, scratch_shapes=[pltpu.SemaphoreType.DMA((2 * rounds,))],
    )
    return (left_new[None], right_new[None], update)


def solution(mesh):
    owners = mesh.shape["shard"]
    paired = mesh.shape["replica"] == 2 and owners // 2 in ORDER
    return jax.shard_map(
        per_device_paired if paired else per_device,
        mesh=mesh,
        in_specs=(
            P("replica", "groups", "shard", None),
            P("groups"),
            P(("groups", "shard"), "replica", None),
            P(("groups", "shard"), "replica", None),
            P(("groups", "shard"), "replica", None),
            P(("groups", "shard"), None, "replica"),
        ),
        out_specs=(
            P(("groups", "shard"), "replica", None),
            P(("groups", "shard"), "replica", None),
            P("groups", "shard", "replica"),
        ),
        check_vma=False,
    )
```

```python
import functools

import jax
import jax.numpy as jnp
from jax import lax
from jax.experimental import pallas as pl
from jax.experimental.pallas import tpu as pltpu
from jax.sharding import PartitionSpec as P

VMEM = pl.BlockSpec(memory_space=pltpu.VMEM)
SMEM = pl.BlockSpec(memory_space=pltpu.SMEM)
ANY = pl.BlockSpec(memory_space=pl.ANY)
LIGHT = pl.CostEstimate(flops=0, bytes_accessed=0, transcendentals=0)
ORDER = {2: (1, 0), 4: (2, 1, 0, 3)}
PARAMS = pltpu.CompilerParams(vmem_limit_bytes=24 * 1024 * 1024)


def per_device(gradients, block_owner, left_gram, right_gram, left_root, right_root):
    owners = lax.axis_size("shard")
    half_rows = left_gram.shape[1]
    full_width = left_gram.shape[2]
    first_row = lax.axis_index("replica") * half_rows
    owner_index = lax.broadcasted_iota(jnp.int32, (owners, block_owner.shape[0]), 0)
    owner_onehot = (owner_index == block_owner[None, :]).astype(jnp.bfloat16)
    outgoing = jnp.einsum(
        "ob,brc->orc", owner_onehot, gradients[0], preferred_element_type=jnp.float32
    )
    arrived = lax.all_to_all(
        outgoing.astype(jnp.bfloat16), "shard", split_axis=0, concat_axis=0, tiled=True
    )
    total = lax.psum(arrived.astype(jnp.float32).astype(jnp.bfloat16), "replica")
    summed_block = total.reshape(full_width, full_width)
    own_rows = lax.dynamic_slice_in_dim(summed_block, first_row, half_rows, 0)
    own_cols = lax.dynamic_slice_in_dim(summed_block, first_row, half_rows, 1)
    left_term = lax.dot_general(
        own_rows, summed_block, (((1,), (1,)), ((), ())), preferred_element_type=jnp.float32
    )
    right_term = lax.dot_general(
        own_cols, summed_block, (((0,), (0,)), ((), ())), preferred_element_type=jnp.float32
    )
    left_new = (0.99 * left_gram[0].astype(jnp.float32) + 0.01 * left_term).astype(jnp.bfloat16)
    right_new = (0.99 * right_gram[0].astype(jnp.float32) + 0.01 * right_term).astype(jnp.bfloat16)
    partial_side = jnp.dot(left_root[0], summed_block, preferred_element_type=jnp.float32).astype(
        jnp.bfloat16
    )
    left_side = lax.all_gather(partial_side, "replica", axis=0, tiled=True)
    both_sides = jnp.dot(left_side, right_root[0], preferred_element_type=jnp.float32)
    side_squares = lax.psum(jnp.sum(both_sides * both_sides), "replica")
    grad_squares = jnp.sum(jnp.square(summed_block.astype(jnp.float32)))
    graft = jnp.sqrt(grad_squares / (side_squares + 1e-06))
    scaled = (
        (both_sides * graft).astype(jnp.bfloat16).reshape(owners, full_width // owners, half_rows)
    )
    returned = lax.all_to_all(scaled, "shard", split_axis=0, concat_axis=0, tiled=True)
    update = jnp.take(returned, block_owner, axis=0)
    return (left_new[None], right_new[None], update)


def codes_of(owners):
    near = ORDER[owners // 2]
    return near, tuple(owners // 2 + code for code in near)


def partner(codes, k, other=False):
    core = lax.axis_index("replica")
    first = core == (1 if other else 0)
    return lax.axis_index("shard") ^ jnp.where(first, codes[0][k], codes[1][k])


def block_of(owner_ref, owner):
    block = jnp.int32(-1)
    for b in range(owner_ref.shape[0]):
        block = jnp.where(owner_ref[b] == owner, b, block)
    return block


def sent_block(codes, owner_ref, k):
    return jnp.maximum(block_of(owner_ref, partner(codes, k)), 0)


def squares(value):
    wide = value.astype(jnp.float32)
    return jnp.sum(jnp.sum(wide * wide, axis=0, keepdims=True), axis=1, keepdims=True)


def fetch_kernel(gradient_ref, after_ref, out_ref):
    out_ref[...] = gradient_ref[...]


def pick_kernel(codes, owner_ref, mine_ref, theirs_ref, *out_refs):
    for k, out_ref in enumerate(out_refs):
        b = sent_block(codes, owner_ref, k)
        total = mine_ref[b].astype(jnp.float32) + theirs_ref[b].astype(jnp.float32)
        out_ref[...] = total.astype(out_ref.dtype)


def order_kernel(codes, slots, own_ref, other_ref, *refs):
    out_refs, rows_ref = refs[:-1], refs[-1]
    half, full = own_ref.shape
    rounds = len(codes[0])
    slab = half // rounds
    core = lax.axis_index("replica")
    for n in range(2 * rounds):
        shard = partner(codes, n % rounds, n >= rounds)
        row = pl.multiple_of(lax.rem(shard, rounds) * slab, slab)
        for ref, near in ((own_ref, True), (other_ref, False)):

            @pl.when((lax.div(shard, rounds) == core) == near)
            def _(ref=ref):
                rows_ref[n * slab:(n + 1) * slab, :] = ref[pl.ds(row, slab), :]

    for out_ref, group in zip(out_refs, slots):
        column = lax.broadcasted_iota(jnp.int32, (1, len(group) * slab), 1)
        source = column
        for n, (k, other) in enumerate(group):
            inside = (column >= n * slab) & (column < (n + 1) * slab)
            shift = (partner(codes, k, other) - n) * slab
            source = jnp.where(inside, column + shift, source)
        row_index = lax.broadcasted_iota(jnp.int32, (full, len(group) * slab), 0)
        choose = (row_index == source).astype(jnp.float32).astype(rows_ref.dtype)
        out_ref[...] = jnp.dot(
            rows_ref[...], choose, preferred_element_type=jnp.float32
        ).astype(out_ref.dtype)


def begin_kernel(left_ref, *refs):
    *slabs, total_ref, grad_sq_ref, stacked_ref = refs
    slab = slabs[0].shape[0]
    for n, ref in enumerate(slabs):
        stacked_ref[n * slab:(n + 1) * slab, :] = ref[...]
    total_ref[...] = jnp.dot(
        left_ref[...], stacked_ref[...], preferred_element_type=jnp.float32
    )
    grad_sq_ref[...] = jnp.broadcast_to(squares(stacked_ref[...]), grad_sq_ref.shape)


def finish_kernel(count, left_ref, total_ref, begun_sq_ref, own_ref, other_ref, *refs):
    slabs = refs[:count]
    *whole_refs, keep_ref, pass_ref, stacked_ref, side_ref, both_ref = refs[count:]
    slab = slabs[0].shape[0]
    for n, ref in enumerate(slabs):
        stacked_ref[n * slab:(n + 1) * slab, :] = ref[...]
    last = stacked_ref[...]
    side = total_ref[...] + jnp.dot(left_ref[...], last, preferred_element_type=jnp.float32)
    side_ref[...] = side.astype(side_ref.dtype)
    grad_sq = begun_sq_ref[0:1, 0:1] + squares(last)
    half = own_ref.shape[1]
    side_sq = jnp.zeros((1, 1), jnp.float32)
    for n, ref in enumerate((own_ref, other_ref)):
        both = jnp.dot(side_ref[...], ref[...], preferred_element_type=jnp.float32)
        both_ref[n] = both[:half]
        side_sq += squares(both)
    graft = jnp.sqrt(grad_sq / (side_sq + 1e-06))
    for k, out_ref in enumerate(whole_refs):
        out_ref[...] = (both_ref[:, k * slab:(k + 1) * slab] * graft).astype(out_ref.dtype)
    for n, out_ref in enumerate((keep_ref, pass_ref)):
        out_ref[...] = (both_ref[n, half - slab:] * graft).astype(out_ref.dtype)


def gram_kernel(codes, owner_ref, left_ref, right_ref, after_ref, *refs):
    rounds = len(codes[0])
    slabs, (left_out, right_out, summed_ref) = refs[:2 * rounds], refs[2 * rounds:]
    slab = slabs[0].shape[0]
    for k in range(rounds):
        for ref, other in ((slabs[k], False), (slabs[rounds + k], True)):
            row = pl.multiple_of(partner(codes, k, other) * slab, slab)
            summed_ref[pl.ds(row, slab), :] = ref[...]
    half = left_ref.shape[0]
    first = pl.multiple_of(lax.axis_index("replica") * half, 128)
    present = block_of(owner_ref, lax.axis_index("shard")) >= 0
    share = jnp.where(present, 0.01, 0.0).astype(jnp.float32)
    summed = summed_ref[...]
    left_term = lax.dot_general(
        summed_ref[pl.ds(first, half), :], summed, (((1,), (1,)), ((), ())),
        preferred_element_type=jnp.float32,
    )
    left_out[...] = (0.99 * left_ref[...].astype(jnp.float32) + share * left_term).astype(
        left_out.dtype
    )
    right_term = lax.dot_general(
        summed_ref[:, pl.ds(first, half)], summed, (((0,), (0,)), ((), ())),
        preferred_element_type=jnp.float32,
    )
    right_out[...] = (0.99 * right_ref[...].astype(jnp.float32) + share * right_term).astype(
        right_out.dtype
    )


def place_kernel(codes, owner_ref, *refs):
    rounds = len(codes[0])
    slabs, (out_ref, sem) = refs[:2 * rounds], refs[2 * rounds:]
    pending = []
    for k in range(rounds):
        for n in range(2):
            block = block_of(owner_ref, partner(codes, k, n == 1))
            source = slabs[n * rounds + k]
            if len(source.shape) == 3:
                source = source.at[0]
            copy = pltpu.make_async_copy(
                source, out_ref.at[jnp.maximum(block, 0)], sem.at[2 * k + n]
            )

            @pl.when(block >= 0)
            def _(copy=copy):
                copy.start()

            pending.append((block, copy))
    for block, copy in pending:

        @pl.when(block >= 0)
        def _(copy=copy):
            copy.wait()


def per_device_paired(gradients, block_owner, left_gram, right_gram, left_root, right_root):
    owners = lax.axis_size("shard")
    rounds = owners // 2
    last = rounds - 1
    codes = codes_of(owners)
    blocks, slab, width = gradients.shape[1:]
    half_rows = left_gram.shape[1]
    slots = [(k, other) for k in range(rounds) for other in (False, True)]
    after = [(k, True) for k in reversed(range(max(last - 1, 0), rounds))]
    slots = ([x for x in slots if x not in after], after)

    def other_core(x):
        return lax.ppermute(x, "replica", [(0, 1), (1, 0)])

    def trade(x, k, turn=0):
        pairs = [
            (s * 2 + r, (s ^ codes[r][k]) * 2 + (r ^ turn)) for s in range(owners) for r in range(2)
        ]
        return lax.ppermute(x, ("shard", "replica"), pairs)

    def shape(dims, dtype=jnp.bfloat16):
        return jax.ShapeDtypeStruct(dims, dtype)

    def call(kernel, out_shape, in_specs, *args, params=PARAMS, cost_estimate=LIGHT, **options):
        return pl.pallas_call(
            kernel, out_shape=out_shape, in_specs=in_specs, compiler_params=params,
            cost_estimate=cost_estimate, **options
        )(*args)

    other_gradient = other_core(gradients[0])
    fetched = call(
        fetch_kernel, shape((blocks, slab, width)), [VMEM, ANY], gradients[0], block_owner,
        out_specs=VMEM,
    )
    *outgoing, = call(
        functools.partial(pick_kernel, codes), [shape((slab, width))] * rounds,
        [SMEM, VMEM, VMEM], block_owner, fetched, other_gradient, out_specs=[VMEM] * rounds,
    )
    mine = [trade(outgoing[k], k) for k in range(rounds)]
    other_left, other_right = other_core(left_root[0]), other_core(right_root[0])
    left_sooner, left_last = call(
        functools.partial(order_kernel, codes, slots),
        [shape((2 * half_rows, len(group) * slab)) for group in slots], [VMEM, VMEM],
        left_root[0], other_left, out_specs=[VMEM, VMEM],
        scratch_shapes=[pltpu.VMEM((2 * half_rows, width), jnp.bfloat16)],
    )
    mine[0], left_sooner, left_last = lax.optimization_barrier((mine[0], left_sooner, left_last))
    theirs = [other_core(x) for x in mine]
    sooner = [(theirs if other else mine)[k] for k, other in slots[0]]
    begun, begun_sq = call(
        begin_kernel,
        [shape((2 * half_rows, width), jnp.float32), shape((8, 128), jnp.float32)],
        [VMEM] * (1 + len(sooner)), left_sooner, *sooner, out_specs=[VMEM, VMEM],
        scratch_shapes=[pltpu.VMEM((len(sooner) * slab, width), jnp.bfloat16)],
    )
    *whole, keep, cross = call(
        functools.partial(finish_kernel, len(after)),
        [shape((2, slab, width // 2))] * last + [shape((slab, width // 2))] * 2,
        [VMEM] * (5 + len(after)),
        left_last, begun, begun_sq, right_root[0], other_right, *[theirs[k] for k, _ in after],
        out_specs=[VMEM] * (last + 2),
        scratch_shapes=[
            pltpu.VMEM((len(after) * slab, width), jnp.bfloat16),
            pltpu.VMEM((2 * half_rows, width), jnp.bfloat16),
            pltpu.VMEM((2, half_rows, width // 2), jnp.float32),
        ],
    )
    returned = [trade(x, k) for k, x in enumerate(whole)] + [trade(keep, last)]
    crossed = trade(cross, last, turn=1)
    left_new, right_new = call(
        functools.partial(gram_kernel, codes),
        [shape(left_gram.shape[1:]), shape(right_gram.shape[1:])],
        [SMEM, VMEM, VMEM, ANY] + [VMEM] * (2 * rounds),
        block_owner, left_gram[0], right_gram[0], returned[0], *mine, *theirs,
        out_specs=[VMEM, VMEM],
        scratch_shapes=[pltpu.VMEM((width, width), jnp.bfloat16)],
        cost_estimate=pl.CostEstimate(
            flops=4 * half_rows * width * width, bytes_accessed=8 * half_rows * width,
            transcendentals=0,
        ),
    )
    left_new, right_new, returned[1] = lax.optimization_barrier((left_new, right_new, returned[1]))
    passed = [other_core(x[1]) for x in returned[:last]] + [crossed]
    update = call(
        functools.partial(place_kernel, codes), shape((blocks, slab, width // 2)),
        [SMEM] + [ANY] * (2 * rounds), block_owner, *returned, *passed,
        out_specs=ANY, scratch_shapes=[pltpu.SemaphoreType.DMA((2 * rounds,))],
    )
    return (left_new[None], right_new[None], update)


def solution(mesh):
    owners = mesh.shape["shard"]
    paired = mesh.shape["replica"] == 2 and owners // 2 in ORDER
    return jax.shard_map(
        per_device_paired if paired else per_device,
        mesh=mesh,
        in_specs=(
            P("replica", "groups", "shard", None),
            P("groups"),
            P(("groups", "shard"), "replica", None),
            P(("groups", "shard"), "replica", None),
            P(("groups", "shard"), "replica", None),
            P(("groups", "shard"), None, "replica"),
        ),
        out_specs=(
            P(("groups", "shard"), "replica", None),
            P(("groups", "shard"), "replica", None),
            P("groups", "shard", "replica"),
        ),
        check_vma=False,
    )
```

```python
import functools

import jax
import jax.numpy as jnp
from jax import lax
from jax.experimental import pallas as pl
from jax.experimental.pallas import tpu as pltpu
from jax.sharding import PartitionSpec as P

VMEM = pl.BlockSpec(memory_space=pltpu.VMEM)
ANY = pl.BlockSpec(memory_space=pl.ANY)
LIGHT = pl.CostEstimate(flops=0, bytes_accessed=0, transcendentals=0)
ORDER = {2: (1, 0), 4: (2, 1, 0, 3)}
PARAMS = pltpu.CompilerParams(vmem_limit_bytes=24 * 1024 * 1024)


def per_device(gradients, block_owner, left_gram, right_gram, left_root, right_root):
    owners = lax.axis_size("shard")
    half_rows = left_gram.shape[1]
    full_width = left_gram.shape[2]
    first_row = lax.axis_index("replica") * half_rows
    owner_index = lax.broadcasted_iota(jnp.int32, (owners, block_owner.shape[0]), 0)
    owner_onehot = (owner_index == block_owner[None, :]).astype(jnp.bfloat16)
    outgoing = jnp.einsum(
        "ob,brc->orc", owner_onehot, gradients[0], preferred_element_type=jnp.float32
    )
    arrived = lax.all_to_all(
        outgoing.astype(jnp.bfloat16), "shard", split_axis=0, concat_axis=0, tiled=True
    )
    total = lax.psum(arrived.astype(jnp.float32).astype(jnp.bfloat16), "replica")
    summed_block = total.reshape(full_width, full_width)
    own_rows = lax.dynamic_slice_in_dim(summed_block, first_row, half_rows, 0)
    own_cols = lax.dynamic_slice_in_dim(summed_block, first_row, half_rows, 1)
    left_term = lax.dot_general(
        own_rows, summed_block, (((1,), (1,)), ((), ())), preferred_element_type=jnp.float32
    )
    right_term = lax.dot_general(
        own_cols, summed_block, (((0,), (0,)), ((), ())), preferred_element_type=jnp.float32
    )
    left_new = (0.99 * left_gram[0].astype(jnp.float32) + 0.01 * left_term).astype(jnp.bfloat16)
    right_new = (0.99 * right_gram[0].astype(jnp.float32) + 0.01 * right_term).astype(jnp.bfloat16)
    partial_side = jnp.dot(left_root[0], summed_block, preferred_element_type=jnp.float32).astype(
        jnp.bfloat16
    )
    left_side = lax.all_gather(partial_side, "replica", axis=0, tiled=True)
    both_sides = jnp.dot(left_side, right_root[0], preferred_element_type=jnp.float32)
    side_squares = lax.psum(jnp.sum(both_sides * both_sides), "replica")
    grad_squares = jnp.sum(jnp.square(summed_block.astype(jnp.float32)))
    graft = jnp.sqrt(grad_squares / (side_squares + 1e-06))
    scaled = (
        (both_sides * graft).astype(jnp.bfloat16).reshape(owners, full_width // owners, half_rows)
    )
    returned = lax.all_to_all(scaled, "shard", split_axis=0, concat_axis=0, tiled=True)
    update = jnp.take(returned, block_owner, axis=0)
    return (left_new[None], right_new[None], update)


def codes_of(owners):
    near = ORDER[owners // 2]
    return near, tuple(owners // 2 + code for code in near)


def partner(codes, k, other=False):
    core = lax.axis_index("replica")
    first = core == (1 if other else 0)
    return lax.axis_index("shard") ^ jnp.where(first, codes[0][k], codes[1][k])


def block_of(owner_ref, owner):
    block = jnp.int32(-1)
    for b in range(owner_ref.shape[1]):
        block = jnp.where(owner_ref[0, b] == owner, b, block)
    return block


def sent_block(codes, owner_ref, k):
    return jnp.maximum(block_of(owner_ref, partner(codes, k)), 0)


def squares(value):
    wide = value.astype(jnp.float32)
    rows = jnp.sum((wide * wide).reshape(-1, 8, wide.shape[1]), axis=0)
    return jnp.sum(jnp.sum(rows, axis=0, keepdims=True), axis=1, keepdims=True)


def fetch_kernel(gradient_ref, after_ref, out_ref):
    out_ref[...] = gradient_ref[...]


def pick_kernel(codes, owner_ref, mine_ref, theirs_ref, *out_refs):
    for k, out_ref in enumerate(out_refs):
        b = sent_block(codes, owner_ref, k)
        total = mine_ref[b].astype(jnp.float32) + theirs_ref[b].astype(jnp.float32)
        out_ref[...] = total.astype(out_ref.dtype)


def order_kernel(codes, slots, own_ref, other_ref, own_right_ref, other_right_ref, *refs):
    *out_refs, right_ref, rows_ref = refs
    right_ref[:, :own_right_ref.shape[1]] = own_right_ref[...]
    right_ref[:, own_right_ref.shape[1]:] = other_right_ref[...]
    half, full = own_ref.shape
    rounds = len(codes[0])
    slab = half // rounds
    core = lax.axis_index("replica")
    for n in range(2 * rounds):
        shard = partner(codes, n % rounds, n >= rounds)
        row = pl.multiple_of(lax.rem(shard, rounds) * slab, slab)
        for ref, near in ((own_ref, True), (other_ref, False)):

            @pl.when((lax.div(shard, rounds) == core) == near)
            def _(ref=ref):
                rows_ref[n * slab:(n + 1) * slab, :] = ref[pl.ds(row, slab), :]

    for out_ref, group in zip(out_refs, slots):
        column = lax.broadcasted_iota(jnp.int32, (1, len(group) * slab), 1)
        source = column
        for n, (k, other) in enumerate(group):
            inside = (column >= n * slab) & (column < (n + 1) * slab)
            shift = (partner(codes, k, other) - n) * slab
            source = jnp.where(inside, column + shift, source)
        row_index = lax.broadcasted_iota(jnp.int32, (full, len(group) * slab), 0)
        choose = (row_index == source).astype(jnp.float32).astype(rows_ref.dtype)
        out_ref[...] = jnp.dot(
            rows_ref[...], choose, preferred_element_type=jnp.float32
        ).astype(out_ref.dtype)


def begin_kernel(left_ref, *refs):
    *slabs, total_ref, grad_sq_ref, stacked_ref = refs
    slab = slabs[0].shape[0]
    for n, ref in enumerate(slabs):
        stacked_ref[n * slab:(n + 1) * slab, :] = ref[...]
    total_ref[...] = jnp.dot(
        left_ref[...], stacked_ref[...], preferred_element_type=jnp.float32
    )
    grad_sq_ref[...] = jnp.broadcast_to(squares(stacked_ref[...]), grad_sq_ref.shape)


def finish_kernel(count, left_ref, total_ref, begun_sq_ref, right_ref, *refs):
    slabs = refs[:count]
    *whole_refs, keep_ref, pass_ref, stacked_ref, side_ref, both_ref = refs[count:]
    slab = slabs[0].shape[0]
    half, full = both_ref.shape
    for n, ref in enumerate(slabs):
        stacked_ref[n * slab:(n + 1) * slab, :] = ref[...]
    last = stacked_ref[...]
    side = total_ref[...] + jnp.dot(left_ref[...], last, preferred_element_type=jnp.float32)
    side_ref[...] = side.astype(side_ref.dtype)
    grad_sq = begun_sq_ref[0:1, 0:1] + squares(last)
    both = jnp.dot(side_ref[...], right_ref[...], preferred_element_type=jnp.float32)
    both_ref[...] = both[:half]
    graft = jnp.sqrt(grad_sq / (squares(both) + 1e-06))
    columns = (slice(None, full // 2), slice(full // 2, None))
    for k, out_ref in enumerate(whole_refs):
        for n in range(2):
            piece = both_ref[k * slab:(k + 1) * slab, columns[n]] * graft
            out_ref[n] = piece.astype(out_ref.dtype)
    for n, out_ref in enumerate((keep_ref, pass_ref)):
        out_ref[...] = (both_ref[half - slab:, columns[n]] * graft).astype(out_ref.dtype)


def gram_kernel(codes, owner_ref, left_ref, right_ref, after_ref, *refs):
    rounds = len(codes[0])
    slabs, (left_out, right_out, summed_ref) = refs[:2 * rounds], refs[2 * rounds:]
    slab = slabs[0].shape[0]
    for k in range(rounds):
        for ref, other in ((slabs[k], False), (slabs[rounds + k], True)):
            row = pl.multiple_of(partner(codes, k, other) * slab, slab)
            summed_ref[pl.ds(row, slab), :] = ref[...]
    half = left_ref.shape[0]
    first = pl.multiple_of(lax.axis_index("replica") * half, 128)
    present = block_of(owner_ref, lax.axis_index("shard")) >= 0
    share = jnp.where(present, 0.01, 0.0).astype(jnp.float32)
    summed = summed_ref[...]
    left_term = lax.dot_general(
        summed_ref[pl.ds(first, half), :], summed, (((1,), (1,)), ((), ())),
        preferred_element_type=jnp.float32,
    )
    left_out[...] = (0.99 * left_ref[...].astype(jnp.float32) + share * left_term).astype(
        left_out.dtype
    )
    right_term = lax.dot_general(
        summed_ref[:, pl.ds(first, half)], summed, (((0,), (0,)), ((), ())),
        preferred_element_type=jnp.float32,
    )
    right_out[...] = (0.99 * right_ref[...].astype(jnp.float32) + share * right_term).astype(
        right_out.dtype
    )


def place_kernel(codes, owner_ref, *refs):
    rounds = len(codes[0])
    slabs, (out_ref, sem) = refs[:2 * rounds], refs[2 * rounds:]
    pending = []
    for k in range(rounds):
        for n in range(2):
            block = block_of(owner_ref, partner(codes, k, n == 1))
            source = slabs[n * rounds + k]
            if len(source.shape) == 3:
                source = source.at[0]
            copy = pltpu.make_async_copy(
                source, out_ref.at[jnp.maximum(block, 0)], sem.at[2 * k + n]
            )

            @pl.when(block >= 0)
            def _(copy=copy):
                copy.start()

            pending.append((block, copy))
    for block, copy in pending:

        @pl.when(block >= 0)
        def _(copy=copy):
            copy.wait()


def per_device_paired(gradients, block_owner, left_gram, right_gram, left_root, right_root):
    owners = lax.axis_size("shard")
    rounds = owners // 2
    last = rounds - 1
    codes = codes_of(owners)
    blocks, slab, width = gradients.shape[1:]
    half_rows = left_gram.shape[1]
    slots = [(k, other) for k in range(rounds) for other in (False, True)]
    after = [(k, True) for k in reversed(range(max(last - 1, 0), rounds))]
    slots = ([x for x in slots if x not in after], after)

    def other_core(x):
        return lax.ppermute(x, "replica", [(0, 1), (1, 0)])

    def trade(x, k, turn=0):
        pairs = [
            (s * 2 + r, (s ^ codes[r][k]) * 2 + (r ^ turn)) for s in range(owners) for r in range(2)
        ]
        return lax.ppermute(x, ("shard", "replica"), pairs)

    def shape(dims, dtype=jnp.bfloat16):
        return jax.ShapeDtypeStruct(dims, dtype)

    def call(kernel, out_shape, in_specs, *args, params=PARAMS, cost_estimate=LIGHT, **options):
        return pl.pallas_call(
            kernel, out_shape=out_shape, in_specs=in_specs, compiler_params=params,
            cost_estimate=cost_estimate, **options
        )(*args)

    block_owner = block_owner.reshape(1, blocks)
    other_gradient = other_core(gradients[0])
    fetched = call(
        fetch_kernel, shape((blocks, slab, width)), [VMEM, ANY], gradients[0], block_owner,
        out_specs=VMEM,
    )
    *outgoing, = call(
        functools.partial(pick_kernel, codes), [shape((slab, width))] * rounds,
        [VMEM, VMEM, VMEM], block_owner, fetched, other_gradient, out_specs=[VMEM] * rounds,
    )
    mine = [trade(outgoing[k], k) for k in range(rounds)]
    other_left, other_right = other_core(left_root[0]), other_core(right_root[0])
    left_sooner, left_last, right = call(
        functools.partial(order_kernel, codes, slots),
        [shape((2 * half_rows, len(group) * slab)) for group in slots] + [shape((width, width))],
        [VMEM] * 4, left_root[0], other_left, right_root[0], other_right, out_specs=[VMEM] * 3,
        scratch_shapes=[pltpu.VMEM((2 * half_rows, width), jnp.bfloat16)],
    )
    mine[0], left_sooner, left_last, right = lax.optimization_barrier(
        (mine[0], left_sooner, left_last, right)
    )
    theirs = [other_core(x) for x in mine]
    sooner = [(theirs if other else mine)[k] for k, other in slots[0]]
    begun, begun_sq = call(
        begin_kernel,
        [shape((2 * half_rows, width), jnp.float32), shape((8, 128), jnp.float32)],
        [VMEM] * (1 + len(sooner)), left_sooner, *sooner, out_specs=[VMEM, VMEM],
        scratch_shapes=[pltpu.VMEM((len(sooner) * slab, width), jnp.bfloat16)],
    )
    *whole, keep, cross = call(
        functools.partial(finish_kernel, len(after)),
        [shape((2, slab, width // 2))] * last + [shape((slab, width // 2))] * 2,
        [VMEM] * (4 + len(after)),
        left_last, begun, begun_sq, right, *[theirs[k] for k, _ in after],
        out_specs=[VMEM] * (last + 2),
        scratch_shapes=[
            pltpu.VMEM((len(after) * slab, width), jnp.bfloat16),
            pltpu.VMEM((2 * half_rows, width), jnp.bfloat16),
            pltpu.VMEM((half_rows, width), jnp.float32),
        ],
    )
    returned = [trade(x, k) for k, x in enumerate(whole)] + [trade(keep, last)]
    crossed = trade(cross, last, turn=1)
    left_new, right_new = call(
        functools.partial(gram_kernel, codes),
        [shape(left_gram.shape[1:]), shape(right_gram.shape[1:])],
        [VMEM, VMEM, VMEM, ANY] + [VMEM] * (2 * rounds),
        block_owner, left_gram[0], right_gram[0], returned[0], *mine, *theirs,
        out_specs=[VMEM, VMEM],
        scratch_shapes=[pltpu.VMEM((width, width), jnp.bfloat16)],
        cost_estimate=pl.CostEstimate(
            flops=4 * half_rows * width * width, bytes_accessed=8 * half_rows * width,
            transcendentals=0,
        ),
    )
    left_new, right_new, returned[1] = lax.optimization_barrier((left_new, right_new, returned[1]))
    passed = [other_core(x[1]) for x in returned[:last]] + [crossed]
    update = call(
        functools.partial(place_kernel, codes), shape((blocks, slab, width // 2)),
        [VMEM] + [ANY] * (2 * rounds), block_owner, *returned, *passed,
        out_specs=ANY, scratch_shapes=[pltpu.SemaphoreType.DMA((2 * rounds,))],
    )
    return (left_new[None], right_new[None], update)


def solution(mesh):
    owners = mesh.shape["shard"]
    paired = mesh.shape["replica"] == 2 and owners // 2 in ORDER
    return jax.shard_map(
        per_device_paired if paired else per_device,
        mesh=mesh,
        in_specs=(
            P("replica", "groups", "shard", None),
            P("groups"),
            P(("groups", "shard"), "replica", None),
            P(("groups", "shard"), "replica", None),
            P(("groups", "shard"), "replica", None),
            P(("groups", "shard"), None, "replica"),
        ),
        out_specs=(
            P(("groups", "shard"), "replica", None),
            P(("groups", "shard"), "replica", None),
            P("groups", "shard", "replica"),
        ),
        check_vma=False,
    )
```

```python
import functools

import jax
import jax.numpy as jnp
from jax import lax
from jax.experimental import pallas as pl
from jax.experimental.pallas import tpu as pltpu
from jax.sharding import PartitionSpec as P

VMEM = pl.BlockSpec(memory_space=pltpu.VMEM)
ANY = pl.BlockSpec(memory_space=pl.ANY)
LIGHT = pl.CostEstimate(flops=0, bytes_accessed=0, transcendentals=0)
OUT = ((2, 6), (1, 5), (0, 4), (3, 7))
BACK = ((2, 4), (3, 5), (1, 7))
SHARED, SELF = (6, 6), (0, 0)
PARAMS = pltpu.CompilerParams(vmem_limit_bytes=24 * 1024 * 1024)


def per_device(gradients, block_owner, left_gram, right_gram, left_root, right_root):
    owners = lax.axis_size("shard")
    half_rows = left_gram.shape[1]
    full_width = left_gram.shape[2]
    first_row = lax.axis_index("replica") * half_rows
    owner_index = lax.broadcasted_iota(jnp.int32, (owners, block_owner.shape[0]), 0)
    owner_onehot = (owner_index == block_owner[None, :]).astype(jnp.bfloat16)
    outgoing = jnp.einsum(
        "ob,brc->orc", owner_onehot, gradients[0], preferred_element_type=jnp.float32
    )
    arrived = lax.all_to_all(
        outgoing.astype(jnp.bfloat16), "shard", split_axis=0, concat_axis=0, tiled=True
    )
    total = lax.psum(arrived.astype(jnp.float32).astype(jnp.bfloat16), "replica")
    summed_block = total.reshape(full_width, full_width)
    own_rows = lax.dynamic_slice_in_dim(summed_block, first_row, half_rows, 0)
    own_cols = lax.dynamic_slice_in_dim(summed_block, first_row, half_rows, 1)
    left_term = lax.dot_general(
        own_rows, summed_block, (((1,), (1,)), ((), ())), preferred_element_type=jnp.float32
    )
    right_term = lax.dot_general(
        own_cols, summed_block, (((0,), (0,)), ((), ())), preferred_element_type=jnp.float32
    )
    left_new = (0.99 * left_gram[0].astype(jnp.float32) + 0.01 * left_term).astype(jnp.bfloat16)
    right_new = (0.99 * right_gram[0].astype(jnp.float32) + 0.01 * right_term).astype(jnp.bfloat16)
    partial_side = jnp.dot(left_root[0], summed_block, preferred_element_type=jnp.float32).astype(
        jnp.bfloat16
    )
    left_side = lax.all_gather(partial_side, "replica", axis=0, tiled=True)
    both_sides = jnp.dot(left_side, right_root[0], preferred_element_type=jnp.float32)
    side_squares = lax.psum(jnp.sum(both_sides * both_sides), "replica")
    grad_squares = jnp.sum(jnp.square(summed_block.astype(jnp.float32)))
    graft = jnp.sqrt(grad_squares / (side_squares + 1e-06))
    scaled = (
        (both_sides * graft).astype(jnp.bfloat16).reshape(owners, full_width // owners, half_rows)
    )
    returned = lax.all_to_all(scaled, "shard", split_axis=0, concat_axis=0, tiled=True)
    update = jnp.take(returned, block_owner, axis=0)
    return (left_new[None], right_new[None], update)


def turned(rounds):
    return tuple(codes[::-1] for codes in rounds)


def partner(codes):
    code = jnp.where(lax.axis_index("replica") == 0, codes[0], codes[1])
    return lax.axis_index("shard") ^ code


def block_of(owner_ref, owner):
    block = jnp.int32(-1)
    for b in range(owner_ref.shape[1]):
        block = jnp.where(owner_ref[0, b] == owner, b, block)
    return block


def squares(value):
    wide = value.astype(jnp.float32)
    rows = jnp.sum((wide * wide).reshape(-1, 8, wide.shape[1]), axis=0)
    return jnp.sum(jnp.sum(rows, axis=0, keepdims=True), axis=1, keepdims=True)


def fetch_kernel(gradient_ref, after_ref, out_ref):
    out_ref[...] = gradient_ref[...]


def pick_kernel(owner_ref, mine_ref, theirs_ref, *out_refs):
    for codes, out_ref in zip(OUT, out_refs):
        b = jnp.maximum(block_of(owner_ref, partner(codes)), 0)
        total = mine_ref[b].astype(jnp.float32) + theirs_ref[b].astype(jnp.float32)
        out_ref[...] = total.astype(out_ref.dtype)


def order_kernel(rows, columns, own_ref, other_ref, own_right_ref, other_right_ref, *refs):
    *out_refs, right_ref, rows_ref = refs
    right_ref[:, :own_right_ref.shape[1]] = own_right_ref[...]
    right_ref[:, own_right_ref.shape[1]:] = other_right_ref[...]
    half, full = own_ref.shape
    slab = full // len(rows)
    core = lax.axis_index("replica")
    for n, codes in enumerate(rows):
        start = partner(codes) * slab
        row = pl.multiple_of(lax.rem(start, half), slab)
        for ref, near in ((own_ref, True), (other_ref, False)):

            @pl.when((lax.div(start, half) == core) == near)
            def _(ref=ref):
                rows_ref[n * slab:(n + 1) * slab, :] = ref[pl.ds(row, slab), :]

    for out_ref, group in zip(out_refs, columns):
        column = lax.broadcasted_iota(jnp.int32, (1, len(group) * slab), 1)
        source = column
        for n, codes in enumerate(group):
            inside = (column >= n * slab) & (column < (n + 1) * slab)
            source = jnp.where(inside, column + (partner(codes) - n) * slab, source)
        row_index = lax.broadcasted_iota(jnp.int32, (full, len(group) * slab), 0)
        choose = (row_index == source).astype(jnp.float32).astype(rows_ref.dtype)
        out_ref[...] = jnp.dot(
            rows_ref[...], choose, preferred_element_type=jnp.float32
        ).astype(out_ref.dtype)


def begin_kernel(left_ref, *refs):
    *slabs, total_ref, grad_sq_ref, stacked_ref = refs
    slab = slabs[0].shape[0]
    for n, ref in enumerate(slabs):
        stacked_ref[n * slab:(n + 1) * slab, :] = ref[...]
    total_ref[...] = jnp.dot(
        left_ref[...], stacked_ref[...], preferred_element_type=jnp.float32
    )
    grad_sq_ref[...] = jnp.broadcast_to(squares(stacked_ref[...]), grad_sq_ref.shape)


def finish_kernel(count, left_ref, total_ref, begun_sq_ref, right_ref, *refs):
    slabs = refs[:count]
    *out_refs, stacked_ref, side_ref, both_ref = refs[count:]
    slab = slabs[0].shape[0]
    used, full = both_ref.shape
    for n, ref in enumerate(slabs):
        stacked_ref[n * slab:(n + 1) * slab, :] = ref[...]
    last = stacked_ref[...]
    side = total_ref[...] + jnp.dot(left_ref[...], last, preferred_element_type=jnp.float32)
    side_ref[...] = side.astype(side_ref.dtype)
    grad_sq = begun_sq_ref[0:1, 0:1] + squares(last)
    both = jnp.dot(side_ref[...], right_ref[...], preferred_element_type=jnp.float32)
    both_ref[...] = both[:used]
    graft = jnp.sqrt(grad_sq / (squares(both) + 1e-06))
    for k, out_ref in enumerate(out_refs):
        rows = slice(k * slab, (k + 1) * slab)
        if len(out_ref.shape) == 2:
            out_ref[...] = (both_ref[rows, :full // 2] * graft).astype(out_ref.dtype)
        else:
            out_ref[0] = (both_ref[rows, :full // 2] * graft).astype(out_ref.dtype)
            out_ref[1] = (both_ref[rows, full // 2:] * graft).astype(out_ref.dtype)


def gram_kernel(owner_ref, left_ref, right_ref, after_ref, *refs):
    *slabs, left_out, right_out, summed_ref = refs
    slab = slabs[0].shape[0]
    for codes, ref in zip(OUT + turned(OUT), slabs):
        row = pl.multiple_of(partner(codes) * slab, slab)
        summed_ref[pl.ds(row, slab), :] = ref[...]
    half = left_ref.shape[0]
    first = pl.multiple_of(lax.axis_index("replica") * half, 128)
    present = block_of(owner_ref, lax.axis_index("shard")) >= 0
    share = jnp.where(present, 0.01, 0.0).astype(jnp.float32)
    summed = summed_ref[...]
    left_term = lax.dot_general(
        summed_ref[pl.ds(first, half), :], summed, (((1,), (1,)), ((), ())),
        preferred_element_type=jnp.float32,
    )
    left_out[...] = (0.99 * left_ref[...].astype(jnp.float32) + share * left_term).astype(
        left_out.dtype
    )
    right_term = lax.dot_general(
        summed_ref[:, pl.ds(first, half)], summed, (((0,), (0,)), ((), ())),
        preferred_element_type=jnp.float32,
    )
    right_out[...] = (0.99 * right_ref[...].astype(jnp.float32) + share * right_term).astype(
        right_out.dtype
    )


def place_kernel(owner_ref, *refs):
    *slabs, out_ref, sem = refs
    pending = []
    for n, codes in enumerate(BACK + turned(BACK) + (SELF, SHARED)):
        block = block_of(owner_ref, partner(codes))
        source = slabs[n] if len(slabs[n].shape) == 2 else slabs[n].at[0]
        copy = pltpu.make_async_copy(source, out_ref.at[jnp.maximum(block, 0)], sem.at[n])

        @pl.when(block >= 0)
        def _(copy=copy):
            copy.start()

        pending.append((block, copy))
    for block, copy in pending:

        @pl.when(block >= 0)
        def _(copy=copy):
            copy.wait()


def per_device_paired(gradients, block_owner, left_gram, right_gram, left_root, right_root):
    owners = lax.axis_size("shard")
    rounds = len(OUT)
    blocks, slab, width = gradients.shape[1:]
    half_rows = left_gram.shape[1]
    rows = BACK + (SHARED, SELF) + turned(BACK)
    theirs_last = (rounds - 1, rounds - 2)
    sooner = OUT + turned(OUT)[:rounds - 2]
    columns = (sooner, tuple(turned(OUT)[k] for k in theirs_last))

    def other_core(x):
        return lax.ppermute(x, "replica", [(0, 1), (1, 0)])

    def trade(x, codes):
        pairs = [(s * 2 + r, (s ^ codes[r]) * 2 + r) for s in range(owners) for r in range(2)]
        return lax.ppermute(x, ("shard", "replica"), pairs)

    def shape(dims, dtype=jnp.bfloat16):
        return jax.ShapeDtypeStruct(dims, dtype)

    def call(kernel, out_shape, in_specs, *args, params=PARAMS, cost_estimate=LIGHT, **options):
        return pl.pallas_call(
            kernel, out_shape=out_shape, in_specs=in_specs, compiler_params=params,
            cost_estimate=cost_estimate, **options
        )(*args)

    block_owner = block_owner.reshape(1, blocks)
    other_gradient = other_core(gradients[0])
    fetched = call(
        fetch_kernel, shape((blocks, slab, width)), [VMEM, ANY], gradients[0], block_owner,
        out_specs=VMEM,
    )
    *outgoing, = call(
        pick_kernel, [shape((slab, width))] * rounds,
        [VMEM, VMEM, VMEM], block_owner, fetched, other_gradient, out_specs=[VMEM] * rounds,
    )
    mine = [trade(x, codes) for x, codes in zip(outgoing, OUT)]
    other_left, other_right = other_core(left_root[0]), other_core(right_root[0])
    left_sooner, left_last, right = call(
        functools.partial(order_kernel, rows, columns),
        [shape((width, len(group) * slab)) for group in columns] + [shape((width, width))],
        [VMEM] * 4, left_root[0], other_left, right_root[0], other_right, out_specs=[VMEM] * 3,
        scratch_shapes=[pltpu.VMEM((width, width), jnp.bfloat16)],
    )
    mine[0], left_sooner, left_last, right = lax.optimization_barrier(
        (mine[0], left_sooner, left_last, right)
    )
    theirs = [other_core(x) for x in mine]
    begun, begun_sq = call(
        begin_kernel,
        [shape((width, width), jnp.float32), shape((8, 128), jnp.float32)],
        [VMEM] * (1 + len(sooner)), left_sooner, *mine, *theirs[:rounds - 2],
        out_specs=[VMEM, VMEM],
        scratch_shapes=[pltpu.VMEM((len(sooner) * slab, width), jnp.bfloat16)],
    )
    half_slab = shape((slab, width // 2))
    *whole, shared, own = call(
        functools.partial(finish_kernel, len(theirs_last)),
        [shape((2, slab, width // 2))] * len(BACK) + [half_slab] * 2,
        [VMEM] * (4 + len(theirs_last)),
        left_last, begun, begun_sq, right, *[theirs[k] for k in theirs_last],
        out_specs=[VMEM] * (len(BACK) + 2),
        scratch_shapes=[
            pltpu.VMEM((len(theirs_last) * slab, width), jnp.bfloat16),
            pltpu.VMEM((width, width), jnp.bfloat16),
            pltpu.VMEM(((len(BACK) + 2) * slab, width), jnp.float32),
        ],
    )
    returned = [trade(x, codes) for x, codes in zip(whole, BACK)]
    shared = trade(shared, SHARED)
    left_new, right_new = call(
        gram_kernel, [shape(left_gram.shape[1:]), shape(right_gram.shape[1:])],
        [VMEM, VMEM, VMEM, ANY] + [VMEM] * (2 * rounds),
        block_owner, left_gram[0], right_gram[0], returned[0], *mine, *theirs,
        out_specs=[VMEM, VMEM],
        scratch_shapes=[pltpu.VMEM((width, width), jnp.bfloat16)],
        cost_estimate=pl.CostEstimate(
            flops=4 * half_rows * width * width, bytes_accessed=8 * half_rows * width,
            transcendentals=0,
        ),
    )
    left_new, right_new, returned[0] = lax.optimization_barrier(
        (left_new, right_new, returned[0])
    )
    passed = [other_core(x[1]) for x in returned]
    update = call(
        place_kernel, shape((blocks, slab, width // 2)), [VMEM] + [ANY] * owners,
        block_owner, *returned, *passed, own, shared,
        out_specs=ANY, scratch_shapes=[pltpu.SemaphoreType.DMA((owners,))],
    )
    return (left_new[None], right_new[None], update)


def solution(mesh):
    owners = mesh.shape["shard"]
    paired = mesh.shape["replica"] == 2 and owners == 2 * len(OUT)
    return jax.shard_map(
        per_device_paired if paired else per_device,
        mesh=mesh,
        in_specs=(
            P("replica", "groups", "shard", None),
            P("groups"),
            P(("groups", "shard"), "replica", None),
            P(("groups", "shard"), "replica", None),
            P(("groups", "shard"), "replica", None),
            P(("groups", "shard"), None, "replica"),
        ),
        out_specs=(
            P(("groups", "shard"), "replica", None),
            P(("groups", "shard"), "replica", None),
            P("groups", "shard", "replica"),
        ),
        check_vma=False,
    )
```

```python
import functools

import jax
import jax.numpy as jnp
from jax import lax
from jax.experimental import pallas as pl
from jax.experimental.pallas import tpu as pltpu
from jax.sharding import PartitionSpec as P

VMEM = pl.BlockSpec(memory_space=pltpu.VMEM)
ANY = pl.BlockSpec(memory_space=pl.ANY)
LIGHT = pl.CostEstimate(flops=0, bytes_accessed=0, transcendentals=0)
OUT = ((2, 6), (1, 5), (0, 4), (3, 7))
BACK = ((2, 4), (3, 5), (1, 7))
SHARED, SELF = (6, 6), (0, 0)
PARAMS = pltpu.CompilerParams(vmem_limit_bytes=24 * 1024 * 1024)


def per_device(gradients, block_owner, left_gram, right_gram, left_root, right_root):
    owners = lax.axis_size("shard")
    half_rows = left_gram.shape[1]
    full_width = left_gram.shape[2]
    first_row = lax.axis_index("replica") * half_rows
    owner_index = lax.broadcasted_iota(jnp.int32, (owners, block_owner.shape[0]), 0)
    owner_onehot = (owner_index == block_owner[None, :]).astype(jnp.bfloat16)
    outgoing = jnp.einsum(
        "ob,brc->orc", owner_onehot, gradients[0], preferred_element_type=jnp.float32
    )
    arrived = lax.all_to_all(
        outgoing.astype(jnp.bfloat16), "shard", split_axis=0, concat_axis=0, tiled=True
    )
    total = lax.psum(arrived.astype(jnp.float32).astype(jnp.bfloat16), "replica")
    summed_block = total.reshape(full_width, full_width)
    own_rows = lax.dynamic_slice_in_dim(summed_block, first_row, half_rows, 0)
    own_cols = lax.dynamic_slice_in_dim(summed_block, first_row, half_rows, 1)
    left_term = lax.dot_general(
        own_rows, summed_block, (((1,), (1,)), ((), ())), preferred_element_type=jnp.float32
    )
    right_term = lax.dot_general(
        own_cols, summed_block, (((0,), (0,)), ((), ())), preferred_element_type=jnp.float32
    )
    left_new = (0.99 * left_gram[0].astype(jnp.float32) + 0.01 * left_term).astype(jnp.bfloat16)
    right_new = (0.99 * right_gram[0].astype(jnp.float32) + 0.01 * right_term).astype(jnp.bfloat16)
    partial_side = jnp.dot(left_root[0], summed_block, preferred_element_type=jnp.float32).astype(
        jnp.bfloat16
    )
    left_side = lax.all_gather(partial_side, "replica", axis=0, tiled=True)
    both_sides = jnp.dot(left_side, right_root[0], preferred_element_type=jnp.float32)
    side_squares = lax.psum(jnp.sum(both_sides * both_sides), "replica")
    grad_squares = jnp.sum(jnp.square(summed_block.astype(jnp.float32)))
    graft = jnp.sqrt(grad_squares / (side_squares + 1e-06))
    scaled = (
        (both_sides * graft).astype(jnp.bfloat16).reshape(owners, full_width // owners, half_rows)
    )
    returned = lax.all_to_all(scaled, "shard", split_axis=0, concat_axis=0, tiled=True)
    update = jnp.take(returned, block_owner, axis=0)
    return (left_new[None], right_new[None], update)


def turned(rounds):
    return tuple(codes[::-1] for codes in rounds)


def partner(codes):
    code = jnp.where(lax.axis_index("replica") == 0, codes[0], codes[1])
    return lax.axis_index("shard") ^ code


def block_of(owner_ref, owner):
    block = jnp.int32(-1)
    for b in range(owner_ref.shape[1]):
        block = jnp.where(owner_ref[0, b] == owner, b, block)
    return block


def squares(value):
    wide = value.astype(jnp.float32)
    rows = jnp.sum((wide * wide).reshape(-1, 8, wide.shape[1]), axis=0)
    return jnp.sum(jnp.sum(rows, axis=0, keepdims=True), axis=1, keepdims=True)


def fetch_kernel(gradient_ref, after_ref, out_ref):
    out_ref[...] = gradient_ref[...]


def pick_kernel(owner_ref, mine_ref, theirs_ref, *out_refs):
    for codes, out_ref in zip(OUT, out_refs):
        b = jnp.maximum(block_of(owner_ref, partner(codes)), 0)
        total = mine_ref[b].astype(jnp.float32) + theirs_ref[b].astype(jnp.float32)
        out_ref[...] = total.astype(out_ref.dtype)


def order_kernel(rows, columns, own_ref, other_ref, own_right_ref, other_right_ref, *refs):
    *out_refs, right_ref, rows_ref = refs
    right_ref[:, :own_right_ref.shape[1]] = own_right_ref[...]
    right_ref[:, own_right_ref.shape[1]:] = other_right_ref[...]
    half, full = own_ref.shape
    slab = full // len(rows)
    core = lax.axis_index("replica")
    for n, codes in enumerate(rows):
        start = partner(codes) * slab
        row = pl.multiple_of(lax.rem(start, half), slab)
        for ref, near in ((own_ref, True), (other_ref, False)):

            @pl.when((lax.div(start, half) == core) == near)
            def _(ref=ref):
                rows_ref[n * slab:(n + 1) * slab, :] = ref[pl.ds(row, slab), :]

    for out_ref, group in zip(out_refs, columns):
        column = lax.broadcasted_iota(jnp.int32, (1, len(group) * slab), 1)
        source = column
        for n, codes in enumerate(group):
            inside = (column >= n * slab) & (column < (n + 1) * slab)
            source = jnp.where(inside, column + (partner(codes) - n) * slab, source)
        row_index = lax.broadcasted_iota(jnp.int32, (full, len(group) * slab), 0)
        choose = (row_index == source).astype(jnp.float32).astype(rows_ref.dtype)
        out_ref[...] = jnp.dot(
            rows_ref[...], choose, preferred_element_type=jnp.float32
        ).astype(out_ref.dtype)


def begin_kernel(left_ref, *refs):
    *slabs, total_ref, grad_sq_ref, stacked_ref = refs
    slab = slabs[0].shape[0]
    for n, ref in enumerate(slabs):
        stacked_ref[n * slab:(n + 1) * slab, :] = ref[...]
    total_ref[...] = jnp.dot(
        left_ref[...], stacked_ref[...], preferred_element_type=jnp.float32
    )
    grad_sq_ref[...] = jnp.broadcast_to(squares(stacked_ref[...]), grad_sq_ref.shape)


def finish_kernel(count, left_ref, total_ref, begun_sq_ref, right_ref, *refs):
    slabs = refs[:count]
    *out_refs, stacked_ref, side_ref, both_ref = refs[count:]
    slab = slabs[0].shape[0]
    used, full = both_ref.shape
    for n, ref in enumerate(slabs):
        stacked_ref[n * slab:(n + 1) * slab, :] = ref[...]
    last = stacked_ref[...]
    side = total_ref[...] + jnp.dot(left_ref[...], last, preferred_element_type=jnp.float32)
    side_ref[...] = side.astype(side_ref.dtype)
    grad_sq = begun_sq_ref[0:1, 0:1] + squares(last)
    both = jnp.dot(side_ref[...], right_ref[...], preferred_element_type=jnp.float32)
    both_ref[...] = both[:used]
    graft = jnp.sqrt(grad_sq / (squares(both) + 1e-06))
    for k, out_ref in enumerate(out_refs):
        rows = slice(k * slab, (k + 1) * slab)
        if len(out_ref.shape) == 2:
            out_ref[...] = (both_ref[rows, :full // 2] * graft).astype(out_ref.dtype)
        else:
            out_ref[0] = (both_ref[rows, :full // 2] * graft).astype(out_ref.dtype)
            out_ref[1] = (both_ref[rows, full // 2:] * graft).astype(out_ref.dtype)


def gram_kernel(owner_ref, left_ref, right_ref, after_ref, *refs):
    *slabs, left_out, right_out, summed_ref = refs
    slab = slabs[0].shape[0]
    for codes, ref in zip(OUT + turned(OUT), slabs):
        row = pl.multiple_of(partner(codes) * slab, slab)
        summed_ref[pl.ds(row, slab), :] = ref[...]
    half = left_ref.shape[0]
    first = pl.multiple_of(lax.axis_index("replica") * half, 128)
    present = block_of(owner_ref, lax.axis_index("shard")) >= 0
    share = jnp.where(present, 0.01, 0.0).astype(jnp.float32)
    summed = summed_ref[...]
    left_term = lax.dot_general(
        summed_ref[pl.ds(first, half), :], summed, (((1,), (1,)), ((), ())),
        preferred_element_type=jnp.float32,
    )
    left_out[...] = (0.99 * left_ref[...].astype(jnp.float32) + share * left_term).astype(
        left_out.dtype
    )
    right_term = lax.dot_general(
        summed_ref[:, pl.ds(first, half)], summed, (((0,), (0,)), ((), ())),
        preferred_element_type=jnp.float32,
    )
    right_out[...] = (0.99 * right_ref[...].astype(jnp.float32) + share * right_term).astype(
        right_out.dtype
    )


def place_kernel(owner_ref, *refs):
    *slabs, out_ref, sem = refs
    pending = []
    for n, codes in enumerate(BACK + turned(BACK) + (SELF, SHARED)):
        block = block_of(owner_ref, partner(codes))
        source = slabs[n] if len(slabs[n].shape) == 2 else slabs[n].at[0]
        copy = pltpu.make_async_copy(source, out_ref.at[jnp.maximum(block, 0)], sem.at[n])

        @pl.when(block >= 0)
        def _(copy=copy):
            copy.start()

        pending.append((block, copy))
    for block, copy in pending:

        @pl.when(block >= 0)
        def _(copy=copy):
            copy.wait()


def per_device_paired(gradients, block_owner, left_gram, right_gram, left_root, right_root):
    owners = lax.axis_size("shard")
    rounds = len(OUT)
    blocks, slab, width = gradients.shape[1:]
    half_rows = left_gram.shape[1]
    rows = BACK + (SHARED, SELF) + turned(BACK)
    theirs_last = (rounds - 1, rounds - 2)
    sooner = OUT + turned(OUT)[:rounds - 2]
    columns = (sooner, tuple(turned(OUT)[k] for k in theirs_last))

    def other_core(x):
        return lax.ppermute(x, "replica", [(0, 1), (1, 0)])

    def trade(x, codes):
        pairs = [(s * 2 + r, (s ^ codes[r]) * 2 + r) for s in range(owners) for r in range(2)]
        return lax.ppermute(x, ("shard", "replica"), pairs)

    def shape(dims, dtype=jnp.bfloat16):
        return jax.ShapeDtypeStruct(dims, dtype)

    def call(kernel, out_shape, in_specs, *args, params=PARAMS, cost_estimate=LIGHT, **options):
        return pl.pallas_call(
            kernel, out_shape=out_shape, in_specs=in_specs, compiler_params=params,
            cost_estimate=cost_estimate, **options
        )(*args)

    block_owner = block_owner.reshape(1, blocks)
    other_gradient = other_core(gradients[0])
    fetched = call(
        fetch_kernel, shape((blocks, slab, width)), [VMEM, ANY], gradients[0], block_owner,
        out_specs=VMEM,
    )
    *outgoing, = call(
        pick_kernel, [shape((slab, width))] * rounds,
        [VMEM, VMEM, VMEM], block_owner, fetched, other_gradient, out_specs=[VMEM] * rounds,
    )
    mine = [trade(x, codes) for x, codes in zip(outgoing, OUT)]
    other_left, other_right = other_core(left_root[0]), other_core(right_root[0])
    left_sooner, left_last, right = call(
        functools.partial(order_kernel, rows, columns),
        [shape((width, len(group) * slab)) for group in columns] + [shape((width, width))],
        [VMEM] * 4, left_root[0], other_left, right_root[0], other_right, out_specs=[VMEM] * 3,
        scratch_shapes=[pltpu.VMEM((width, width), jnp.bfloat16)],
    )
    mine[0], left_sooner, left_last, right = lax.optimization_barrier(
        (mine[0], left_sooner, left_last, right)
    )
    theirs = [other_core(x) for x in mine]
    begun, begun_sq = call(
        begin_kernel,
        [shape((width, width), jnp.float32), shape((8, 128), jnp.float32)],
        [VMEM] * (1 + len(sooner)), left_sooner, *mine, *theirs[:rounds - 2],
        out_specs=[VMEM, VMEM],
        scratch_shapes=[pltpu.VMEM((len(sooner) * slab, width), jnp.bfloat16)],
    )
    half_slab = shape((slab, width // 2))
    *whole, shared, own = call(
        functools.partial(finish_kernel, len(theirs_last)),
        [shape((2, slab, width // 2))] * len(BACK) + [half_slab] * 2,
        [VMEM] * (4 + len(theirs_last)),
        left_last, begun, begun_sq, right, *[theirs[k] for k in theirs_last],
        out_specs=[VMEM] * (len(BACK) + 2),
        scratch_shapes=[
            pltpu.VMEM((len(theirs_last) * slab, width), jnp.bfloat16),
            pltpu.VMEM((width, width), jnp.bfloat16),
            pltpu.VMEM(((len(BACK) + 2) * slab, width), jnp.float32),
        ],
    )
    returned = [trade(x, codes) for x, codes in zip(whole, BACK)]
    left_new, right_new = call(
        gram_kernel, [shape(left_gram.shape[1:]), shape(right_gram.shape[1:])],
        [VMEM, VMEM, VMEM, ANY] + [VMEM] * (2 * rounds),
        block_owner, left_gram[0], right_gram[0], own, *mine, *theirs,
        out_specs=[VMEM, VMEM],
        scratch_shapes=[pltpu.VMEM((width, width), jnp.bfloat16)],
        cost_estimate=pl.CostEstimate(
            flops=4 * half_rows * width * width, bytes_accessed=8 * half_rows * width,
            transcendentals=0,
        ),
    )
    left_new, right_new, shared, returned[0] = lax.optimization_barrier(
        (left_new, right_new, shared, returned[0])
    )
    shared = trade(shared, SHARED)
    passed = [other_core(x[1]) for x in returned]
    update = call(
        place_kernel, shape((blocks, slab, width // 2)), [VMEM] + [ANY] * owners,
        block_owner, *returned, *passed, own, shared,
        out_specs=ANY, scratch_shapes=[pltpu.SemaphoreType.DMA((owners,))],
    )
    return (left_new[None], right_new[None], update)


def solution(mesh):
    owners = mesh.shape["shard"]
    paired = mesh.shape["replica"] == 2 and owners == 2 * len(OUT)
    return jax.shard_map(
        per_device_paired if paired else per_device,
        mesh=mesh,
        in_specs=(
            P("replica", "groups", "shard", None),
            P("groups"),
            P(("groups", "shard"), "replica", None),
            P(("groups", "shard"), "replica", None),
            P(("groups", "shard"), "replica", None),
            P(("groups", "shard"), None, "replica"),
        ),
        out_specs=(
            P(("groups", "shard"), "replica", None),
            P(("groups", "shard"), "replica", None),
            P("groups", "shard", "replica"),
        ),
        check_vma=False,
    )
```

```python
import functools

import jax
import jax.numpy as jnp
from jax import lax
from jax.experimental import pallas as pl
from jax.experimental.pallas import tpu as pltpu
from jax.sharding import PartitionSpec as P

VMEM = pl.BlockSpec(memory_space=pltpu.VMEM)
ANY = pl.BlockSpec(memory_space=pl.ANY)
LIGHT = pl.CostEstimate(flops=0, bytes_accessed=0, transcendentals=0)
OUT = ((2, 6), (1, 5), (0, 4), (3, 7))
BACK = ((2, 4), (3, 5), (1, 6))
SHARED, SELF = (7, 7), (0, 0)
PARAMS = pltpu.CompilerParams(vmem_limit_bytes=24 * 1024 * 1024)


def per_device(gradients, block_owner, left_gram, right_gram, left_root, right_root):
    owners = lax.axis_size("shard")
    half_rows = left_gram.shape[1]
    full_width = left_gram.shape[2]
    first_row = lax.axis_index("replica") * half_rows
    owner_index = lax.broadcasted_iota(jnp.int32, (owners, block_owner.shape[0]), 0)
    owner_onehot = (owner_index == block_owner[None, :]).astype(jnp.bfloat16)
    outgoing = jnp.einsum(
        "ob,brc->orc", owner_onehot, gradients[0], preferred_element_type=jnp.float32
    )
    arrived = lax.all_to_all(
        outgoing.astype(jnp.bfloat16), "shard", split_axis=0, concat_axis=0, tiled=True
    )
    total = lax.psum(arrived.astype(jnp.float32).astype(jnp.bfloat16), "replica")
    summed_block = total.reshape(full_width, full_width)
    own_rows = lax.dynamic_slice_in_dim(summed_block, first_row, half_rows, 0)
    own_cols = lax.dynamic_slice_in_dim(summed_block, first_row, half_rows, 1)
    left_term = lax.dot_general(
        own_rows, summed_block, (((1,), (1,)), ((), ())), preferred_element_type=jnp.float32
    )
    right_term = lax.dot_general(
        own_cols, summed_block, (((0,), (0,)), ((), ())), preferred_element_type=jnp.float32
    )
    left_new = (0.99 * left_gram[0].astype(jnp.float32) + 0.01 * left_term).astype(jnp.bfloat16)
    right_new = (0.99 * right_gram[0].astype(jnp.float32) + 0.01 * right_term).astype(jnp.bfloat16)
    partial_side = jnp.dot(left_root[0], summed_block, preferred_element_type=jnp.float32).astype(
        jnp.bfloat16
    )
    left_side = lax.all_gather(partial_side, "replica", axis=0, tiled=True)
    both_sides = jnp.dot(left_side, right_root[0], preferred_element_type=jnp.float32)
    side_squares = lax.psum(jnp.sum(both_sides * both_sides), "replica")
    grad_squares = jnp.sum(jnp.square(summed_block.astype(jnp.float32)))
    graft = jnp.sqrt(grad_squares / (side_squares + 1e-06))
    scaled = (
        (both_sides * graft).astype(jnp.bfloat16).reshape(owners, full_width // owners, half_rows)
    )
    returned = lax.all_to_all(scaled, "shard", split_axis=0, concat_axis=0, tiled=True)
    update = jnp.take(returned, block_owner, axis=0)
    return (left_new[None], right_new[None], update)


def turned(rounds):
    return tuple(codes[::-1] for codes in rounds)


def partner(codes):
    code = jnp.where(lax.axis_index("replica") == 0, codes[0], codes[1])
    return lax.axis_index("shard") ^ code


def block_of(owner_ref, owner):
    block = jnp.int32(-1)
    for b in range(owner_ref.shape[1]):
        block = jnp.where(owner_ref[0, b] == owner, b, block)
    return block


def squares(value):
    wide = value.astype(jnp.float32)
    rows = jnp.sum((wide * wide).reshape(-1, 8, wide.shape[1]), axis=0)
    return jnp.sum(jnp.sum(rows, axis=0, keepdims=True), axis=1, keepdims=True)


def fetch_kernel(gradient_ref, after_ref, out_ref):
    out_ref[...] = gradient_ref[...]


def pick_kernel(owner_ref, mine_ref, theirs_ref, *out_refs):
    for codes, out_ref in zip(OUT, out_refs):
        b = jnp.maximum(block_of(owner_ref, partner(codes)), 0)
        total = mine_ref[b].astype(jnp.float32) + theirs_ref[b].astype(jnp.float32)
        out_ref[...] = total.astype(out_ref.dtype)


def order_kernel(rows, columns, own_ref, other_ref, own_right_ref, other_right_ref, *refs):
    *out_refs, right_ref, rows_ref = refs
    right_ref[:, :own_right_ref.shape[1]] = own_right_ref[...]
    right_ref[:, own_right_ref.shape[1]:] = other_right_ref[...]
    half, full = own_ref.shape
    slab = full // len(rows)
    core = lax.axis_index("replica")
    for n, codes in enumerate(rows):
        start = partner(codes) * slab
        row = pl.multiple_of(lax.rem(start, half), slab)
        for ref, near in ((own_ref, True), (other_ref, False)):

            @pl.when((lax.div(start, half) == core) == near)
            def _(ref=ref):
                rows_ref[n * slab:(n + 1) * slab, :] = ref[pl.ds(row, slab), :]

    for out_ref, group in zip(out_refs, columns):
        column = lax.broadcasted_iota(jnp.int32, (1, len(group) * slab), 1)
        source = column
        for n, codes in enumerate(group):
            inside = (column >= n * slab) & (column < (n + 1) * slab)
            source = jnp.where(inside, column + (partner(codes) - n) * slab, source)
        row_index = lax.broadcasted_iota(jnp.int32, (full, len(group) * slab), 0)
        choose = (row_index == source).astype(jnp.float32).astype(rows_ref.dtype)
        out_ref[...] = jnp.dot(
            rows_ref[...], choose, preferred_element_type=jnp.float32
        ).astype(out_ref.dtype)


def begin_kernel(left_ref, *refs):
    *slabs, total_ref, grad_sq_ref, stacked_ref = refs
    slab = slabs[0].shape[0]
    for n, ref in enumerate(slabs):
        stacked_ref[n * slab:(n + 1) * slab, :] = ref[...]
    total_ref[...] = jnp.dot(
        left_ref[...], stacked_ref[...], preferred_element_type=jnp.float32
    )
    grad_sq_ref[...] = jnp.broadcast_to(squares(stacked_ref[...]), grad_sq_ref.shape)


def finish_kernel(count, left_ref, total_ref, begun_sq_ref, right_ref, *refs):
    slabs = refs[:count]
    *out_refs, stacked_ref, side_ref, both_ref = refs[count:]
    slab = slabs[0].shape[0]
    used, full = both_ref.shape
    for n, ref in enumerate(slabs):
        stacked_ref[n * slab:(n + 1) * slab, :] = ref[...]
    last = stacked_ref[...]
    side = total_ref[...] + jnp.dot(left_ref[...], last, preferred_element_type=jnp.float32)
    side_ref[...] = side.astype(side_ref.dtype)
    grad_sq = begun_sq_ref[0:1, 0:1] + squares(last)
    both = jnp.dot(side_ref[...], right_ref[...], preferred_element_type=jnp.float32)
    both_ref[...] = both[:used]
    graft = jnp.sqrt(grad_sq / (squares(both) + 1e-06))
    for k, out_ref in enumerate(out_refs):
        rows = slice(k * slab, (k + 1) * slab)
        if len(out_ref.shape) == 2:
            out_ref[...] = (both_ref[rows, :full // 2] * graft).astype(out_ref.dtype)
        else:
            out_ref[0] = (both_ref[rows, :full // 2] * graft).astype(out_ref.dtype)
            out_ref[1] = (both_ref[rows, full // 2:] * graft).astype(out_ref.dtype)


def gram_kernel(owner_ref, left_ref, right_ref, after_ref, *refs):
    *slabs, left_out, right_out, summed_ref = refs
    slab = slabs[0].shape[0]
    for codes, ref in zip(OUT + turned(OUT), slabs):
        row = pl.multiple_of(partner(codes) * slab, slab)
        summed_ref[pl.ds(row, slab), :] = ref[...]
    half = left_ref.shape[0]
    first = pl.multiple_of(lax.axis_index("replica") * half, 128)
    present = block_of(owner_ref, lax.axis_index("shard")) >= 0
    share = jnp.where(present, 0.01, 0.0).astype(jnp.float32)
    summed = summed_ref[...]
    left_term = lax.dot_general(
        summed_ref[pl.ds(first, half), :], summed, (((1,), (1,)), ((), ())),
        preferred_element_type=jnp.float32,
    )
    left_out[...] = (0.99 * left_ref[...].astype(jnp.float32) + share * left_term).astype(
        left_out.dtype
    )
    right_term = lax.dot_general(
        summed_ref[:, pl.ds(first, half)], summed, (((0,), (0,)), ((), ())),
        preferred_element_type=jnp.float32,
    )
    right_out[...] = (0.99 * right_ref[...].astype(jnp.float32) + share * right_term).astype(
        right_out.dtype
    )


def place_kernel(owner_ref, *refs):
    *slabs, out_ref, sem = refs
    pending = []
    for n, codes in enumerate(BACK + turned(BACK) + (SELF, SHARED)):
        block = block_of(owner_ref, partner(codes))
        source = slabs[n] if len(slabs[n].shape) == 2 else slabs[n].at[0]
        copy = pltpu.make_async_copy(source, out_ref.at[jnp.maximum(block, 0)], sem.at[n])

        @pl.when(block >= 0)
        def _(copy=copy):
            copy.start()

        pending.append((block, copy))
    for block, copy in pending:

        @pl.when(block >= 0)
        def _(copy=copy):
            copy.wait()


def per_device_paired(gradients, block_owner, left_gram, right_gram, left_root, right_root):
    owners = lax.axis_size("shard")
    rounds = len(OUT)
    blocks, slab, width = gradients.shape[1:]
    half_rows = left_gram.shape[1]
    rows = BACK + (SHARED, SELF) + turned(BACK)
    theirs_last = (rounds - 1, rounds - 2)
    sooner = OUT + turned(OUT)[:rounds - 2]
    columns = (sooner, tuple(turned(OUT)[k] for k in theirs_last))

    def other_core(x):
        return lax.ppermute(x, "replica", [(0, 1), (1, 0)])

    def trade(x, codes):
        pairs = [(s * 2 + r, (s ^ codes[r]) * 2 + r) for s in range(owners) for r in range(2)]
        return lax.ppermute(x, ("shard", "replica"), pairs)

    def shape(dims, dtype=jnp.bfloat16):
        return jax.ShapeDtypeStruct(dims, dtype)

    def call(kernel, out_shape, in_specs, *args, params=PARAMS, cost_estimate=LIGHT, **options):
        return pl.pallas_call(
            kernel, out_shape=out_shape, in_specs=in_specs, compiler_params=params,
            cost_estimate=cost_estimate, **options
        )(*args)

    block_owner = block_owner.reshape(1, blocks)
    other_gradient = other_core(gradients[0])
    fetched = call(
        fetch_kernel, shape((blocks, slab, width)), [VMEM, ANY], gradients[0], block_owner,
        out_specs=VMEM,
    )
    *outgoing, = call(
        pick_kernel, [shape((slab, width))] * rounds,
        [VMEM, VMEM, VMEM], block_owner, fetched, other_gradient, out_specs=[VMEM] * rounds,
    )
    mine = [trade(x, codes) for x, codes in zip(outgoing, OUT)]
    other_left, other_right = other_core(left_root[0]), other_core(right_root[0])
    left_sooner, left_last, right = call(
        functools.partial(order_kernel, rows, columns),
        [shape((width, len(group) * slab)) for group in columns] + [shape((width, width))],
        [VMEM] * 4, left_root[0], other_left, right_root[0], other_right, out_specs=[VMEM] * 3,
        scratch_shapes=[pltpu.VMEM((width, width), jnp.bfloat16)],
    )
    mine[0], left_sooner, left_last, right = lax.optimization_barrier(
        (mine[0], left_sooner, left_last, right)
    )
    theirs = [other_core(x) for x in mine]
    begun, begun_sq = call(
        begin_kernel,
        [shape((width, width), jnp.float32), shape((8, 128), jnp.float32)],
        [VMEM] * (1 + len(sooner)), left_sooner, *mine, *theirs[:rounds - 2],
        out_specs=[VMEM, VMEM],
        scratch_shapes=[pltpu.VMEM((len(sooner) * slab, width), jnp.bfloat16)],
    )
    half_slab = shape((slab, width // 2))
    *whole, shared, own = call(
        functools.partial(finish_kernel, len(theirs_last)),
        [shape((2, slab, width // 2))] * len(BACK) + [half_slab] * 2,
        [VMEM] * (4 + len(theirs_last)),
        left_last, begun, begun_sq, right, *[theirs[k] for k in theirs_last],
        out_specs=[VMEM] * (len(BACK) + 2),
        scratch_shapes=[
            pltpu.VMEM((len(theirs_last) * slab, width), jnp.bfloat16),
            pltpu.VMEM((width, width), jnp.bfloat16),
            pltpu.VMEM(((len(BACK) + 2) * slab, width), jnp.float32),
        ],
    )
    returned = [trade(x, codes) for x, codes in zip(whole, BACK)]
    shared = trade(shared, SHARED)
    left_new, right_new = call(
        gram_kernel, [shape(left_gram.shape[1:]), shape(right_gram.shape[1:])],
        [VMEM, VMEM, VMEM, ANY] + [VMEM] * (2 * rounds),
        block_owner, left_gram[0], right_gram[0], returned[0], *mine, *theirs,
        out_specs=[VMEM, VMEM],
        scratch_shapes=[pltpu.VMEM((width, width), jnp.bfloat16)],
        cost_estimate=pl.CostEstimate(
            flops=4 * half_rows * width * width, bytes_accessed=8 * half_rows * width,
            transcendentals=0,
        ),
    )
    left_new, right_new, returned[0] = lax.optimization_barrier(
        (left_new, right_new, returned[0])
    )
    passed = [other_core(x[1]) for x in returned]
    update = call(
        place_kernel, shape((blocks, slab, width // 2)), [VMEM] + [ANY] * owners,
        block_owner, *returned, *passed, own, shared,
        out_specs=ANY, scratch_shapes=[pltpu.SemaphoreType.DMA((owners,))],
    )
    return (left_new[None], right_new[None], update)


def solution(mesh):
    owners = mesh.shape["shard"]
    paired = mesh.shape["replica"] == 2 and owners == 2 * len(OUT)
    return jax.shard_map(
        per_device_paired if paired else per_device,
        mesh=mesh,
        in_specs=(
            P("replica", "groups", "shard", None),
            P("groups"),
            P(("groups", "shard"), "replica", None),
            P(("groups", "shard"), "replica", None),
            P(("groups", "shard"), "replica", None),
            P(("groups", "shard"), None, "replica"),
        ),
        out_specs=(
            P(("groups", "shard"), "replica", None),
            P(("groups", "shard"), "replica", None),
            P("groups", "shard", "replica"),
        ),
        check_vma=False,
    )
```

```python
import functools

import jax
import jax.numpy as jnp
from jax import lax
from jax.experimental import pallas as pl
from jax.experimental.pallas import tpu as pltpu
from jax.sharding import PartitionSpec as P

VMEM = pl.BlockSpec(memory_space=pltpu.VMEM)
ANY = pl.BlockSpec(memory_space=pl.ANY)
LIGHT = pl.CostEstimate(flops=0, bytes_accessed=0, transcendentals=0)
OUT = ((2, 6), (1, 5), (0, 4), (3, 7))
BACK = ((2, 6), (3, 5), (1, 4))
SHARED, SELF = (7, 7), (0, 0)
PARAMS = pltpu.CompilerParams(vmem_limit_bytes=24 * 1024 * 1024)


def per_device(gradients, block_owner, left_gram, right_gram, left_root, right_root):
    owners = lax.axis_size("shard")
    half_rows = left_gram.shape[1]
    full_width = left_gram.shape[2]
    first_row = lax.axis_index("replica") * half_rows
    owner_index = lax.broadcasted_iota(jnp.int32, (owners, block_owner.shape[0]), 0)
    owner_onehot = (owner_index == block_owner[None, :]).astype(jnp.bfloat16)
    outgoing = jnp.einsum(
        "ob,brc->orc", owner_onehot, gradients[0], preferred_element_type=jnp.float32
    )
    arrived = lax.all_to_all(
        outgoing.astype(jnp.bfloat16), "shard", split_axis=0, concat_axis=0, tiled=True
    )
    total = lax.psum(arrived.astype(jnp.float32).astype(jnp.bfloat16), "replica")
    summed_block = total.reshape(full_width, full_width)
    own_rows = lax.dynamic_slice_in_dim(summed_block, first_row, half_rows, 0)
    own_cols = lax.dynamic_slice_in_dim(summed_block, first_row, half_rows, 1)
    left_term = lax.dot_general(
        own_rows, summed_block, (((1,), (1,)), ((), ())), preferred_element_type=jnp.float32
    )
    right_term = lax.dot_general(
        own_cols, summed_block, (((0,), (0,)), ((), ())), preferred_element_type=jnp.float32
    )
    left_new = (0.99 * left_gram[0].astype(jnp.float32) + 0.01 * left_term).astype(jnp.bfloat16)
    right_new = (0.99 * right_gram[0].astype(jnp.float32) + 0.01 * right_term).astype(jnp.bfloat16)
    partial_side = jnp.dot(left_root[0], summed_block, preferred_element_type=jnp.float32).astype(
        jnp.bfloat16
    )
    left_side = lax.all_gather(partial_side, "replica", axis=0, tiled=True)
    both_sides = jnp.dot(left_side, right_root[0], preferred_element_type=jnp.float32)
    side_squares = lax.psum(jnp.sum(both_sides * both_sides), "replica")
    grad_squares = jnp.sum(jnp.square(summed_block.astype(jnp.float32)))
    graft = jnp.sqrt(grad_squares / (side_squares + 1e-06))
    scaled = (
        (both_sides * graft).astype(jnp.bfloat16).reshape(owners, full_width // owners, half_rows)
    )
    returned = lax.all_to_all(scaled, "shard", split_axis=0, concat_axis=0, tiled=True)
    update = jnp.take(returned, block_owner, axis=0)
    return (left_new[None], right_new[None], update)


def turned(rounds):
    return tuple(codes[::-1] for codes in rounds)


def partner(codes):
    code = jnp.where(lax.axis_index("replica") == 0, codes[0], codes[1])
    return lax.axis_index("shard") ^ code


def block_of(owner_ref, owner):
    block = jnp.int32(-1)
    for b in range(owner_ref.shape[1]):
        block = jnp.where(owner_ref[0, b] == owner, b, block)
    return block


def squares(value):
    wide = value.astype(jnp.float32)
    rows = jnp.sum((wide * wide).reshape(-1, 8, wide.shape[1]), axis=0)
    return jnp.sum(jnp.sum(rows, axis=0, keepdims=True), axis=1, keepdims=True)


def fetch_kernel(gradient_ref, after_ref, out_ref):
    out_ref[...] = gradient_ref[...]


def pick_kernel(owner_ref, mine_ref, theirs_ref, *out_refs):
    for codes, out_ref in zip(OUT, out_refs):
        b = jnp.maximum(block_of(owner_ref, partner(codes)), 0)
        total = mine_ref[b].astype(jnp.float32) + theirs_ref[b].astype(jnp.float32)
        out_ref[...] = total.astype(out_ref.dtype)


def order_kernel(rows, columns, own_ref, other_ref, own_right_ref, other_right_ref, *refs):
    *out_refs, right_ref, rows_ref = refs
    right_ref[:, :own_right_ref.shape[1]] = own_right_ref[...]
    right_ref[:, own_right_ref.shape[1]:] = other_right_ref[...]
    half, full = own_ref.shape
    slab = full // len(rows)
    core = lax.axis_index("replica")
    for n, codes in enumerate(rows):
        start = partner(codes) * slab
        row = pl.multiple_of(lax.rem(start, half), slab)
        for ref, near in ((own_ref, True), (other_ref, False)):

            @pl.when((lax.div(start, half) == core) == near)
            def _(ref=ref):
                rows_ref[n * slab:(n + 1) * slab, :] = ref[pl.ds(row, slab), :]

    for out_ref, group in zip(out_refs, columns):
        column = lax.broadcasted_iota(jnp.int32, (1, len(group) * slab), 1)
        source = column
        for n, codes in enumerate(group):
            inside = (column >= n * slab) & (column < (n + 1) * slab)
            source = jnp.where(inside, column + (partner(codes) - n) * slab, source)
        row_index = lax.broadcasted_iota(jnp.int32, (full, len(group) * slab), 0)
        choose = (row_index == source).astype(jnp.float32).astype(rows_ref.dtype)
        out_ref[...] = jnp.dot(
            rows_ref[...], choose, preferred_element_type=jnp.float32
        ).astype(out_ref.dtype)


def begin_kernel(left_ref, *refs):
    *slabs, total_ref, grad_sq_ref, stacked_ref = refs
    slab = slabs[0].shape[0]
    for n, ref in enumerate(slabs):
        stacked_ref[n * slab:(n + 1) * slab, :] = ref[...]
    total_ref[...] = jnp.dot(
        left_ref[...], stacked_ref[...], preferred_element_type=jnp.float32
    )
    grad_sq_ref[...] = jnp.broadcast_to(squares(stacked_ref[...]), grad_sq_ref.shape)


def finish_kernel(count, left_ref, total_ref, begun_sq_ref, right_ref, *refs):
    slabs = refs[:count]
    *out_refs, stacked_ref, side_ref, both_ref = refs[count:]
    slab = slabs[0].shape[0]
    used, full = both_ref.shape
    for n, ref in enumerate(slabs):
        stacked_ref[n * slab:(n + 1) * slab, :] = ref[...]
    last = stacked_ref[...]
    side = total_ref[...] + jnp.dot(left_ref[...], last, preferred_element_type=jnp.float32)
    side_ref[...] = side.astype(side_ref.dtype)
    grad_sq = begun_sq_ref[0:1, 0:1] + squares(last)
    both = jnp.dot(side_ref[...], right_ref[...], preferred_element_type=jnp.float32)
    both_ref[...] = both[:used]
    graft = jnp.sqrt(grad_sq / (squares(both) + 1e-06))
    for k, out_ref in enumerate(out_refs):
        rows = slice(k * slab, (k + 1) * slab)
        if len(out_ref.shape) == 2:
            out_ref[...] = (both_ref[rows, :full // 2] * graft).astype(out_ref.dtype)
        else:
            out_ref[0] = (both_ref[rows, :full // 2] * graft).astype(out_ref.dtype)
            out_ref[1] = (both_ref[rows, full // 2:] * graft).astype(out_ref.dtype)


def gram_kernel(owner_ref, left_ref, right_ref, after_ref, *refs):
    *slabs, left_out, right_out, summed_ref = refs
    slab = slabs[0].shape[0]
    for codes, ref in zip(OUT + turned(OUT), slabs):
        row = pl.multiple_of(partner(codes) * slab, slab)
        summed_ref[pl.ds(row, slab), :] = ref[...]
    half = left_ref.shape[0]
    first = pl.multiple_of(lax.axis_index("replica") * half, 128)
    present = block_of(owner_ref, lax.axis_index("shard")) >= 0
    share = jnp.where(present, 0.01, 0.0).astype(jnp.float32)
    summed = summed_ref[...]
    left_term = lax.dot_general(
        summed_ref[pl.ds(first, half), :], summed, (((1,), (1,)), ((), ())),
        preferred_element_type=jnp.float32,
    )
    left_out[...] = (0.99 * left_ref[...].astype(jnp.float32) + share * left_term).astype(
        left_out.dtype
    )
    right_term = lax.dot_general(
        summed_ref[:, pl.ds(first, half)], summed, (((0,), (0,)), ((), ())),
        preferred_element_type=jnp.float32,
    )
    right_out[...] = (0.99 * right_ref[...].astype(jnp.float32) + share * right_term).astype(
        right_out.dtype
    )


def place_kernel(owner_ref, *refs):
    *slabs, out_ref, sem = refs
    pending = []
    for n, codes in enumerate(BACK + turned(BACK) + (SELF, SHARED)):
        block = block_of(owner_ref, partner(codes))
        source = slabs[n] if len(slabs[n].shape) == 2 else slabs[n].at[0]
        copy = pltpu.make_async_copy(source, out_ref.at[jnp.maximum(block, 0)], sem.at[n])

        @pl.when(block >= 0)
        def _(copy=copy):
            copy.start()

        pending.append((block, copy))
    for block, copy in pending:

        @pl.when(block >= 0)
        def _(copy=copy):
            copy.wait()


def per_device_paired(gradients, block_owner, left_gram, right_gram, left_root, right_root):
    owners = lax.axis_size("shard")
    rounds = len(OUT)
    blocks, slab, width = gradients.shape[1:]
    half_rows = left_gram.shape[1]
    rows = BACK + (SHARED, SELF) + turned(BACK)
    theirs_last = (rounds - 1, rounds - 2)
    sooner = OUT + turned(OUT)[:rounds - 2]
    columns = (sooner, tuple(turned(OUT)[k] for k in theirs_last))

    def other_core(x):
        return lax.ppermute(x, "replica", [(0, 1), (1, 0)])

    def trade(x, codes):
        pairs = [(s * 2 + r, (s ^ codes[r]) * 2 + r) for s in range(owners) for r in range(2)]
        return lax.ppermute(x, ("shard", "replica"), pairs)

    def shape(dims, dtype=jnp.bfloat16):
        return jax.ShapeDtypeStruct(dims, dtype)

    def call(kernel, out_shape, in_specs, *args, params=PARAMS, cost_estimate=LIGHT, **options):
        return pl.pallas_call(
            kernel, out_shape=out_shape, in_specs=in_specs, compiler_params=params,
            cost_estimate=cost_estimate, **options
        )(*args)

    block_owner = block_owner.reshape(1, blocks)
    other_gradient = other_core(gradients[0])
    fetched = call(
        fetch_kernel, shape((blocks, slab, width)), [VMEM, ANY], gradients[0], block_owner,
        out_specs=VMEM,
    )
    *outgoing, = call(
        pick_kernel, [shape((slab, width))] * rounds,
        [VMEM, VMEM, VMEM], block_owner, fetched, other_gradient, out_specs=[VMEM] * rounds,
    )
    mine = [trade(x, codes) for x, codes in zip(outgoing, OUT)]
    other_left, other_right = other_core(left_root[0]), other_core(right_root[0])
    left_sooner, left_last, right = call(
        functools.partial(order_kernel, rows, columns),
        [shape((width, len(group) * slab)) for group in columns] + [shape((width, width))],
        [VMEM] * 4, left_root[0], other_left, right_root[0], other_right, out_specs=[VMEM] * 3,
        scratch_shapes=[pltpu.VMEM((width, width), jnp.bfloat16)],
    )
    mine[0], left_sooner, left_last, right = lax.optimization_barrier(
        (mine[0], left_sooner, left_last, right)
    )
    theirs = [other_core(x) for x in mine]
    begun, begun_sq = call(
        begin_kernel,
        [shape((width, width), jnp.float32), shape((8, 128), jnp.float32)],
        [VMEM] * (1 + len(sooner)), left_sooner, *mine, *theirs[:rounds - 2],
        out_specs=[VMEM, VMEM],
        scratch_shapes=[pltpu.VMEM((len(sooner) * slab, width), jnp.bfloat16)],
    )
    half_slab = shape((slab, width // 2))
    *whole, shared, own = call(
        functools.partial(finish_kernel, len(theirs_last)),
        [shape((2, slab, width // 2))] * len(BACK) + [half_slab] * 2,
        [VMEM] * (4 + len(theirs_last)),
        left_last, begun, begun_sq, right, *[theirs[k] for k in theirs_last],
        out_specs=[VMEM] * (len(BACK) + 2),
        scratch_shapes=[
            pltpu.VMEM((len(theirs_last) * slab, width), jnp.bfloat16),
            pltpu.VMEM((width, width), jnp.bfloat16),
            pltpu.VMEM(((len(BACK) + 2) * slab, width), jnp.float32),
        ],
    )
    returned = [trade(x, codes) for x, codes in zip(whole, BACK)]
    shared = trade(shared, SHARED)
    left_new, right_new = call(
        gram_kernel, [shape(left_gram.shape[1:]), shape(right_gram.shape[1:])],
        [VMEM, VMEM, VMEM, ANY] + [VMEM] * (2 * rounds),
        block_owner, left_gram[0], right_gram[0], returned[0], *mine, *theirs,
        out_specs=[VMEM, VMEM],
        scratch_shapes=[pltpu.VMEM((width, width), jnp.bfloat16)],
        cost_estimate=pl.CostEstimate(
            flops=4 * half_rows * width * width, bytes_accessed=8 * half_rows * width,
            transcendentals=0,
        ),
    )
    left_new, right_new, returned[0] = lax.optimization_barrier(
        (left_new, right_new, returned[0])
    )
    passed = [other_core(x[1]) for x in returned]
    update = call(
        place_kernel, shape((blocks, slab, width // 2)), [VMEM] + [ANY] * owners,
        block_owner, *returned, *passed, own, shared,
        out_specs=ANY, scratch_shapes=[pltpu.SemaphoreType.DMA((owners,))],
    )
    return (left_new[None], right_new[None], update)


def solution(mesh):
    owners = mesh.shape["shard"]
    paired = mesh.shape["replica"] == 2 and owners == 2 * len(OUT)
    return jax.shard_map(
        per_device_paired if paired else per_device,
        mesh=mesh,
        in_specs=(
            P("replica", "groups", "shard", None),
            P("groups"),
            P(("groups", "shard"), "replica", None),
            P(("groups", "shard"), "replica", None),
            P(("groups", "shard"), "replica", None),
            P(("groups", "shard"), None, "replica"),
        ),
        out_specs=(
            P(("groups", "shard"), "replica", None),
            P(("groups", "shard"), "replica", None),
            P("groups", "shard", "replica"),
        ),
        check_vma=False,
    )
```

```python
import functools

import jax
import jax.numpy as jnp
from jax import lax
from jax.experimental import pallas as pl
from jax.experimental.pallas import tpu as pltpu
from jax.sharding import PartitionSpec as P

VMEM = pl.BlockSpec(memory_space=pltpu.VMEM)
ANY = pl.BlockSpec(memory_space=pl.ANY)
LIGHT = pl.CostEstimate(flops=0, bytes_accessed=0, transcendentals=0)
OUT = ((2, 4), (1, 5), (0, 7), (3, 6))
BACK = ((2, 4), (3, 5), (1, 6))
SHARED, SELF = (7, 7), (0, 0)
PARAMS = pltpu.CompilerParams(vmem_limit_bytes=24 * 1024 * 1024)


def per_device(gradients, block_owner, left_gram, right_gram, left_root, right_root):
    owners = lax.axis_size("shard")
    half_rows = left_gram.shape[1]
    full_width = left_gram.shape[2]
    first_row = lax.axis_index("replica") * half_rows
    owner_index = lax.broadcasted_iota(jnp.int32, (owners, block_owner.shape[0]), 0)
    owner_onehot = (owner_index == block_owner[None, :]).astype(jnp.bfloat16)
    outgoing = jnp.einsum(
        "ob,brc->orc", owner_onehot, gradients[0], preferred_element_type=jnp.float32
    )
    arrived = lax.all_to_all(
        outgoing.astype(jnp.bfloat16), "shard", split_axis=0, concat_axis=0, tiled=True
    )
    total = lax.psum(arrived.astype(jnp.float32).astype(jnp.bfloat16), "replica")
    summed_block = total.reshape(full_width, full_width)
    own_rows = lax.dynamic_slice_in_dim(summed_block, first_row, half_rows, 0)
    own_cols = lax.dynamic_slice_in_dim(summed_block, first_row, half_rows, 1)
    left_term = lax.dot_general(
        own_rows, summed_block, (((1,), (1,)), ((), ())), preferred_element_type=jnp.float32
    )
    right_term = lax.dot_general(
        own_cols, summed_block, (((0,), (0,)), ((), ())), preferred_element_type=jnp.float32
    )
    left_new = (0.99 * left_gram[0].astype(jnp.float32) + 0.01 * left_term).astype(jnp.bfloat16)
    right_new = (0.99 * right_gram[0].astype(jnp.float32) + 0.01 * right_term).astype(jnp.bfloat16)
    partial_side = jnp.dot(left_root[0], summed_block, preferred_element_type=jnp.float32).astype(
        jnp.bfloat16
    )
    left_side = lax.all_gather(partial_side, "replica", axis=0, tiled=True)
    both_sides = jnp.dot(left_side, right_root[0], preferred_element_type=jnp.float32)
    side_squares = lax.psum(jnp.sum(both_sides * both_sides), "replica")
    grad_squares = jnp.sum(jnp.square(summed_block.astype(jnp.float32)))
    graft = jnp.sqrt(grad_squares / (side_squares + 1e-06))
    scaled = (
        (both_sides * graft).astype(jnp.bfloat16).reshape(owners, full_width // owners, half_rows)
    )
    returned = lax.all_to_all(scaled, "shard", split_axis=0, concat_axis=0, tiled=True)
    update = jnp.take(returned, block_owner, axis=0)
    return (left_new[None], right_new[None], update)


def turned(rounds):
    return tuple(codes[::-1] for codes in rounds)


def partner(codes):
    code = jnp.where(lax.axis_index("replica") == 0, codes[0], codes[1])
    return lax.axis_index("shard") ^ code


def block_of(owner_ref, owner):
    block = jnp.int32(-1)
    for b in range(owner_ref.shape[1]):
        block = jnp.where(owner_ref[0, b] == owner, b, block)
    return block


def squares(value):
    wide = value.astype(jnp.float32)
    rows = jnp.sum((wide * wide).reshape(-1, 8, wide.shape[1]), axis=0)
    return jnp.sum(jnp.sum(rows, axis=0, keepdims=True), axis=1, keepdims=True)


def fetch_kernel(gradient_ref, after_ref, out_ref):
    out_ref[...] = gradient_ref[...]


def pick_kernel(owner_ref, mine_ref, theirs_ref, *out_refs):
    for codes, out_ref in zip(OUT, out_refs):
        b = jnp.maximum(block_of(owner_ref, partner(codes)), 0)
        total = mine_ref[b].astype(jnp.float32) + theirs_ref[b].astype(jnp.float32)
        out_ref[...] = total.astype(out_ref.dtype)


def order_kernel(rows, columns, own_ref, other_ref, own_right_ref, other_right_ref, *refs):
    *out_refs, right_ref, rows_ref = refs
    right_ref[:, :own_right_ref.shape[1]] = own_right_ref[...]
    right_ref[:, own_right_ref.shape[1]:] = other_right_ref[...]
    half, full = own_ref.shape
    slab = full // len(rows)
    core = lax.axis_index("replica")
    for n, codes in enumerate(rows):
        start = partner(codes) * slab
        row = pl.multiple_of(lax.rem(start, half), slab)
        for ref, near in ((own_ref, True), (other_ref, False)):

            @pl.when((lax.div(start, half) == core) == near)
            def _(ref=ref):
                rows_ref[n * slab:(n + 1) * slab, :] = ref[pl.ds(row, slab), :]

    for out_ref, group in zip(out_refs, columns):
        column = lax.broadcasted_iota(jnp.int32, (1, len(group) * slab), 1)
        source = column
        for n, codes in enumerate(group):
            inside = (column >= n * slab) & (column < (n + 1) * slab)
            source = jnp.where(inside, column + (partner(codes) - n) * slab, source)
        row_index = lax.broadcasted_iota(jnp.int32, (full, len(group) * slab), 0)
        choose = (row_index == source).astype(jnp.float32).astype(rows_ref.dtype)
        out_ref[...] = jnp.dot(
            rows_ref[...], choose, preferred_element_type=jnp.float32
        ).astype(out_ref.dtype)


def begin_kernel(left_ref, *refs):
    *slabs, total_ref, grad_sq_ref, stacked_ref = refs
    slab = slabs[0].shape[0]
    for n, ref in enumerate(slabs):
        stacked_ref[n * slab:(n + 1) * slab, :] = ref[...]
    total_ref[...] = jnp.dot(
        left_ref[...], stacked_ref[...], preferred_element_type=jnp.float32
    )
    grad_sq_ref[...] = jnp.broadcast_to(squares(stacked_ref[...]), grad_sq_ref.shape)


def finish_kernel(count, left_ref, total_ref, begun_sq_ref, right_ref, *refs):
    slabs = refs[:count]
    *out_refs, stacked_ref, side_ref, both_ref = refs[count:]
    slab = slabs[0].shape[0]
    used, full = both_ref.shape
    for n, ref in enumerate(slabs):
        stacked_ref[n * slab:(n + 1) * slab, :] = ref[...]
    last = stacked_ref[...]
    side = total_ref[...] + jnp.dot(left_ref[...], last, preferred_element_type=jnp.float32)
    side_ref[...] = side.astype(side_ref.dtype)
    grad_sq = begun_sq_ref[0:1, 0:1] + squares(last)
    both = jnp.dot(side_ref[...], right_ref[...], preferred_element_type=jnp.float32)
    both_ref[...] = both[:used]
    graft = jnp.sqrt(grad_sq / (squares(both) + 1e-06))
    for k, out_ref in enumerate(out_refs):
        rows = slice(k * slab, (k + 1) * slab)
        if len(out_ref.shape) == 2:
            out_ref[...] = (both_ref[rows, :full // 2] * graft).astype(out_ref.dtype)
        else:
            out_ref[0] = (both_ref[rows, :full // 2] * graft).astype(out_ref.dtype)
            out_ref[1] = (both_ref[rows, full // 2:] * graft).astype(out_ref.dtype)


def gram_kernel(owner_ref, left_ref, right_ref, after_ref, *refs):
    *slabs, left_out, right_out, summed_ref = refs
    slab = slabs[0].shape[0]
    for codes, ref in zip(OUT + turned(OUT), slabs):
        row = pl.multiple_of(partner(codes) * slab, slab)
        summed_ref[pl.ds(row, slab), :] = ref[...]
    half = left_ref.shape[0]
    first = pl.multiple_of(lax.axis_index("replica") * half, 128)
    present = block_of(owner_ref, lax.axis_index("shard")) >= 0
    share = jnp.where(present, 0.01, 0.0).astype(jnp.float32)
    summed = summed_ref[...]
    left_term = lax.dot_general(
        summed_ref[pl.ds(first, half), :], summed, (((1,), (1,)), ((), ())),
        preferred_element_type=jnp.float32,
    )
    left_out[...] = (0.99 * left_ref[...].astype(jnp.float32) + share * left_term).astype(
        left_out.dtype
    )
    right_term = lax.dot_general(
        summed_ref[:, pl.ds(first, half)], summed, (((0,), (0,)), ((), ())),
        preferred_element_type=jnp.float32,
    )
    right_out[...] = (0.99 * right_ref[...].astype(jnp.float32) + share * right_term).astype(
        right_out.dtype
    )


def place_kernel(owner_ref, *refs):
    *slabs, out_ref, sem = refs
    pending = []
    for n, codes in enumerate(BACK + turned(BACK) + (SELF, SHARED)):
        block = block_of(owner_ref, partner(codes))
        source = slabs[n] if len(slabs[n].shape) == 2 else slabs[n].at[0]
        copy = pltpu.make_async_copy(source, out_ref.at[jnp.maximum(block, 0)], sem.at[n])

        @pl.when(block >= 0)
        def _(copy=copy):
            copy.start()

        pending.append((block, copy))
    for block, copy in pending:

        @pl.when(block >= 0)
        def _(copy=copy):
            copy.wait()


def per_device_paired(gradients, block_owner, left_gram, right_gram, left_root, right_root):
    owners = lax.axis_size("shard")
    rounds = len(OUT)
    blocks, slab, width = gradients.shape[1:]
    half_rows = left_gram.shape[1]
    rows = BACK + (SHARED, SELF) + turned(BACK)
    theirs_last = (rounds - 1, rounds - 2)
    sooner = OUT + turned(OUT)[:rounds - 2]
    columns = (sooner, tuple(turned(OUT)[k] for k in theirs_last))

    def other_core(x):
        return lax.ppermute(x, "replica", [(0, 1), (1, 0)])

    def trade(x, codes):
        pairs = [(s * 2 + r, (s ^ codes[r]) * 2 + r) for s in range(owners) for r in range(2)]
        return lax.ppermute(x, ("shard", "replica"), pairs)

    def shape(dims, dtype=jnp.bfloat16):
        return jax.ShapeDtypeStruct(dims, dtype)

    def call(kernel, out_shape, in_specs, *args, params=PARAMS, cost_estimate=LIGHT, **options):
        return pl.pallas_call(
            kernel, out_shape=out_shape, in_specs=in_specs, compiler_params=params,
            cost_estimate=cost_estimate, **options
        )(*args)

    block_owner = block_owner.reshape(1, blocks)
    other_gradient = other_core(gradients[0])
    fetched = call(
        fetch_kernel, shape((blocks, slab, width)), [VMEM, ANY], gradients[0], block_owner,
        out_specs=VMEM,
    )
    *outgoing, = call(
        pick_kernel, [shape((slab, width))] * rounds,
        [VMEM, VMEM, VMEM], block_owner, fetched, other_gradient, out_specs=[VMEM] * rounds,
    )
    mine = [trade(x, codes) for x, codes in zip(outgoing, OUT)]
    other_left, other_right = other_core(left_root[0]), other_core(right_root[0])
    left_sooner, left_last, right = call(
        functools.partial(order_kernel, rows, columns),
        [shape((width, len(group) * slab)) for group in columns] + [shape((width, width))],
        [VMEM] * 4, left_root[0], other_left, right_root[0], other_right, out_specs=[VMEM] * 3,
        scratch_shapes=[pltpu.VMEM((width, width), jnp.bfloat16)],
    )
    mine[0], left_sooner, left_last, right = lax.optimization_barrier(
        (mine[0], left_sooner, left_last, right)
    )
    theirs = [other_core(x) for x in mine]
    begun, begun_sq = call(
        begin_kernel,
        [shape((width, width), jnp.float32), shape((8, 128), jnp.float32)],
        [VMEM] * (1 + len(sooner)), left_sooner, *mine, *theirs[:rounds - 2],
        out_specs=[VMEM, VMEM],
        scratch_shapes=[pltpu.VMEM((len(sooner) * slab, width), jnp.bfloat16)],
    )
    half_slab = shape((slab, width // 2))
    *whole, shared, own = call(
        functools.partial(finish_kernel, len(theirs_last)),
        [shape((2, slab, width // 2))] * len(BACK) + [half_slab] * 2,
        [VMEM] * (4 + len(theirs_last)),
        left_last, begun, begun_sq, right, *[theirs[k] for k in theirs_last],
        out_specs=[VMEM] * (len(BACK) + 2),
        scratch_shapes=[
            pltpu.VMEM((len(theirs_last) * slab, width), jnp.bfloat16),
            pltpu.VMEM((width, width), jnp.bfloat16),
            pltpu.VMEM(((len(BACK) + 2) * slab, width), jnp.float32),
        ],
    )
    returned = [trade(x, codes) for x, codes in zip(whole, BACK)]
    shared = trade(shared, SHARED)
    left_new, right_new = call(
        gram_kernel, [shape(left_gram.shape[1:]), shape(right_gram.shape[1:])],
        [VMEM, VMEM, VMEM, ANY] + [VMEM] * (2 * rounds),
        block_owner, left_gram[0], right_gram[0], returned[0], *mine, *theirs,
        out_specs=[VMEM, VMEM],
        scratch_shapes=[pltpu.VMEM((width, width), jnp.bfloat16)],
        cost_estimate=pl.CostEstimate(
            flops=4 * half_rows * width * width, bytes_accessed=8 * half_rows * width,
            transcendentals=0,
        ),
    )
    left_new, right_new, returned[0] = lax.optimization_barrier(
        (left_new, right_new, returned[0])
    )
    passed = [other_core(x[1]) for x in returned]
    update = call(
        place_kernel, shape((blocks, slab, width // 2)), [VMEM] + [ANY] * owners,
        block_owner, *returned, *passed, own, shared,
        out_specs=ANY, scratch_shapes=[pltpu.SemaphoreType.DMA((owners,))],
    )
    return (left_new[None], right_new[None], update)


def solution(mesh):
    owners = mesh.shape["shard"]
    paired = mesh.shape["replica"] == 2 and owners == 2 * len(OUT)
    return jax.shard_map(
        per_device_paired if paired else per_device,
        mesh=mesh,
        in_specs=(
            P("replica", "groups", "shard", None),
            P("groups"),
            P(("groups", "shard"), "replica", None),
            P(("groups", "shard"), "replica", None),
            P(("groups", "shard"), "replica", None),
            P(("groups", "shard"), None, "replica"),
        ),
        out_specs=(
            P(("groups", "shard"), "replica", None),
            P(("groups", "shard"), "replica", None),
            P("groups", "shard", "replica"),
        ),
        check_vma=False,
    )
```

```python
import functools

import jax
import jax.numpy as jnp
from jax import lax
from jax.experimental import pallas as pl
from jax.experimental.pallas import tpu as pltpu
from jax.sharding import PartitionSpec as P

VMEM = pl.BlockSpec(memory_space=pltpu.VMEM)
ANY = pl.BlockSpec(memory_space=pl.ANY)
LIGHT = pl.CostEstimate(flops=0, bytes_accessed=0, transcendentals=0)
OUT = ((2, 6), (1, 5), (0, 4), (3, 7))
BACK = ((2, 4), (3, 5), (1, 6))
SHARED, SELF = (7, 7), (0, 0)
PARAMS = pltpu.CompilerParams(vmem_limit_bytes=24 * 1024 * 1024)


def per_device(gradients, block_owner, left_gram, right_gram, left_root, right_root):
    owners = lax.axis_size("shard")
    half_rows = left_gram.shape[1]
    full_width = left_gram.shape[2]
    first_row = lax.axis_index("replica") * half_rows
    owner_index = lax.broadcasted_iota(jnp.int32, (owners, block_owner.shape[0]), 0)
    owner_onehot = (owner_index == block_owner[None, :]).astype(jnp.bfloat16)
    outgoing = jnp.einsum(
        "ob,brc->orc", owner_onehot, gradients[0], preferred_element_type=jnp.float32
    )
    arrived = lax.all_to_all(
        outgoing.astype(jnp.bfloat16), "shard", split_axis=0, concat_axis=0, tiled=True
    )
    total = lax.psum(arrived.astype(jnp.float32).astype(jnp.bfloat16), "replica")
    summed_block = total.reshape(full_width, full_width)
    own_rows = lax.dynamic_slice_in_dim(summed_block, first_row, half_rows, 0)
    own_cols = lax.dynamic_slice_in_dim(summed_block, first_row, half_rows, 1)
    left_term = lax.dot_general(
        own_rows, summed_block, (((1,), (1,)), ((), ())), preferred_element_type=jnp.float32
    )
    right_term = lax.dot_general(
        own_cols, summed_block, (((0,), (0,)), ((), ())), preferred_element_type=jnp.float32
    )
    left_new = (0.99 * left_gram[0].astype(jnp.float32) + 0.01 * left_term).astype(jnp.bfloat16)
    right_new = (0.99 * right_gram[0].astype(jnp.float32) + 0.01 * right_term).astype(jnp.bfloat16)
    partial_side = jnp.dot(left_root[0], summed_block, preferred_element_type=jnp.float32).astype(
        jnp.bfloat16
    )
    left_side = lax.all_gather(partial_side, "replica", axis=0, tiled=True)
    both_sides = jnp.dot(left_side, right_root[0], preferred_element_type=jnp.float32)
    side_squares = lax.psum(jnp.sum(both_sides * both_sides), "replica")
    grad_squares = jnp.sum(jnp.square(summed_block.astype(jnp.float32)))
    graft = jnp.sqrt(grad_squares / (side_squares + 1e-06))
    scaled = (
        (both_sides * graft).astype(jnp.bfloat16).reshape(owners, full_width // owners, half_rows)
    )
    returned = lax.all_to_all(scaled, "shard", split_axis=0, concat_axis=0, tiled=True)
    update = jnp.take(returned, block_owner, axis=0)
    return (left_new[None], right_new[None], update)


def turned(rounds):
    return tuple(codes[::-1] for codes in rounds)


def partner(codes):
    code = jnp.where(lax.axis_index("replica") == 0, codes[0], codes[1])
    return lax.axis_index("shard") ^ code


def block_of(owner_ref, owner):
    block = jnp.int32(-1)
    for b in range(owner_ref.shape[1]):
        block = jnp.where(owner_ref[0, b] == owner, b, block)
    return block


def squares(value):
    wide = value.astype(jnp.float32)
    rows = jnp.sum((wide * wide).reshape(-1, 8, wide.shape[1]), axis=0)
    return jnp.sum(jnp.sum(rows, axis=0, keepdims=True), axis=1, keepdims=True)


def fetch_kernel(gradient_ref, after_ref, out_ref):
    out_ref[...] = gradient_ref[...]


def pick_kernel(owner_ref, mine_ref, theirs_ref, *out_refs):
    for codes, out_ref in zip(OUT, out_refs):
        b = jnp.maximum(block_of(owner_ref, partner(codes)), 0)
        total = mine_ref[b].astype(jnp.float32) + theirs_ref[b].astype(jnp.float32)
        out_ref[...] = total.astype(out_ref.dtype)


def order_kernel(rows, columns, own_ref, other_ref, own_right_ref, other_right_ref, *refs):
    *out_refs, right_ref, rows_ref = refs
    right_ref[:, :own_right_ref.shape[1]] = own_right_ref[...]
    right_ref[:, own_right_ref.shape[1]:] = other_right_ref[...]
    half, full = own_ref.shape
    slab = full // len(rows)
    core = lax.axis_index("replica")
    for n, codes in enumerate(rows):
        start = partner(codes) * slab
        row = pl.multiple_of(lax.rem(start, half), slab)
        for ref, near in ((own_ref, True), (other_ref, False)):

            @pl.when((lax.div(start, half) == core) == near)
            def _(ref=ref):
                rows_ref[n * slab:(n + 1) * slab, :] = ref[pl.ds(row, slab), :]

    for out_ref, group in zip(out_refs, columns):
        column = lax.broadcasted_iota(jnp.int32, (1, len(group) * slab), 1)
        source = column
        for n, codes in enumerate(group):
            inside = (column >= n * slab) & (column < (n + 1) * slab)
            source = jnp.where(inside, column + (partner(codes) - n) * slab, source)
        row_index = lax.broadcasted_iota(jnp.int32, (full, len(group) * slab), 0)
        choose = (row_index == source).astype(jnp.float32).astype(rows_ref.dtype)
        out_ref[...] = jnp.dot(
            rows_ref[...], choose, preferred_element_type=jnp.float32
        ).astype(out_ref.dtype)


def begin_kernel(left_ref, *refs):
    *slabs, total_ref, grad_sq_ref, stacked_ref = refs
    slab = slabs[0].shape[0]
    for n, ref in enumerate(slabs):
        stacked_ref[n * slab:(n + 1) * slab, :] = ref[...]
    total_ref[...] = jnp.dot(
        left_ref[...], stacked_ref[...], preferred_element_type=jnp.float32
    )
    grad_sq_ref[...] = jnp.broadcast_to(squares(stacked_ref[...]), grad_sq_ref.shape)


def finish_kernel(count, left_ref, total_ref, begun_sq_ref, right_ref, *refs):
    slabs = refs[:count]
    *out_refs, stacked_ref, side_ref, both_ref = refs[count:]
    slab = slabs[0].shape[0]
    used, full = both_ref.shape
    for n, ref in enumerate(slabs):
        stacked_ref[n * slab:(n + 1) * slab, :] = ref[...]
    last = stacked_ref[...]
    side = total_ref[...] + jnp.dot(left_ref[...], last, preferred_element_type=jnp.float32)
    side_ref[...] = side.astype(side_ref.dtype)
    grad_sq = begun_sq_ref[0:1, 0:1] + squares(last)
    both = jnp.dot(side_ref[...], right_ref[...], preferred_element_type=jnp.float32)
    both_ref[...] = both[:used]
    graft = jnp.sqrt(grad_sq / (squares(both) + 1e-06))
    for k, out_ref in enumerate(out_refs):
        rows = slice(k * slab, (k + 1) * slab)
        if len(out_ref.shape) == 2:
            out_ref[...] = (both_ref[rows, :full // 2] * graft).astype(out_ref.dtype)
        else:
            out_ref[0] = (both_ref[rows, :full // 2] * graft).astype(out_ref.dtype)
            out_ref[1] = (both_ref[rows, full // 2:] * graft).astype(out_ref.dtype)


def gram_kernel(owner_ref, left_ref, right_ref, after_ref, *refs):
    *slabs, left_out, right_out, summed_ref = refs
    slab = slabs[0].shape[0]
    for codes, ref in zip(OUT + turned(OUT), slabs):
        row = pl.multiple_of(partner(codes) * slab, slab)
        summed_ref[pl.ds(row, slab), :] = ref[...]
    half = left_ref.shape[0]
    first = pl.multiple_of(lax.axis_index("replica") * half, 128)
    present = block_of(owner_ref, lax.axis_index("shard")) >= 0
    share = jnp.where(present, 0.01, 0.0).astype(jnp.float32)
    summed = summed_ref[...]
    left_term = lax.dot_general(
        summed_ref[pl.ds(first, half), :], summed, (((1,), (1,)), ((), ())),
        preferred_element_type=jnp.float32,
    )
    left_out[...] = (0.99 * left_ref[...].astype(jnp.float32) + share * left_term).astype(
        left_out.dtype
    )
    right_term = lax.dot_general(
        summed_ref[:, pl.ds(first, half)], summed, (((0,), (0,)), ((), ())),
        preferred_element_type=jnp.float32,
    )
    right_out[...] = (0.99 * right_ref[...].astype(jnp.float32) + share * right_term).astype(
        right_out.dtype
    )


def place_kernel(owner_ref, *refs):
    *slabs, out_ref, sem = refs
    pending = []
    for n, codes in enumerate(BACK + turned(BACK) + (SELF, SHARED)):
        block = block_of(owner_ref, partner(codes))
        source = slabs[n] if len(slabs[n].shape) == 2 else slabs[n].at[0]
        copy = pltpu.make_async_copy(source, out_ref.at[jnp.maximum(block, 0)], sem.at[n])

        @pl.when(block >= 0)
        def _(copy=copy):
            copy.start()

        pending.append((block, copy))
    for block, copy in pending:

        @pl.when(block >= 0)
        def _(copy=copy):
            copy.wait()


def per_device_paired(gradients, block_owner, left_gram, right_gram, left_root, right_root):
    owners = lax.axis_size("shard")
    rounds = len(OUT)
    blocks, slab, width = gradients.shape[1:]
    half_rows = left_gram.shape[1]
    rows = BACK + (SHARED, SELF) + turned(BACK)
    theirs_last = (rounds - 1, rounds - 2)
    sooner = OUT + turned(OUT)[:rounds - 2]
    columns = (sooner, tuple(turned(OUT)[k] for k in theirs_last))

    def other_core(x):
        return lax.ppermute(x, "replica", [(0, 1), (1, 0)])

    def trade(x, codes):
        pairs = [(s * 2 + r, (s ^ codes[r]) * 2 + r) for s in range(owners) for r in range(2)]
        return lax.ppermute(x, ("shard", "replica"), pairs)

    def shape(dims, dtype=jnp.bfloat16):
        return jax.ShapeDtypeStruct(dims, dtype)

    def call(kernel, out_shape, in_specs, *args, params=PARAMS, cost_estimate=LIGHT, **options):
        return pl.pallas_call(
            kernel, out_shape=out_shape, in_specs=in_specs, compiler_params=params,
            cost_estimate=cost_estimate, **options
        )(*args)

    block_owner = block_owner.reshape(1, blocks)
    other_gradient = other_core(gradients[0])
    fetched = call(
        fetch_kernel, shape((blocks, slab, width)), [VMEM, ANY], gradients[0], block_owner,
        out_specs=VMEM,
    )
    *outgoing, = call(
        pick_kernel, [shape((slab, width))] * rounds,
        [VMEM, VMEM, VMEM], block_owner, fetched, other_gradient, out_specs=[VMEM] * rounds,
    )
    mine = [trade(x, codes) for x, codes in zip(outgoing, OUT)]
    other_left, other_right = other_core(left_root[0]), other_core(right_root[0])
    left_sooner, left_last, right = call(
        functools.partial(order_kernel, rows, columns),
        [shape((width, len(group) * slab)) for group in columns] + [shape((width, width))],
        [VMEM] * 4, left_root[0], other_left, right_root[0], other_right, out_specs=[VMEM] * 3,
        scratch_shapes=[pltpu.VMEM((width, width), jnp.bfloat16)],
    )
    mine[0], left_sooner, left_last, right = lax.optimization_barrier(
        (mine[0], left_sooner, left_last, right)
    )
    theirs = [other_core(x) for x in mine]
    begun, begun_sq = call(
        begin_kernel,
        [shape((width, width), jnp.float32), shape((8, 128), jnp.float32)],
        [VMEM] * (1 + len(sooner)), left_sooner, *mine, *theirs[:rounds - 2],
        out_specs=[VMEM, VMEM],
        scratch_shapes=[pltpu.VMEM((len(sooner) * slab, width), jnp.bfloat16)],
    )
    half_slab = shape((slab, width // 2))
    *whole, shared, own = call(
        functools.partial(finish_kernel, len(theirs_last)),
        [shape((2, slab, width // 2))] * len(BACK) + [half_slab] * 2,
        [VMEM] * (4 + len(theirs_last)),
        left_last, begun, begun_sq, right, *[theirs[k] for k in theirs_last],
        out_specs=[VMEM] * (len(BACK) + 2),
        scratch_shapes=[
            pltpu.VMEM((len(theirs_last) * slab, width), jnp.bfloat16),
            pltpu.VMEM((width, width), jnp.bfloat16),
            pltpu.VMEM(((len(BACK) + 2) * slab, width), jnp.float32),
        ],
    )
    returned = [trade(x, codes) for x, codes in zip(whole, BACK)]
    left_new, right_new = call(
        gram_kernel, [shape(left_gram.shape[1:]), shape(right_gram.shape[1:])],
        [VMEM, VMEM, VMEM, ANY] + [VMEM] * (2 * rounds),
        block_owner, left_gram[0], right_gram[0], own, *mine, *theirs,
        out_specs=[VMEM, VMEM],
        scratch_shapes=[pltpu.VMEM((width, width), jnp.bfloat16)],
        cost_estimate=pl.CostEstimate(
            flops=4 * half_rows * width * width, bytes_accessed=8 * half_rows * width,
            transcendentals=0,
        ),
    )
    left_new, right_new, shared, returned[0] = lax.optimization_barrier(
        (left_new, right_new, shared, returned[0])
    )
    shared = trade(shared, SHARED)
    passed = [other_core(x[1]) for x in returned]
    update = call(
        place_kernel, shape((blocks, slab, width // 2)), [VMEM] + [ANY] * owners,
        block_owner, *returned, *passed, own, shared,
        out_specs=ANY, scratch_shapes=[pltpu.SemaphoreType.DMA((owners,))],
    )
    return (left_new[None], right_new[None], update)


def solution(mesh):
    owners = mesh.shape["shard"]
    paired = mesh.shape["replica"] == 2 and owners == 2 * len(OUT)
    return jax.shard_map(
        per_device_paired if paired else per_device,
        mesh=mesh,
        in_specs=(
            P("replica", "groups", "shard", None),
            P("groups"),
            P(("groups", "shard"), "replica", None),
            P(("groups", "shard"), "replica", None),
            P(("groups", "shard"), "replica", None),
            P(("groups", "shard"), None, "replica"),
        ),
        out_specs=(
            P(("groups", "shard"), "replica", None),
            P(("groups", "shard"), "replica", None),
            P("groups", "shard", "replica"),
        ),
        check_vma=False,
    )
```

```python
import functools

import jax
import jax.numpy as jnp
from jax import lax
from jax.experimental import pallas as pl
from jax.experimental.pallas import tpu as pltpu
from jax.sharding import PartitionSpec as P

VMEM = pl.BlockSpec(memory_space=pltpu.VMEM)
ANY = pl.BlockSpec(memory_space=pl.ANY)
LIGHT = pl.CostEstimate(flops=0, bytes_accessed=0, transcendentals=0)
OUT = ((2, 6), (1, 5), (0, 4), (3, 7))
BACK = ((2, 4), (3, 5), (1, 6))
SHARED, SELF = (7, 7), (0, 0)
PARAMS = pltpu.CompilerParams(vmem_limit_bytes=24 * 1024 * 1024)


def per_device(gradients, block_owner, left_gram, right_gram, left_root, right_root):
    owners = lax.axis_size("shard")
    half_rows = left_gram.shape[1]
    full_width = left_gram.shape[2]
    first_row = lax.axis_index("replica") * half_rows
    owner_index = lax.broadcasted_iota(jnp.int32, (owners, block_owner.shape[0]), 0)
    owner_onehot = (owner_index == block_owner[None, :]).astype(jnp.bfloat16)
    outgoing = jnp.einsum(
        "ob,brc->orc", owner_onehot, gradients[0], preferred_element_type=jnp.float32
    )
    arrived = lax.all_to_all(
        outgoing.astype(jnp.bfloat16), "shard", split_axis=0, concat_axis=0, tiled=True
    )
    total = lax.psum(arrived.astype(jnp.float32).astype(jnp.bfloat16), "replica")
    summed_block = total.reshape(full_width, full_width)
    own_rows = lax.dynamic_slice_in_dim(summed_block, first_row, half_rows, 0)
    own_cols = lax.dynamic_slice_in_dim(summed_block, first_row, half_rows, 1)
    left_term = lax.dot_general(
        own_rows, summed_block, (((1,), (1,)), ((), ())), preferred_element_type=jnp.float32
    )
    right_term = lax.dot_general(
        own_cols, summed_block, (((0,), (0,)), ((), ())), preferred_element_type=jnp.float32
    )
    left_new = (0.99 * left_gram[0].astype(jnp.float32) + 0.01 * left_term).astype(jnp.bfloat16)
    right_new = (0.99 * right_gram[0].astype(jnp.float32) + 0.01 * right_term).astype(jnp.bfloat16)
    partial_side = jnp.dot(left_root[0], summed_block, preferred_element_type=jnp.float32).astype(
        jnp.bfloat16
    )
    left_side = lax.all_gather(partial_side, "replica", axis=0, tiled=True)
    both_sides = jnp.dot(left_side, right_root[0], preferred_element_type=jnp.float32)
    side_squares = lax.psum(jnp.sum(both_sides * both_sides), "replica")
    grad_squares = jnp.sum(jnp.square(summed_block.astype(jnp.float32)))
    graft = jnp.sqrt(grad_squares / (side_squares + 1e-06))
    scaled = (
        (both_sides * graft).astype(jnp.bfloat16).reshape(owners, full_width // owners, half_rows)
    )
    returned = lax.all_to_all(scaled, "shard", split_axis=0, concat_axis=0, tiled=True)
    update = jnp.take(returned, block_owner, axis=0)
    return (left_new[None], right_new[None], update)


def turned(rounds):
    return tuple(codes[::-1] for codes in rounds)


def partner(codes):
    code = jnp.where(lax.axis_index("replica") == 0, codes[0], codes[1])
    return lax.axis_index("shard") ^ code


def block_of(owner_ref, owner):
    block = jnp.int32(-1)
    for b in range(owner_ref.shape[1]):
        block = jnp.where(owner_ref[0, b] == owner, b, block)
    return block


def squares(value):
    wide = value.astype(jnp.float32)
    rows = jnp.sum((wide * wide).reshape(-1, 8, wide.shape[1]), axis=0)
    return jnp.sum(jnp.sum(rows, axis=0, keepdims=True), axis=1, keepdims=True)


def fetch_kernel(gradient_ref, after_ref, out_ref):
    out_ref[...] = gradient_ref[...]


def pick_kernel(owner_ref, mine_ref, theirs_ref, *out_refs):
    for codes, out_ref in zip(OUT, out_refs):
        b = jnp.maximum(block_of(owner_ref, partner(codes)), 0)
        total = mine_ref[b].astype(jnp.float32) + theirs_ref[b].astype(jnp.float32)
        out_ref[...] = total.astype(out_ref.dtype)


def order_kernel(rows, columns, own_ref, other_ref, own_right_ref, other_right_ref, *refs):
    *out_refs, right_ref, rows_ref = refs
    right_ref[:, :own_right_ref.shape[1]] = own_right_ref[...]
    right_ref[:, own_right_ref.shape[1]:] = other_right_ref[...]
    half, full = own_ref.shape
    slab = full // len(rows)
    core = lax.axis_index("replica")
    for n, codes in enumerate(rows):
        start = partner(codes) * slab
        row = pl.multiple_of(lax.rem(start, half), slab)
        for ref, near in ((own_ref, True), (other_ref, False)):

            @pl.when((lax.div(start, half) == core) == near)
            def _(ref=ref):
                rows_ref[n * slab:(n + 1) * slab, :] = ref[pl.ds(row, slab), :]

    for out_ref, group in zip(out_refs, columns):
        column = lax.broadcasted_iota(jnp.int32, (1, len(group) * slab), 1)
        source = column
        for n, codes in enumerate(group):
            inside = (column >= n * slab) & (column < (n + 1) * slab)
            source = jnp.where(inside, column + (partner(codes) - n) * slab, source)
        row_index = lax.broadcasted_iota(jnp.int32, (full, len(group) * slab), 0)
        choose = (row_index == source).astype(jnp.float32).astype(rows_ref.dtype)
        out_ref[...] = jnp.dot(
            rows_ref[...], choose, preferred_element_type=jnp.float32
        ).astype(out_ref.dtype)


def begin_kernel(left_ref, *refs):
    *slabs, total_ref, grad_sq_ref, stacked_ref = refs
    slab = slabs[0].shape[0]
    for n, ref in enumerate(slabs):
        stacked_ref[n * slab:(n + 1) * slab, :] = ref[...]
    total_ref[...] = jnp.dot(
        left_ref[...], stacked_ref[...], preferred_element_type=jnp.float32
    )
    grad_sq_ref[...] = jnp.broadcast_to(squares(stacked_ref[...]), grad_sq_ref.shape)


def finish_kernel(count, left_ref, total_ref, begun_sq_ref, right_ref, *refs):
    slabs = refs[:count]
    *out_refs, stacked_ref, side_ref = refs[count:]
    slab = slabs[0].shape[0]
    full = right_ref.shape[1]
    for n, ref in enumerate(slabs):
        stacked_ref[n * slab:(n + 1) * slab, :] = ref[...]
    last = stacked_ref[...]
    side = total_ref[...] + jnp.dot(left_ref[...], last, preferred_element_type=jnp.float32)
    side_ref[...] = side.astype(side_ref.dtype)
    grad_sq = begun_sq_ref[0:1, 0:1] + squares(last)
    both = jnp.dot(side_ref[...], right_ref[...], preferred_element_type=jnp.float32)
    graft = jnp.sqrt(grad_sq / (squares(both) + 1e-06))
    for k, out_ref in enumerate(out_refs):
        rows = slice(k * slab, (k + 1) * slab)
        if len(out_ref.shape) == 2:
            out_ref[...] = (both[rows, :full // 2] * graft).astype(out_ref.dtype)
        else:
            out_ref[0] = (both[rows, :full // 2] * graft).astype(out_ref.dtype)
            out_ref[1] = (both[rows, full // 2:] * graft).astype(out_ref.dtype)


def gram_kernel(owner_ref, left_ref, right_ref, after_ref, *refs):
    *slabs, left_out, right_out, summed_ref = refs
    slab = slabs[0].shape[0]
    for codes, ref in zip(OUT + turned(OUT), slabs):
        row = pl.multiple_of(partner(codes) * slab, slab)
        summed_ref[pl.ds(row, slab), :] = ref[...]
    half = left_ref.shape[0]
    first = pl.multiple_of(lax.axis_index("replica") * half, 128)
    present = block_of(owner_ref, lax.axis_index("shard")) >= 0
    share = jnp.where(present, 0.01, 0.0).astype(jnp.float32)
    summed = summed_ref[...]
    left_term = lax.dot_general(
        summed_ref[pl.ds(first, half), :], summed, (((1,), (1,)), ((), ())),
        preferred_element_type=jnp.float32,
    )
    left_out[...] = (0.99 * left_ref[...].astype(jnp.float32) + share * left_term).astype(
        left_out.dtype
    )
    right_term = lax.dot_general(
        summed_ref[:, pl.ds(first, half)], summed, (((0,), (0,)), ((), ())),
        preferred_element_type=jnp.float32,
    )
    right_out[...] = (0.99 * right_ref[...].astype(jnp.float32) + share * right_term).astype(
        right_out.dtype
    )


def place_kernel(owner_ref, *refs):
    *slabs, out_ref, sem = refs
    pending = []
    for n, codes in enumerate(BACK + turned(BACK) + (SELF, SHARED)):
        block = block_of(owner_ref, partner(codes))
        source = slabs[n] if len(slabs[n].shape) == 2 else slabs[n].at[0]
        copy = pltpu.make_async_copy(source, out_ref.at[jnp.maximum(block, 0)], sem.at[n])

        @pl.when(block >= 0)
        def _(copy=copy):
            copy.start()

        pending.append((block, copy))
    for block, copy in pending:

        @pl.when(block >= 0)
        def _(copy=copy):
            copy.wait()


def per_device_paired(gradients, block_owner, left_gram, right_gram, left_root, right_root):
    owners = lax.axis_size("shard")
    rounds = len(OUT)
    blocks, slab, width = gradients.shape[1:]
    half_rows = left_gram.shape[1]
    rows = BACK + (SHARED, SELF) + turned(BACK)
    theirs_last = (rounds - 1, rounds - 2)
    sooner = OUT + turned(OUT)[:rounds - 2]
    columns = (sooner, tuple(turned(OUT)[k] for k in theirs_last))

    def other_core(x):
        return lax.ppermute(x, "replica", [(0, 1), (1, 0)])

    def trade(x, codes):
        pairs = [(s * 2 + r, (s ^ codes[r]) * 2 + r) for s in range(owners) for r in range(2)]
        return lax.ppermute(x, ("shard", "replica"), pairs)

    def shape(dims, dtype=jnp.bfloat16):
        return jax.ShapeDtypeStruct(dims, dtype)

    def call(kernel, out_shape, in_specs, *args, params=PARAMS, cost_estimate=LIGHT, **options):
        return pl.pallas_call(
            kernel, out_shape=out_shape, in_specs=in_specs, compiler_params=params,
            cost_estimate=cost_estimate, **options
        )(*args)

    block_owner = block_owner.reshape(1, blocks)
    other_gradient = other_core(gradients[0])
    fetched = call(
        fetch_kernel, shape((blocks, slab, width)), [VMEM, ANY], gradients[0], block_owner,
        out_specs=VMEM,
    )
    *outgoing, = call(
        pick_kernel, [shape((slab, width))] * rounds,
        [VMEM, VMEM, VMEM], block_owner, fetched, other_gradient, out_specs=[VMEM] * rounds,
    )
    mine = [trade(x, codes) for x, codes in zip(outgoing, OUT)]
    other_left, other_right = other_core(left_root[0]), other_core(right_root[0])
    left_sooner, left_last, right = call(
        functools.partial(order_kernel, rows, columns),
        [shape((width, len(group) * slab)) for group in columns] + [shape((width, width))],
        [VMEM] * 4, left_root[0], other_left, right_root[0], other_right, out_specs=[VMEM] * 3,
        scratch_shapes=[pltpu.VMEM((width, width), jnp.bfloat16)],
    )
    mine[0], left_sooner, left_last, right = lax.optimization_barrier(
        (mine[0], left_sooner, left_last, right)
    )
    theirs = [other_core(x) for x in mine]
    begun, begun_sq = call(
        begin_kernel,
        [shape((width, width), jnp.float32), shape((8, 128), jnp.float32)],
        [VMEM] * (1 + len(sooner)), left_sooner, *mine, *theirs[:rounds - 2],
        out_specs=[VMEM, VMEM],
        scratch_shapes=[pltpu.VMEM((len(sooner) * slab, width), jnp.bfloat16)],
    )
    half_slab = shape((slab, width // 2))
    *whole, shared, own = call(
        functools.partial(finish_kernel, len(theirs_last)),
        [shape((2, slab, width // 2))] * len(BACK) + [half_slab] * 2,
        [VMEM] * (4 + len(theirs_last)),
        left_last, begun, begun_sq, right, *[theirs[k] for k in theirs_last],
        out_specs=[VMEM] * (len(BACK) + 2),
        scratch_shapes=[
            pltpu.VMEM((len(theirs_last) * slab, width), jnp.bfloat16),
            pltpu.VMEM((width, width), jnp.bfloat16),
        ],
    )
    returned = [trade(x, codes) for x, codes in zip(whole, BACK)]
    shared = trade(shared, SHARED)
    left_new, right_new = call(
        gram_kernel, [shape(left_gram.shape[1:]), shape(right_gram.shape[1:])],
        [VMEM, VMEM, VMEM, ANY] + [VMEM] * (2 * rounds),
        block_owner, left_gram[0], right_gram[0], returned[0], *mine, *theirs,
        out_specs=[VMEM, VMEM],
        scratch_shapes=[pltpu.VMEM((width, width), jnp.bfloat16)],
        cost_estimate=pl.CostEstimate(
            flops=4 * half_rows * width * width, bytes_accessed=8 * half_rows * width,
            transcendentals=0,
        ),
    )
    left_new, right_new, returned[0] = lax.optimization_barrier(
        (left_new, right_new, returned[0])
    )
    passed = [other_core(x[1]) for x in returned]
    update = call(
        place_kernel, shape((blocks, slab, width // 2)), [VMEM] + [ANY] * owners,
        block_owner, *returned, *passed, own, shared,
        out_specs=ANY, scratch_shapes=[pltpu.SemaphoreType.DMA((owners,))],
    )
    return (left_new[None], right_new[None], update)


def solution(mesh):
    owners = mesh.shape["shard"]
    paired = mesh.shape["replica"] == 2 and owners == 2 * len(OUT)
    return jax.shard_map(
        per_device_paired if paired else per_device,
        mesh=mesh,
        in_specs=(
            P("replica", "groups", "shard", None),
            P("groups"),
            P(("groups", "shard"), "replica", None),
            P(("groups", "shard"), "replica", None),
            P(("groups", "shard"), "replica", None),
            P(("groups", "shard"), None, "replica"),
        ),
        out_specs=(
            P(("groups", "shard"), "replica", None),
            P(("groups", "shard"), "replica", None),
            P("groups", "shard", "replica"),
        ),
        check_vma=False,
    )
```
